32 devices in a mesh: groups: 2 (over y), sector: 4 (over z), op: 2 (over x), rep: 2 (over core).
Axes of the slice: x: 2, y: 2, z: 4, core: 2. Of those that a mesh axis runs over, the one named last changes fastest.
Arguments:
- wavefunction: bfloat16 [32, 256, 256], P(('groups', 'sector')), parts along dimension 0, may hold values from -6 to 6
- left_ops: bfloat16 [128, 256, 256], P(('groups', 'op'), 'rep'), parts along dimension 0, may hold values from -0.375 to 0.375
- right_ops: bfloat16 [128, 256, 256], P(('groups', 'op')), parts along dimension 0, may hold values from -0.375 to 0.375
- site_coef: float32 [128, 16], P(('groups', 'op'), 'sector'), parts along dimension 0, may hold values from -4 to 4
- coupled: int32 [128, 16], P(('groups', 'op'), 'sector'), parts along dimension 0, may hold values from 0 to 1, as said below
- sector_shift: int32 [128], P(('groups', 'op')), parts along dimension 0, may hold values from 0 to 15
Outputs:
- sigma: float32 [32, 256, 256], P(('groups', 'sector'), 'rep', 'op'), parts along dimension 0
The draws below stay inside these ranges and needn't reach their ends.
There are 2 independent parts, one for each index of `groups`. The reference program is written for one: setup_inputs(seed, part) draws one part's arguments, and reference() takes and returns one part's arrays. A program takes and returns all parts, laid end to end along the dimension named above; each array names one. Nothing has to cross between parts.
Inputs may be any that keep to these rules, and one draw needn't show every extreme that they name: coupled holds only 0 and 1; the share of coupled terms differs from sector to sector.
All inputs are finite; a program needn't handle non-finite values.
Results may differ from the reference program's by a relative error of at most 0.0029.
Values may be sent and summed in bfloat16 or wider, within the bound.
No kernel may reach another device: no remote copies, remote signals or barrier semaphores. Data moves between devices by JAX's collectives and lax.ppermute only.
A program may use at most 64 MiB of HBM per device.

```python
import jax
import jax.numpy as jnp
from jax import lax

M = 256
S = 16
K = 64


def draw_coupled(key, part):
    key = jax.random.fold_in(key, 5)
    first, second = jax.random.split(key)
    density = jax.random.randint(first, (S,), 1, 9)
    values = jax.random.randint(second, (K, S), 0, 8)
    return (values < density[None, :]).astype(jnp.int32)


def plant(array, own_key, smallest, top_value):
    dims = array.shape
    place = [jax.random.randint(jax.random.fold_in(own_key, axis), (), 0, dims[axis]) for axis in range(len(dims))]
    array = array.at[tuple(place)].set(smallest)
    longest = dims.index(max(dims))
    place[longest] = (place[longest] + 1) % dims[longest]
    return array.at[tuple(place)].set(top_value)


def steps_of(stream_key, extent, shards, smallest, largest):
    loudness = 1.0
    for axis_at, shards_of in shards:
        heights = jax.random.uniform(jax.random.fold_in(jax.random.fold_in(stream_key, 6), axis_at), (shards_of,), jnp.float32, smallest / len(shards), largest / len(shards))
        loudness = loudness * jnp.repeat(jnp.exp(heights), extent[axis_at] // shards_of).reshape((-1,) + (1,) * (len(extent) - 1 - axis_at))
    return loudness


def centred(stream_key, extent, scale, bound, pieces=(), kind=jnp.bfloat16):
    drawn = jax.random.normal(stream_key, extent, jnp.float32) * scale
    if len(pieces) > 0:
        drawn = steps_of(stream_key, extent, pieces, -0.22, 0.18) * drawn
    return jnp.clip(drawn, min=-bound, max=bound).astype(kind)


def setup_inputs(seed: int = 0, part: int = 0) -> dict:
    key_list = jax.random.split(jax.random.key(seed), 7)
    part_keys = jax.random.split(jax.random.fold_in(key_list[6], part), 7)
    return {
        "wavefunction": centred(part_keys[0], (S, M, M), 1.0, 6.0, ((0, 4),)),
        "left_ops": centred(part_keys[1], (K, M, M), M ** -0.5, 0.375, ((0, 2), (1, 2))),
        "right_ops": centred(part_keys[2], (K, M, M), M ** -0.5, 0.375, ((0, 2),)),
        "site_coef": centred(part_keys[3], (K, S), 0.25, 4.0, ((0, 2), (1, 4)), jnp.float32),
        "coupled": draw_coupled(jax.random.fold_in(jax.random.fold_in(key_list[6], part), 71), part),
        "sector_shift": plant(jax.random.randint(part_keys[5], (K,), 0, S), jax.random.fold_in(part_keys[5], 1), 0, S - 1).astype(jnp.int32),
    }


def reference(wavefunction, left_ops, right_ops, site_coef, coupled, sector_shift):
    sectors = jnp.arange(S, dtype=jnp.int32)

    def one_term(running, term_index):
        source = (sectors + sector_shift[term_index]) % S
        blocks = wavefunction[source].astype(jnp.float32)
        left = left_ops[term_index].astype(jnp.float32)
        mixed = jnp.einsum("ij,sjk->sik", left, blocks).astype(jnp.bfloat16)
        right = right_ops[term_index].astype(jnp.float32)
        product = jnp.einsum("sik,lk->sil", mixed.astype(jnp.float32), right)
        weight = site_coef[term_index] * coupled[term_index].astype(jnp.float32)
        return running + weight[:, None, None] * product, None

    initial = jnp.zeros((S, M, M), jnp.float32)
    sigma, unused = lax.scan(one_term, initial, jnp.arange(K, dtype=jnp.int32))
    return sigma
```

```python
import functools

import jax
import jax.numpy as jnp
from jax import lax
from jax.experimental import pallas as pl
from jax.experimental.pallas import tpu as pltpu
from jax.sharding import PartitionSpec as P

TERMS_A_STEP = 4


def sigma_kernel(counts, split, place_ref, weight_ref, side_ref, *refs):
    pieces = refs[: len(counts)]
    left_ref, right_ref = refs[len(counts) : len(counts) + 2]
    outs = refs[len(counts) + 2 : -3]
    blocks, total, sems = refs[-3:]
    step = pl.program_id(0)
    terms = left_ref.shape[0]
    sectors, rows, width = total.shape

    @pl.when(step == 0)
    def _():
        copies = []
        at = 0
        for number, count in enumerate(counts):
            copy = pltpu.make_async_copy(
                pieces[number], blocks.at[pl.ds(at, count)], sems.at[number]
            )
            copy.start()
            copies.append(copy)
            at += count
        total[...] = jnp.zeros_like(total)
        for copy in copies:
            copy.wait()

    for t in range(terms):
        k = step * terms + t
        left = left_ref[t]
        mixed = [
            jnp.dot(
                left, blocks[place_ref[k, s]], preferred_element_type=jnp.float32
            ).astype(jnp.bfloat16)
            for s in range(sectors)
        ]
        product = lax.dot_general(
            jnp.concatenate(mixed, axis=0),
            right_ref[t],
            (((1,), (1,)), ((), ())),
            preferred_element_type=jnp.float32,
        )
        for s in range(sectors):
            total[s] += weight_ref[k, s] * product[s * rows : (s + 1) * rows]

    @pl.when(step == pl.num_programs(0) - 1)
    def _():
        if not split:
            outs[0][...] = total[...]
        else:
            first = side_ref[0] == 0
            half = width // 2
            low, high = total[:, :, :half], total[:, :, half:]
            outs[0][...] = jnp.where(first, low, high)
            outs[1][...] = jnp.where(first, high, low).astype(jnp.bfloat16)


def all_terms(pieces, place, weight, side, left_ops, right_ops, split):
    k_dev, half_rows, width = left_ops.shape
    sec_dev = place.shape[1]
    counts = tuple(piece.shape[0] for piece in pieces)
    terms = TERMS_A_STEP
    if split:
        shape = (sec_dev, half_rows, width // 2)
        outs = [jax.ShapeDtypeStruct(shape, jnp.float32), jax.ShapeDtypeStruct(shape, jnp.bfloat16)]
    else:
        outs = [jax.ShapeDtypeStruct((sec_dev, half_rows, width), jnp.float32)]
    return pl.pallas_call(
        functools.partial(sigma_kernel, counts, split),
        grid=(k_dev // terms,),
        out_shape=outs,
        in_specs=[pl.BlockSpec(memory_space=pltpu.SMEM)] * 3
        + [pl.BlockSpec(memory_space=pl.ANY)] * len(pieces)
        + [
            pl.BlockSpec((terms, half_rows, width), lambda i: (i, 0, 0)),
            pl.BlockSpec((terms, width, width), lambda i: (i, 0, 0)),
        ],
        out_specs=[pl.BlockSpec(out.shape, lambda i: (0, 0, 0)) for out in outs],
        scratch_shapes=[
            pltpu.VMEM((sum(counts), width, width), jnp.bfloat16),
            pltpu.VMEM((sec_dev, half_rows, width), jnp.float32),
            pltpu.SemaphoreType.DMA((len(counts),)),
        ],
        compiler_params=pltpu.CompilerParams(vmem_limit_bytes=40 * 1024 * 1024),
        cost_estimate=pl.CostEstimate(
            flops=k_dev * sec_dev * 4 * half_rows * width * width,
            bytes_accessed=2 * (left_ops.size + right_ops.size + sum(counts) * width * width),
            transcendentals=0,
        ),
    )(place, weight, side, *pieces, left_ops, right_ops)


def shift_by(value, axis, distance):
    size = lax.axis_size(axis)
    return lax.ppermute(value, axis, [(i, (i + distance) % size) for i in range(size)])


def per_device(wavefunction, left_ops, right_ops, site_coef, coupled, sector_shift):
    sec_dev, width = wavefunction.shape[:2]
    devices = lax.axis_size("sector")
    total_sectors = sec_dev * devices
    me, op, rep = lax.axis_index("sector"), lax.axis_index("op"), lax.axis_index("rep")
    local_ids = jnp.arange(sec_dev, dtype=jnp.int32)
    source = (me * sec_dev + local_ids[None, :] + sector_shift[:, None]) % total_sectors
    weight = jnp.where(coupled > 0, site_coef, 0.0)
    side = jnp.reshape(op, (1,)).astype(jnp.int32)
    four = lax.axis_size("op") == 2 and lax.axis_size("rep") == 2

    if four and sec_dev == 4 and devices <= 4:
        own = lax.dynamic_slice_in_dim(wavefunction, op * 2 + rep, 1, 0)
        pieces = [wavefunction]
        for distance in range(1, devices):
            straight = shift_by(own, "sector", distance)
            across = shift_by(straight, "op", 1)
            beside = shift_by(straight, "rep", 1)
            diagonal = shift_by(across, "rep", 1)
            pieces += [straight, beside, across, diagonal]
        origin, block = source // sec_dev, source % sec_dev
        distance = (me - origin) % devices
        relative = block ^ (op * 2 + rep)
        place = jnp.where(distance == 0, block, distance * sec_dev + relative)
    else:
        pieces = [lax.all_gather(wavefunction, "sector", axis=0, tiled=True)]
        place = source

    if lax.axis_size("op") == 2:
        mine, theirs = all_terms(pieces, place, weight, side, left_ops, right_ops, True)
        return mine + shift_by(theirs, "op", 1).astype(jnp.float32)
    (total,) = all_terms(pieces, place, weight, side, left_ops, right_ops, False)
    return lax.psum_scatter(total, "op", scatter_dimension=2, tiled=True)


def solution(mesh):
    placed = (
        P(("groups", "sector"), None, None),
        P(("groups", "op"), "rep", None),
        P(("groups", "op"), None, None),
        P(("groups", "op"), "sector"),
        P(("groups", "op"), "sector"),
        P(("groups", "op")),
    )
    return jax.shard_map(
        per_device,
        mesh=mesh,
        in_specs=placed,
        out_specs=P(("groups", "sector"), "rep", "op"),
        check_vma=False,
    )
```

```python
import functools

import jax
import jax.numpy as jnp
from jax import lax
from jax.experimental import pallas as pl
from jax.experimental.pallas import tpu as pltpu
from jax.sharding import PartitionSpec as P

MIX_TERMS = 8
SUM_TERMS = 4
VMEM_BYTES = 24 * 1024 * 1024


def mix_kernel(left_ref, wave_ref, mixed_ref):
    terms, rows, width = left_ref.shape
    left = left_ref[...].reshape(terms * rows, width)
    for s in range(wave_ref.shape[0]):
        product = jnp.dot(left, wave_ref[s], preferred_element_type=jnp.float32)
        mixed_ref[:, s] = product.astype(jnp.bfloat16).reshape(terms, rows, width)


def mix(left_ops, wavefunction):
    k_dev, rows, width = left_ops.shape
    sec_dev = wavefunction.shape[0]
    return pl.pallas_call(
        mix_kernel,
        grid=(k_dev // MIX_TERMS,),
        out_shape=jax.ShapeDtypeStruct((k_dev, sec_dev, rows, width), jnp.bfloat16),
        in_specs=[
            pl.BlockSpec((MIX_TERMS, rows, width), lambda i: (i, 0, 0)),
            pl.BlockSpec(wavefunction.shape, lambda i: (0, 0, 0)),
        ],
        out_specs=pl.BlockSpec((MIX_TERMS, sec_dev, rows, width), lambda i: (i, 0, 0, 0)),
        compiler_params=pltpu.CompilerParams(vmem_limit_bytes=VMEM_BYTES),
        cost_estimate=pl.CostEstimate(
            flops=2 * k_dev * sec_dev * rows * width * width,
            bytes_accessed=2 * k_dev * rows * width * (1 + sec_dev),
            transcendentals=0,
        ),
    )(left_ops, wavefunction)


def sum_kernel(split, shift_ref, coef_ref, base_ref, side_ref, mixed_ref, right_ref, *refs):
    outs, total = refs[:-1], refs[-1]
    step = pl.program_id(0)
    terms, sec_dev, rows, width = mixed_ref.shape
    targets = total.shape[0]

    @pl.when(step == 0)
    def _():
        total[...] = jnp.zeros_like(total)

    for t in range(terms):
        k = step * terms + t
        product = lax.dot_general(
            mixed_ref[t].reshape(sec_dev * rows, width),
            right_ref[t],
            (((1,), (1,)), ((), ())),
            preferred_element_type=jnp.float32,
        )
        for s in range(sec_dev):
            target = lax.rem(base_ref[0] + s + targets - shift_ref[k], targets)
            total[target] += coef_ref[k, target] * product[s * rows : (s + 1) * rows]

    @pl.when(step == pl.num_programs(0) - 1)
    def _():
        if not split:
            outs[0][...] = total[...]
        else:
            groups = len(outs) // 2
            first = side_ref[0] == 0
            half = width // 2
            for g in range(groups):
                low = total[g * sec_dev : (g + 1) * sec_dev, :, :half]
                high = total[g * sec_dev : (g + 1) * sec_dev, :, half:]
                outs[g][...] = jnp.where(first, low, high)
                outs[groups + g][...] = jnp.where(first, high, low).astype(jnp.bfloat16)


def summed(shift, coef, base, side, mixed, right_ops, split):
    k_dev, sec_dev, rows, width = mixed.shape
    targets = coef.shape[1]
    if split:
        shape = (sec_dev, rows, width // 2)
        groups = targets // sec_dev
        outs = [jax.ShapeDtypeStruct(shape, jnp.float32)] * groups
        outs += [jax.ShapeDtypeStruct(shape, jnp.bfloat16)] * groups
    else:
        outs = [jax.ShapeDtypeStruct((targets, rows, width), jnp.float32)]
    return pl.pallas_call(
        functools.partial(sum_kernel, split),
        grid=(k_dev // SUM_TERMS,),
        out_shape=outs,
        in_specs=[pl.BlockSpec(memory_space=pltpu.SMEM)] * 4
        + [
            pl.BlockSpec((SUM_TERMS, sec_dev, rows, width), lambda i: (i, 0, 0, 0)),
            pl.BlockSpec((SUM_TERMS, width, width), lambda i: (i, 0, 0)),
        ],
        out_specs=[pl.BlockSpec(out.shape, lambda i: (0, 0, 0)) for out in outs],
        scratch_shapes=[pltpu.VMEM((targets, rows, width), jnp.float32)],
        compiler_params=pltpu.CompilerParams(
            vmem_limit_bytes=VMEM_BYTES + 3 * targets * rows * width * 4
        ),
        cost_estimate=pl.CostEstimate(
            flops=2 * k_dev * sec_dev * rows * width * width,
            bytes_accessed=2 * (mixed.size + right_ops.size),
            transcendentals=0,
        ),
    )(shift, coef, base, side, mixed, right_ops)


def shift_by(value, axis, distance):
    size = lax.axis_size(axis)
    return lax.ppermute(value, axis, [(i, (i + distance) % size) for i in range(size)])


def per_device(wavefunction, left_ops, right_ops, site_coef, coupled, sector_shift):
    sec_dev = wavefunction.shape[0]
    devices = lax.axis_size("sector")
    live = jnp.where(coupled > 0, site_coef, 0.0)
    shift = lax.rem(sector_shift, sec_dev * devices)
    side = jnp.reshape(lax.axis_index("op"), (1,)).astype(jnp.int32)
    me = lax.axis_index("sector")

    if lax.axis_size("op") == 2 and devices <= 4:
        coefs = [live] + [shift_by(live, "sector", -g) for g in range(1, devices)]
        mixed = mix(left_ops, wavefunction)
        coef = jnp.concatenate(coefs, axis=1)
        base = jnp.zeros((1,), jnp.int32)
        parts = summed(shift, coef, base, side, mixed, right_ops, True)
        mine, theirs = parts[:devices], parts[devices:]
        order = sorted(range(devices), key=lambda g: (g == 0, abs(2 * g - devices)))
        crossed = {g: shift_by(theirs[g], "op", 1) for g in order}
        sigma = mine[0] + crossed[0].astype(jnp.float32)
        for g in order[:-1]:
            both = (mine[g] + crossed[g].astype(jnp.float32)).astype(jnp.bfloat16)
            sigma = sigma + shift_by(both, "sector", g).astype(jnp.float32)
        return sigma

    coef = lax.all_gather(live, "sector", axis=1, tiled=True)
    mixed = mix(left_ops, wavefunction)
    base = jnp.reshape(me * sec_dev, (1,)).astype(jnp.int32)
    (total,) = summed(shift, coef, base, side, mixed, right_ops, False)
    total = lax.psum_scatter(total, "op", scatter_dimension=2, tiled=True)
    return lax.psum_scatter(total, "sector", scatter_dimension=0, tiled=True)


def solution(mesh):
    placed = (
        P(("groups", "sector"), None, None),
        P(("groups", "op"), "rep", None),
        P(("groups", "op"), None, None),
        P(("groups", "op"), "sector"),
        P(("groups", "op"), "sector"),
        P(("groups", "op")),
    )
    return jax.shard_map(
        per_device,
        mesh=mesh,
        in_specs=placed,
        out_specs=P(("groups", "sector"), "rep", "op"),
        check_vma=False,
    )
```

```python
import functools

import jax
import jax.numpy as jnp
from jax import lax
from jax.experimental import pallas as pl
from jax.experimental.pallas import tpu as pltpu
from jax.sharding import PartitionSpec as P

MIX_TERMS = 8
SUM_TERMS = 4
MIB = 1024 * 1024


def mix_kernel(split, side_ref, wave_ref, left_ref, right_ref, mixed_ref, held_ref, wave, left, sems):
    sec_dev = wave.shape[0]
    terms, rows, width = left.shape
    chunks = terms // MIX_TERMS

    def left_copy(c):
        part = pl.ds(c * MIX_TERMS, MIX_TERMS)
        return pltpu.make_async_copy(left_ref.at[part], left.at[part], sems.at[3 + c])

    wave_copy = pltpu.make_async_copy(wave_ref, wave, sems.at[0])
    wave_copy.start()
    for c in range(chunks):
        left_copy(c).start()
    if split:
        half = width // 2
        mine = pl.multiple_of(side_ref[0] * half, half)
        theirs = pl.multiple_of((1 - side_ref[0]) * half, half)
        right_copies = [
            pltpu.make_async_copy(
                right_ref.at[:, pl.ds(theirs, half)], held_ref.at[:, pl.ds(0, half)], sems.at[1]
            ),
            pltpu.make_async_copy(
                right_ref.at[:, pl.ds(mine, half)], held_ref.at[:, pl.ds(half, half)], sems.at[2]
            ),
        ]
    else:
        right_copies = [pltpu.make_async_copy(right_ref, held_ref, sems.at[1])]
    for copy in right_copies:
        copy.start()
    wave_copy.wait()

    @pl.loop(0, chunks)
    def _(c):
        left_copy(c).wait()
        part = pl.ds(c * MIX_TERMS, MIX_TERMS)
        rows_in = left[part].reshape(MIX_TERMS * rows, width)
        for s in range(sec_dev):
            product = jnp.dot(rows_in, wave[s], preferred_element_type=jnp.float32)
            mixed_ref[part, s] = product.astype(jnp.bfloat16).reshape(MIX_TERMS, rows, width)

    for copy in right_copies:
        copy.wait()


def mix(side, wavefunction, left_ops, right_ops, split):
    k_dev, rows, width = left_ops.shape
    sec_dev = wavefunction.shape[0]
    return pl.pallas_call(
        functools.partial(mix_kernel, split),
        out_shape=[
            pltpu.VMEM((k_dev, sec_dev, rows, width), jnp.bfloat16),
            pltpu.VMEM(right_ops.shape, jnp.bfloat16),
        ],
        in_specs=[pl.BlockSpec(memory_space=pltpu.SMEM)] + [pl.BlockSpec(memory_space=pltpu.HBM)] * 3,
        out_specs=[pl.BlockSpec(memory_space=pltpu.VMEM)] * 2,
        scratch_shapes=[
            pltpu.VMEM(wavefunction.shape, jnp.bfloat16),
            pltpu.VMEM(left_ops.shape, jnp.bfloat16),
            pltpu.SemaphoreType.DMA((3 + k_dev // MIX_TERMS,)),
        ],
        compiler_params=pltpu.CompilerParams(vmem_limit_bytes=24 * MIB),
        cost_estimate=pl.CostEstimate(
            flops=2 * k_dev * sec_dev * rows * width * width,
            bytes_accessed=2 * (left_ops.size + right_ops.size),
            transcendentals=0,
        ),
    )(
        side,
        *(pltpu.with_memory_space_constraint(x, pltpu.HBM) for x in (wavefunction, left_ops, right_ops)),
    )


def sum_kernel(split, base_ref, shift_ref, coef_ref, mixed_ref, held_ref, *refs):
    terms, sec_dev, rows, width = mixed_ref.shape
    targets = coef_ref.shape[0]
    half = width // 2
    mine = refs[0]
    mine[...] = jnp.zeros_like(mine)
    if split:
        theirs, total = refs[1:-1], refs[-1]
        total[...] = jnp.zeros_like(total)

    @pl.loop(0, terms // SUM_TERMS)
    def _(step):
        for t in range(SUM_TERMS):
            k = step * SUM_TERMS + t
            product = lax.dot_general(
                mixed_ref[k].reshape(sec_dev * rows, width),
                held_ref[k],
                (((1,), (1,)), ((), ())),
                preferred_element_type=jnp.float32,
            )
            for s in range(sec_dev):
                target = lax.rem(base_ref[0] + s + targets - shift_ref[k], targets)
                scaled = coef_ref[target, k] * product[s * rows : (s + 1) * rows]
                if split:
                    total[target] += scaled[:, :half]
                    mine[target] += scaled[:, half:]
                else:
                    mine[target] += scaled

    if split:
        for g, out in enumerate(theirs):
            out[...] = total[g * sec_dev : (g + 1) * sec_dev].astype(jnp.bfloat16)


def summed(base, shift, coef, mixed, held, split):
    k_dev, sec_dev, rows, width = mixed.shape
    targets = coef.shape[0]
    if split:
        out_shape = [pltpu.VMEM((targets, rows, width // 2), jnp.float32)]
        out_shape += [pltpu.VMEM((sec_dev, rows, width // 2), jnp.bfloat16)] * (targets // sec_dev)
        scratch = [pltpu.VMEM((targets, rows, width // 2), jnp.float32)]
    else:
        out_shape = [pltpu.VMEM((targets, rows, width), jnp.float32)]
        scratch = []
    return pl.pallas_call(
        functools.partial(sum_kernel, split),
        out_shape=out_shape,
        in_specs=[pl.BlockSpec(memory_space=pltpu.SMEM)] * 3
        + [pl.BlockSpec(memory_space=pltpu.VMEM)] * 2,
        out_specs=[pl.BlockSpec(memory_space=pltpu.VMEM)] * len(out_shape),
        scratch_shapes=scratch,
        compiler_params=pltpu.CompilerParams(vmem_limit_bytes=24 * MIB),
        cost_estimate=pl.CostEstimate(
            flops=2 * k_dev * sec_dev * rows * width * width,
            bytes_accessed=2 * (mixed.size + held.size),
            transcendentals=0,
        ),
    )(
        base,
        shift,
        coef,
        pltpu.with_memory_space_constraint(mixed, pltpu.VMEM),
        pltpu.with_memory_space_constraint(held, pltpu.VMEM),
    )


def shift_by(value, axis, distance):
    size = lax.axis_size(axis)
    return lax.ppermute(value, axis, [(i, (i + distance) % size) for i in range(size)])


def after(value, other):
    return lax.optimization_barrier((value, other))[0]


def per_device(wavefunction, left_ops, right_ops, site_coef, coupled, sector_shift):
    sec_dev = wavefunction.shape[0]
    devices = lax.axis_size("sector")
    live = jnp.where(coupled.T > 0, site_coef.T, 0.0)
    shift = lax.rem(sector_shift, sec_dev * devices)
    side = jnp.reshape(lax.axis_index("op"), (1,)).astype(jnp.int32)
    me = lax.axis_index("sector")

    if lax.axis_size("op") == 2 and devices <= 4:
        coefs = [live] + [shift_by(live, "sector", -g) for g in range(1, devices)]
        mixed, held = mix(side, wavefunction, left_ops, right_ops, True)
        base = jnp.zeros((1,), jnp.int32)
        mine, *theirs = summed(base, shift, jnp.concatenate(coefs, axis=0), mixed, held, True)
        mine = [mine[g * sec_dev : (g + 1) * sec_dev] for g in range(devices)]
        order = sorted(range(1, devices), key=lambda g: abs(2 * g - devices))
        crossed = {g: shift_by(theirs[g], "op", 1) for g in order}
        arrived, both = [], None
        for g in order:
            other = crossed[g] if both is None else after(crossed[g], both)
            both = (mine[g] + other.astype(jnp.float32)).astype(jnp.bfloat16)
            if not arrived:
                theirs[0] = after(theirs[0], both)
            arrived.append(shift_by(both, "sector", g))
        sigma = mine[0] + shift_by(theirs[0], "op", 1).astype(jnp.float32)
        for other in arrived:
            sigma = sigma + other.astype(jnp.float32)
        return sigma

    coef = lax.all_gather(live, "sector", axis=0, tiled=True)
    mixed, held = mix(side, wavefunction, left_ops, right_ops, False)
    base = jnp.reshape(me * sec_dev, (1,)).astype(jnp.int32)
    (total,) = summed(base, shift, coef, mixed, held, False)
    total = lax.psum_scatter(total, "op", scatter_dimension=2, tiled=True)
    return lax.psum_scatter(total, "sector", scatter_dimension=0, tiled=True)


def solution(mesh):
    placed = (
        P(("groups", "sector"), None, None),
        P(("groups", "op"), "rep", None),
        P(("groups", "op"), None, None),
        P(("groups", "op"), "sector"),
        P(("groups", "op"), "sector"),
        P(("groups", "op")),
    )
    return jax.shard_map(
        per_device,
        mesh=mesh,
        in_specs=placed,
        out_specs=P(("groups", "sector"), "rep", "op"),
        check_vma=False,
    )
```

```python
import functools

import jax
import jax.numpy as jnp
from jax import lax
from jax.experimental import pallas as pl
from jax.experimental.pallas import tpu as pltpu
from jax.sharding import PartitionSpec as P

PAIRS_A_STEP = 8
MIB = 1024 * 1024


def list_words(terms, sec_dev):
    return terms * sec_dev + 2 * PAIRS_A_STEP


def load_kernel(split, groups, side_ref, shift_ref, wave_ref, left_ref, right_ref, *refs):
    wave, left, right, lists, sems = refs
    terms, width = right.shape[:2]
    sec_dev = wave.shape[0]
    targets = groups * sec_dev
    words = list_words(terms, sec_dev)
    half = width // 2
    copies = [
        pltpu.make_async_copy(wave_ref, wave, sems.at[0]),
        pltpu.make_async_copy(left_ref, left, sems.at[1]),
    ]
    if split:
        theirs = pl.multiple_of((1 - side_ref[0]) * half, half)
        mine = pl.multiple_of(side_ref[0] * half, half)
        for at, (low, high) in enumerate(((theirs, 0), (mine, half))):
            source = right_ref.at[:, pl.ds(low, half)]
            copies.append(
                pltpu.make_async_copy(source, right.at[:, pl.ds(high, half)], sems.at[2 + at])
            )
    else:
        copies.append(pltpu.make_async_copy(right_ref, right, sems.at[2]))
    for copy in copies:
        copy.start()

    for g in range(groups):
        lists[(g + 1) * words - 1] = 0

    @pl.loop(0, terms)
    def _(k):
        for s in range(sec_dev):
            target = lax.rem(s + targets - shift_ref[k], targets)
            group = lax.div(target, sec_dev)
            start = group * words
            count = lists[start + words - 1]
            lists[start + count] = (k * sec_dev + s) * sec_dev + lax.rem(target, sec_dev)
            lists[start + words - 1] = count + 1

    for copy in copies:
        copy.wait()


def load(side, shift, wavefunction, left_ops, right_ops, groups, split):
    k_dev = left_ops.shape[0]
    sec_dev = wavefunction.shape[0]
    arrays = (wavefunction, left_ops, right_ops)
    return pl.pallas_call(
        functools.partial(load_kernel, split, groups),
        out_shape=[pltpu.VMEM(x.shape, x.dtype) for x in arrays]
        + [jax.ShapeDtypeStruct((groups * list_words(k_dev, sec_dev),), jnp.int32)],
        in_specs=[pl.BlockSpec(memory_space=pltpu.SMEM)] * 2
        + [pl.BlockSpec(memory_space=pltpu.HBM)] * 3,
        out_specs=[pl.BlockSpec(memory_space=pltpu.VMEM)] * 3
        + [pl.BlockSpec(memory_space=pltpu.SMEM)],
        scratch_shapes=[pltpu.SemaphoreType.DMA((4,))],
        compiler_params=pltpu.CompilerParams(vmem_limit_bytes=24 * MIB),
        cost_estimate=pl.CostEstimate(
            flops=0, bytes_accessed=4 * (left_ops.size + right_ops.size), transcendentals=0
        ),
    )(side, *(pltpu.with_memory_space_constraint(x, pltpu.HBM) for x in (shift, *arrays)))


def group_kernel(split, group, coef_ref, lists_ref, wave_ref, left_ref, right_ref, *refs):
    pairs, weights = refs[-2:]
    terms, rows, width = left_ref.shape
    sec_dev = wave_ref.shape[0]
    half = width // 2
    words = list_words(terms, sec_dev)
    start = group * words
    mine = refs[0]
    mine[...] = jnp.zeros_like(mine)
    if split:
        theirs, total = refs[1:3]
        total[...] = jnp.zeros_like(total)

    def keep(i, kept):
        triple = lists_ref[start + i]
        k = lax.div(triple, sec_dev * sec_dev)
        weight = coef_ref[group * sec_dev + lax.rem(triple, sec_dev), k]
        pairs[kept] = triple
        weights[kept] = weight
        return kept + (weight != 0.0).astype(jnp.int32)

    kept = lax.fori_loop(0, lists_ref[start + words - 1], keep, 0)
    for i in range(PAIRS_A_STEP):
        pairs[kept + i] = 0
        weights[kept + i] = 0.0

    @pl.loop(0, lax.div(kept + PAIRS_A_STEP - 1, PAIRS_A_STEP))
    def _(step):
        triples = [pairs[step * PAIRS_A_STEP + i] for i in range(PAIRS_A_STEP)]
        terms_of = [lax.div(triple, sec_dev * sec_dev) for triple in triples]
        mixed = [
            jnp.dot(
                left_ref[k],
                wave_ref[lax.rem(lax.div(triple, sec_dev), sec_dev)],
                preferred_element_type=jnp.float32,
            ).astype(jnp.bfloat16)
            for triple, k in zip(triples, terms_of)
        ]
        for i, (triple, k) in enumerate(zip(triples, terms_of)):
            product = lax.dot_general(
                mixed[i],
                right_ref[k],
                (((1,), (1,)), ((), ())),
                preferred_element_type=jnp.float32,
            )
            scaled = weights[step * PAIRS_A_STEP + i] * product
            target = lax.rem(triple, sec_dev)
            if split:
                total[target] += scaled[:, :half]
                mine[target] += scaled[:, half:]
            else:
                mine[target] += scaled

    if split:
        theirs[...] = total[...].astype(jnp.bfloat16)


def group_sum(group, coef, lists, wave, left, right, split):
    k_dev, rows, width = left.shape
    sec_dev = wave.shape[0]
    words = list_words(k_dev, sec_dev)
    columns = width // 2 if split else width
    shape = (sec_dev, rows, columns)
    out_shape = [pltpu.VMEM(shape, jnp.float32)]
    scratch = [pltpu.SMEM((words,), jnp.int32), pltpu.SMEM((words,), jnp.float32)]
    if split:
        out_shape.append(pltpu.VMEM(shape, jnp.bfloat16))
        scratch = [pltpu.VMEM(shape, jnp.float32)] + scratch
    return pl.pallas_call(
        functools.partial(group_kernel, split, group),
        out_shape=out_shape,
        in_specs=[pl.BlockSpec(memory_space=pltpu.SMEM)] * 2
        + [pl.BlockSpec(memory_space=pltpu.VMEM)] * 3,
        out_specs=[pl.BlockSpec(memory_space=pltpu.VMEM)] * len(out_shape),
        scratch_shapes=scratch,
        compiler_params=pltpu.CompilerParams(vmem_limit_bytes=24 * MIB),
        cost_estimate=pl.CostEstimate(
            flops=k_dev * rows * width * width * 2,
            bytes_accessed=left.size + right.size,
            transcendentals=0,
        ),
    )(coef, lists, *(pltpu.with_memory_space_constraint(x, pltpu.VMEM) for x in (wave, left, right)))


def shift_by(value, axis, distance):
    size = lax.axis_size(axis)
    return lax.ppermute(value, axis, [(i, (i + distance) % size) for i in range(size)])


def after(value, other):
    return lax.optimization_barrier((value, other))[0]


def per_device(wavefunction, left_ops, right_ops, site_coef, coupled, sector_shift):
    sec_dev = wavefunction.shape[0]
    devices = lax.axis_size("sector")
    live = jnp.where(coupled.T > 0, site_coef.T, 0.0)
    side = jnp.reshape(lax.axis_index("op"), (1,)).astype(jnp.int32)
    split = lax.axis_size("op") == 2 and devices <= 4
    held = load(side, sector_shift, wavefunction, left_ops, right_ops, devices, split)
    wave, left, right, lists = held

    if split:
        coefs = [live] + [shift_by(live, "sector", -g) for g in range(1, devices)]
        coef = jnp.concatenate(coefs, axis=0)
        order = sorted(range(1, devices), key=lambda g: abs(2 * g - devices)) + [0]
        mine, crossed, arrived = {}, {}, []
        for at, g in enumerate(order):
            mine[g], theirs = group_sum(g, coef, lists, wave, left, right, True)
            crossed[g] = shift_by(theirs, "op", 1)
            coef = after(coef, theirs)
            if at > 0:
                last = order[at - 1]
                other = after(crossed[last], theirs)
                both = (mine[last] + other.astype(jnp.float32)).astype(jnp.bfloat16)
                arrived.append(shift_by(both, "sector", last))
                coef = after(coef, both)
        sigma = mine[0] + crossed[0].astype(jnp.float32)
        for other in arrived:
            sigma = sigma + other.astype(jnp.float32)
        return sigma

    first = lax.axis_index("sector") * sec_dev
    coef = jnp.roll(lax.all_gather(live, "sector", axis=0, tiled=True), -first, axis=0)
    parts = [group_sum(g, coef, lists, wave, left, right, False)[0] for g in range(devices)]
    total = jnp.roll(jnp.concatenate(parts, axis=0), first, axis=0)
    total = lax.psum_scatter(total, "op", scatter_dimension=2, tiled=True)
    return lax.psum_scatter(total, "sector", scatter_dimension=0, tiled=True)


def solution(mesh):
    placed = (
        P(("groups", "sector"), None, None),
        P(("groups", "op"), "rep", None),
        P(("groups", "op"), None, None),
        P(("groups", "op"), "sector"),
        P(("groups", "op"), "sector"),
        P(("groups", "op")),
    )
    return jax.shard_map(
        per_device,
        mesh=mesh,
        in_specs=placed,
        out_specs=P(("groups", "sector"), "rep", "op"),
        check_vma=False,
    )
```

```python
import functools

import jax
import jax.numpy as jnp
from jax import lax
from jax.experimental import pallas as pl
from jax.experimental.pallas import tpu as pltpu
from jax.sharding import PartitionSpec as P

MIX_TERMS = 8
PAIRS_A_STEP = 8
FIELD = 256
MIB = 1024 * 1024


def wrapped(value, size):
    if size & (size - 1) == 0:
        return value & (size - 1)
    return lax.rem(value + size, size)


def divided(value, size):
    if size & (size - 1) == 0:
        return value >> (size.bit_length() - 1)
    return lax.div(value, size)


def list_words(pairs):
    return pairs + 2 * PAIRS_A_STEP


def slot_of(target, batch, sec_dev):
    if len(batch) == 1:
        return divided(target, sec_dev) == batch[0], wrapped(target, sec_dev)
    if batch == list(range(len(batch))):
        return divided(target, sec_dev) < len(batch), target
    held, place = False, 0
    for at, group in enumerate(batch):
        here = divided(target, sec_dev) == group
        held = held | here
        place = jnp.where(here, at * sec_dev, place)
    return held, place + wrapped(target, sec_dev)


def mix_kernel(split, batches, targets, side_ref, shift_ref, wave_ref, left_ref, right_ref, *refs):
    mixed_ref, held_ref, lists, wave, left, sems = refs
    sec_dev = wave.shape[0]
    terms, rows, width = left.shape
    chunks = terms // MIX_TERMS
    words = list_words(terms * sec_dev)

    def left_copy(c):
        part = pl.ds(c * MIX_TERMS, MIX_TERMS)
        return pltpu.make_async_copy(left_ref.at[part], left.at[part], sems.at[3 + c])

    wave_copy = pltpu.make_async_copy(wave_ref, wave, sems.at[0])
    wave_copy.start()
    for c in range(chunks):
        left_copy(c).start()
    if split:
        half = width // 2
        mine = pl.multiple_of(side_ref[0] * half, half)
        theirs = pl.multiple_of((1 - side_ref[0]) * half, half)
        right_copies = [
            pltpu.make_async_copy(
                right_ref.at[:, pl.ds(theirs, half)], held_ref.at[:, pl.ds(0, half)], sems.at[1]
            ),
            pltpu.make_async_copy(
                right_ref.at[:, pl.ds(mine, half)], held_ref.at[:, pl.ds(half, half)], sems.at[2]
            ),
        ]
    else:
        right_copies = [pltpu.make_async_copy(right_ref, held_ref, sems.at[1])]
    for copy in right_copies:
        copy.start()

    def add_term(k, counts):
        counts = list(counts)
        for s in range(sec_dev):
            target = wrapped(s - shift_ref[k], targets)
            for b, batch in enumerate(batches):
                held, slot = slot_of(target, batch, sec_dev)
                lists[b * words + counts[b]] = ((k * sec_dev + s) * FIELD + slot) * FIELD + target
                counts[b] = counts[b] + jnp.where(held, 1, 0)
        return tuple(counts)

    counts = lax.fori_loop(0, terms, add_term, (0,) * len(batches))
    for b, count in enumerate(counts):
        lists[(b + 1) * words - 1] = count
    wave_copy.wait()

    @pl.loop(0, chunks)
    def _(c):
        left_copy(c).wait()
        part = pl.ds(c * MIX_TERMS, MIX_TERMS)
        rows_in = left[part].reshape(MIX_TERMS * rows, width)
        for s in range(sec_dev):
            product = jnp.dot(rows_in, wave[s], preferred_element_type=jnp.float32)
            mixed_ref[part, s] = product.astype(jnp.bfloat16).reshape(MIX_TERMS, rows, width)

    for copy in right_copies:
        copy.wait()


def mix(side, shift, wavefunction, left_ops, right_ops, batches, targets, split):
    k_dev, rows, width = left_ops.shape
    sec_dev = wavefunction.shape[0]
    arrays = (shift, wavefunction, left_ops, right_ops)
    return pl.pallas_call(
        functools.partial(mix_kernel, split, batches, targets),
        out_shape=[
            pltpu.VMEM((k_dev, sec_dev, rows, width), jnp.bfloat16),
            pltpu.VMEM(right_ops.shape, jnp.bfloat16),
            jax.ShapeDtypeStruct((len(batches) * list_words(k_dev * sec_dev),), jnp.int32),
        ],
        in_specs=[pl.BlockSpec(memory_space=pltpu.SMEM)] * 2
        + [pl.BlockSpec(memory_space=pltpu.HBM)] * 3,
        out_specs=[pl.BlockSpec(memory_space=pltpu.VMEM)] * 2
        + [pl.BlockSpec(memory_space=pltpu.SMEM)],
        scratch_shapes=[
            pltpu.VMEM(wavefunction.shape, jnp.bfloat16),
            pltpu.VMEM(left_ops.shape, jnp.bfloat16),
            pltpu.SemaphoreType.DMA((3 + k_dev // MIX_TERMS,)),
        ],
        compiler_params=pltpu.CompilerParams(vmem_limit_bytes=24 * MIB),
        cost_estimate=pl.CostEstimate(
            flops=2 * k_dev * sec_dev * rows * width * width,
            bytes_accessed=2 * (left_ops.size + right_ops.size),
            transcendentals=0,
        ),
    )(side, *(pltpu.with_memory_space_constraint(x, pltpu.HBM) for x in arrays))


def sum_kernel(split, number, coef_ref, lists_ref, mixed_ref, held_ref, *refs):
    pairs, weights = refs[-2:]
    terms, sec_dev, rows, width = mixed_ref.shape
    half = width // 2
    words = list_words(terms * sec_dev)
    start = number * words
    mine = refs[0]
    mine[...] = jnp.zeros_like(mine)
    if split:
        theirs, total = refs[1:-3], refs[-3]
        total[...] = jnp.zeros_like(total)

    def keep(i, kept):
        entry = lists_ref[start + i]
        k = divided(divided(entry, FIELD * FIELD), sec_dev)
        weight = coef_ref[wrapped(entry, FIELD), k]
        pairs[kept] = divided(entry, FIELD)
        weights[kept] = weight
        return kept + jnp.where(weight != 0.0, 1, 0)

    kept = lax.fori_loop(0, lists_ref[start + words - 1], keep, 0)
    for i in range(PAIRS_A_STEP):
        pairs[kept + i] = 0
        weights[kept + i] = 0.0

    @pl.loop(0, divided(kept + PAIRS_A_STEP - 1, PAIRS_A_STEP))
    def _(step):
        for i in range(PAIRS_A_STEP):
            pair = pairs[step * PAIRS_A_STEP + i]
            place = divided(pair, FIELD)
            slot = wrapped(pair, FIELD)
            k = divided(place, sec_dev)
            product = lax.dot_general(
                mixed_ref[k, wrapped(place, sec_dev)],
                held_ref[k],
                (((1,), (1,)), ((), ())),
                preferred_element_type=jnp.float32,
            )
            scaled = weights[step * PAIRS_A_STEP + i] * product
            if split:
                total[slot] += scaled[:, :half]
                mine[slot] += scaled[:, half:]
            else:
                mine[slot] += scaled

    if split:
        for g, out in enumerate(theirs):
            out[...] = total[g * sec_dev : (g + 1) * sec_dev].astype(jnp.bfloat16)


def summed(number, batch, coef, lists, mixed, held, split):
    k_dev, sec_dev, rows, width = mixed.shape
    words = list_words(k_dev * sec_dev)
    slots = len(batch) * sec_dev
    columns = width // 2 if split else width
    out_shape = [pltpu.VMEM((slots, rows, columns), jnp.float32)]
    scratch = [pltpu.SMEM((words,), jnp.int32), pltpu.SMEM((words,), jnp.float32)]
    if split:
        out_shape += [pltpu.VMEM((sec_dev, rows, columns), jnp.bfloat16)] * len(batch)
        scratch = [pltpu.VMEM((slots, rows, columns), jnp.float32)] + scratch
    return pl.pallas_call(
        functools.partial(sum_kernel, split, number),
        out_shape=out_shape,
        in_specs=[pl.BlockSpec(memory_space=pltpu.SMEM)] * 2
        + [pl.BlockSpec(memory_space=pltpu.VMEM)] * 2,
        out_specs=[pl.BlockSpec(memory_space=pltpu.VMEM)] * len(out_shape),
        scratch_shapes=scratch,
        compiler_params=pltpu.CompilerParams(vmem_limit_bytes=24 * MIB),
        cost_estimate=pl.CostEstimate(
            flops=2 * k_dev * slots * rows * width * width // 4,
            bytes_accessed=2 * (mixed.size + held.size),
            transcendentals=0,
        ),
    )(
        coef,
        lists,
        pltpu.with_memory_space_constraint(mixed, pltpu.VMEM),
        pltpu.with_memory_space_constraint(held, pltpu.VMEM),
    )


def shift_by(value, axis, distance):
    size = lax.axis_size(axis)
    return lax.ppermute(value, axis, [(i, (i + distance) % size) for i in range(size)])


def after(value, other):
    return lax.optimization_barrier((value, other))[0]


def per_device(wavefunction, left_ops, right_ops, site_coef, coupled, sector_shift):
    sec_dev = wavefunction.shape[0]
    devices = lax.axis_size("sector")
    live = jnp.where(coupled.T > 0, site_coef.T, 0.0)
    side = jnp.reshape(lax.axis_index("op"), (1,)).astype(jnp.int32)
    split = lax.axis_size("op") == 2 and devices <= 4

    if split:
        far, *near = sorted(range(1, devices), key=lambda g: abs(2 * g - devices))
        batches = [[far], near, [0]]
    else:
        batches = [list(range(devices))]
    targets = devices * sec_dev
    mixed, held, lists = mix(
        side, sector_shift, wavefunction, left_ops, right_ops, batches, targets, split
    )

    if split:
        coefs = [live] + [shift_by(live, "sector", -g) for g in range(1, devices)]
        coef = jnp.concatenate(coefs, axis=0)
        mine, crossed, arrived, both = {}, {}, [], None

        def pass_on(g):
            other = crossed[g] if both is None else after(crossed[g], both)
            summed_up = (mine[g] + other.astype(jnp.float32)).astype(jnp.bfloat16)
            arrived.append(shift_by(summed_up, "sector", g))
            return summed_up

        for number, batch in enumerate(batches):
            sums, *theirs = summed(number, batch, coef, lists, mixed, held, True)
            for at, g in enumerate(batch):
                mine[g] = sums[at * sec_dev : (at + 1) * sec_dev]
                crossed[g] = shift_by(theirs[at], "op", 1)
            coef = after(coef, sums)
            if number == 1:
                crossed[far] = after(crossed[far], sums)
                both = pass_on(far)
                coef = after(coef, both)
        for g in near:
            both = pass_on(g)
        sigma = mine[0] + crossed[0].astype(jnp.float32)
        for other in arrived:
            sigma = sigma + other.astype(jnp.float32)
        return sigma

    first = lax.axis_index("sector") * sec_dev
    coef = jnp.roll(lax.all_gather(live, "sector", axis=0, tiled=True), -first, axis=0)
    (total,) = summed(0, batches[0], coef, lists, mixed, held, False)
    total = jnp.roll(total, first, axis=0)
    total = lax.psum_scatter(total, "op", scatter_dimension=2, tiled=True)
    return lax.psum_scatter(total, "sector", scatter_dimension=0, tiled=True)


def solution(mesh):
    placed = (
        P(("groups", "sector"), None, None),
        P(("groups", "op"), "rep", None),
        P(("groups", "op"), None, None),
        P(("groups", "op"), "sector"),
        P(("groups", "op"), "sector"),
        P(("groups", "op")),
    )
    return jax.shard_map(
        per_device,
        mesh=mesh,
        in_specs=placed,
        out_specs=P(("groups", "sector"), "rep", "op"),
        check_vma=False,
    )
```

```python
import functools

import jax
import jax.numpy as jnp
from jax import lax
from jax.experimental import pallas as pl
from jax.experimental.pallas import tpu as pltpu
from jax.sharding import PartitionSpec as P

BLOCK_TERMS = 8
MIB = 1024 * 1024


def wrapped(value, size):
    if size & (size - 1) == 0:
        return value & (size - 1)
    return lax.rem(value + size, size)


def sigma_kernel(split, side_ref, shift_ref, coef_ref, wave_ref, left_ref, right_ref, *refs):
    wave, left, right, even, odd, wave_sem, left_sems, right_sems = refs[-8:]
    terms, rows, width = left.shape
    sec_dev = wave.shape[0]
    targets = coef_ref.shape[0]
    blocks = terms // BLOCK_TERMS
    half = width // 2
    mine = refs[0]

    def part(block):
        return pl.ds(block * BLOCK_TERMS, BLOCK_TERMS)

    def left_copy(block):
        return pltpu.make_async_copy(
            left_ref.at[part(block)], left.at[part(block)], left_sems.at[block]
        )

    def right_copies(block):
        if not split:
            source, target = right_ref.at[part(block)], right.at[part(block)]
            return [pltpu.make_async_copy(source, target, right_sems.at[0, block])]
        copies = []
        for at, side in enumerate((1 - side_ref[0], side_ref[0])):
            source = right_ref.at[part(block), pl.ds(pl.multiple_of(side * half, half), half)]
            target = right.at[part(block), pl.ds(at * half, half)]
            copies.append(pltpu.make_async_copy(source, target, right_sems.at[at, block]))
        return copies

    def first_product(block, mixed):
        rows_in = left[part(block)].reshape(BLOCK_TERMS * rows, width)
        for s in range(sec_dev):
            product = jnp.dot(rows_in, wave[s], preferred_element_type=jnp.float32)
            mixed[:, s] = product.astype(jnp.bfloat16).reshape(BLOCK_TERMS, rows, width)

    def second_product(block, mixed):
        for t in range(BLOCK_TERMS):
            k = block * BLOCK_TERMS + t
            product = lax.dot_general(
                mixed[t].reshape(sec_dev * rows, width),
                right[k],
                (((1,), (1,)), ((), ())),
                preferred_element_type=jnp.float32,
            )
            for s in range(sec_dev):
                target = wrapped(s - shift_ref[k], targets)
                scaled = coef_ref[target, k] * product[s * rows : (s + 1) * rows]
                if split:
                    total[target] += scaled[:, :half]
                    mine[target] += scaled[:, half:]
                else:
                    mine[target] += scaled

    wave_copy = pltpu.make_async_copy(wave_ref, wave, wave_sem)
    wave_copy.start()
    for block in range(blocks):
        left_copy(block).start()
        for copy in right_copies(block):
            copy.start()
    mine[...] = jnp.zeros_like(mine)
    if split:
        theirs, total = refs[1:-9], refs[-9]
        total[...] = jnp.zeros_like(total)
    wave_copy.wait()
    left_copy(0).wait()
    first_product(0, even)

    @pl.loop(0, blocks // 2)
    def _(step):
        block = 2 * step
        left_copy(block + 1).wait()
        for copy in right_copies(block):
            copy.wait()
        first_product(block + 1, odd)
        second_product(block, even)
        for copy in right_copies(block + 1):
            copy.wait()

        @pl.when(block + 2 < blocks)
        def _():
            left_copy(block + 2).wait()
            first_product(block + 2, even)

        second_product(block + 1, odd)

    if split:
        for g, out in enumerate(theirs):
            out[...] = total[g * sec_dev : (g + 1) * sec_dev].astype(jnp.bfloat16)


def partial_sums(side, shift, coef, wavefunction, left_ops, right_ops, split):
    k_dev, rows, width = left_ops.shape
    sec_dev = wavefunction.shape[0]
    targets = coef.shape[0]
    blocks = k_dev // BLOCK_TERMS
    scratch = [pltpu.VMEM(x.shape, x.dtype) for x in (wavefunction, left_ops, right_ops)]
    scratch += [pltpu.VMEM((BLOCK_TERMS, sec_dev, rows, width), jnp.bfloat16)] * 2
    scratch += [
        pltpu.SemaphoreType.DMA(()),
        pltpu.SemaphoreType.DMA((blocks,)),
        pltpu.SemaphoreType.DMA((2, blocks)),
    ]
    if split:
        out_shape = [pltpu.VMEM((targets, rows, width // 2), jnp.float32)]
        out_shape += [pltpu.VMEM((sec_dev, rows, width // 2), jnp.bfloat16)] * (targets // sec_dev)
        scratch = [pltpu.VMEM((targets, rows, width // 2), jnp.float32)] + scratch
    else:
        out_shape = [pltpu.VMEM((targets, rows, width), jnp.float32)]
    return pl.pallas_call(
        functools.partial(sigma_kernel, split),
        out_shape=out_shape,
        in_specs=[pl.BlockSpec(memory_space=pltpu.SMEM)] * 3
        + [pl.BlockSpec(memory_space=pltpu.HBM)] * 3,
        out_specs=[pl.BlockSpec(memory_space=pltpu.VMEM)] * len(out_shape),
        scratch_shapes=scratch,
        compiler_params=pltpu.CompilerParams(vmem_limit_bytes=40 * MIB),
        cost_estimate=pl.CostEstimate(
            flops=4 * k_dev * sec_dev * rows * width * width,
            bytes_accessed=2 * (left_ops.size + right_ops.size),
            transcendentals=0,
        ),
    )(
        side,
        pltpu.with_memory_space_constraint(shift, pltpu.HBM),
        coef,
        *(pltpu.with_memory_space_constraint(x, pltpu.HBM) for x in (wavefunction, left_ops, right_ops)),
    )


def shift_by(value, axis, distance):
    size = lax.axis_size(axis)
    return lax.ppermute(value, axis, [(i, (i + distance) % size) for i in range(size)])


def after(value, other):
    return lax.optimization_barrier((value, other))[0]


def per_device(wavefunction, left_ops, right_ops, site_coef, coupled, sector_shift):
    sec_dev = wavefunction.shape[0]
    devices = lax.axis_size("sector")
    live = jnp.where(coupled.T > 0, site_coef.T, 0.0)
    side = jnp.reshape(lax.axis_index("op"), (1,)).astype(jnp.int32)
    arrays = (wavefunction, left_ops, right_ops)

    if lax.axis_size("op") == 2 and devices <= 4:
        coefs = [live] + [shift_by(live, "sector", -g) for g in range(1, devices)]
        coef = jnp.concatenate(coefs, axis=0)
        mine, *theirs = partial_sums(side, sector_shift, coef, *arrays, True)
        mine = [mine[g * sec_dev : (g + 1) * sec_dev] for g in range(devices)]
        order = sorted(range(1, devices), key=lambda g: abs(2 * g - devices))
        crossed = {g: shift_by(theirs[g], "op", 1) for g in order}
        arrived, both = [], None
        for g in order:
            other = crossed[g] if both is None else after(crossed[g], both)
            both = (mine[g] + other.astype(jnp.float32)).astype(jnp.bfloat16)
            if not arrived:
                theirs[0] = after(theirs[0], both)
            arrived.append(shift_by(both, "sector", g))
        sigma = mine[0] + after(shift_by(theirs[0], "op", 1), both).astype(jnp.float32)
        for other in arrived:
            sigma = lax.optimization_barrier(sigma) + other.astype(jnp.float32)
        return sigma

    first = lax.axis_index("sector") * sec_dev
    coef = jnp.roll(lax.all_gather(live, "sector", axis=0, tiled=True), -first, axis=0)
    (total,) = partial_sums(side, sector_shift, coef, *arrays, False)
    total = jnp.roll(total, first, axis=0)
    total = lax.psum_scatter(total, "op", scatter_dimension=2, tiled=True)
    return lax.psum_scatter(total, "sector", scatter_dimension=0, tiled=True)


def solution(mesh):
    placed = (
        P(("groups", "sector"), None, None),
        P(("groups", "op"), "rep", None),
        P(("groups", "op"), None, None),
        P(("groups", "op"), "sector"),
        P(("groups", "op"), "sector"),
        P(("groups", "op")),
    )
    return jax.shard_map(
        per_device,
        mesh=mesh,
        in_specs=placed,
        out_specs=P(("groups", "sector"), "rep", "op"),
        check_vma=False,
    )
```

```python
import functools

import jax
import jax.numpy as jnp
from jax import lax
from jax.experimental import pallas as pl
from jax.experimental.pallas import tpu as pltpu
from jax.sharding import PartitionSpec as P

MIX_TERMS = 8
SUM_TERMS = 4
MIB = 1024 * 1024


def wrapped(value, size):
    if size & (size - 1) == 0:
        return value & (size - 1)
    return lax.rem(value + size, size)


def mix_kernel(split, side_ref, wave_ref, left_ref, right_ref, mixed_ref, turned_ref, *refs):
    wave, left, right, wave_sem, left_sems, right_sems = refs
    sec_dev = wave.shape[0]
    terms, rows, width = left.shape
    blocks = terms // MIX_TERMS
    half = width // 2

    def part(block):
        return pl.ds(block * MIX_TERMS, MIX_TERMS)

    def left_copy(block):
        return pltpu.make_async_copy(
            left_ref.at[part(block)], left.at[part(block)], left_sems.at[block]
        )

    def right_copies(block):
        if not split:
            source, target = right_ref.at[part(block)], right.at[part(block)]
            return [pltpu.make_async_copy(source, target, right_sems.at[0, block])]
        copies = []
        for at, side in enumerate((1 - side_ref[0], side_ref[0])):
            source = right_ref.at[part(block), pl.ds(pl.multiple_of(side * half, half), half)]
            target = right.at[part(block), pl.ds(at * half, half)]
            copies.append(pltpu.make_async_copy(source, target, right_sems.at[at, block]))
        return copies

    wave_copy = pltpu.make_async_copy(wave_ref, wave, wave_sem)
    wave_copy.start()
    for block in range(blocks):
        left_copy(block).start()
        for copy in right_copies(block):
            copy.start()
    wave_copy.wait()

    @pl.loop(0, blocks)
    def _(block):
        left_copy(block).wait()
        for copy in right_copies(block):
            copy.wait()
        rows_in = left[part(block)].reshape(MIX_TERMS * rows, width)
        for s in range(sec_dev):
            product = jnp.dot(rows_in, wave[s], preferred_element_type=jnp.float32)
            mixed_ref[part(block), s] = product.astype(jnp.bfloat16).reshape(MIX_TERMS, rows, width)
        for t in range(MIX_TERMS):
            k = block * MIX_TERMS + t
            turned_ref[k] = right[k].T


def mix(side, wavefunction, left_ops, right_ops, split):
    k_dev, rows, width = left_ops.shape
    sec_dev = wavefunction.shape[0]
    blocks = k_dev // MIX_TERMS
    arrays = (wavefunction, left_ops, right_ops)
    return pl.pallas_call(
        functools.partial(mix_kernel, split),
        out_shape=[
            pltpu.VMEM((k_dev, sec_dev, rows, width), jnp.bfloat16),
            pltpu.VMEM(right_ops.shape, jnp.bfloat16),
        ],
        in_specs=[pl.BlockSpec(memory_space=pltpu.SMEM)] + [pl.BlockSpec(memory_space=pltpu.HBM)] * 3,
        out_specs=[pl.BlockSpec(memory_space=pltpu.VMEM)] * 2,
        scratch_shapes=[pltpu.VMEM(x.shape, x.dtype) for x in arrays]
        + [
            pltpu.SemaphoreType.DMA(()),
            pltpu.SemaphoreType.DMA((blocks,)),
            pltpu.SemaphoreType.DMA((2, blocks)),
        ],
        compiler_params=pltpu.CompilerParams(vmem_limit_bytes=32 * MIB),
        cost_estimate=pl.CostEstimate(
            flops=2 * k_dev * sec_dev * rows * width * width,
            bytes_accessed=2 * (left_ops.size + right_ops.size),
            transcendentals=0,
        ),
    )(side, *(pltpu.with_memory_space_constraint(x, pltpu.HBM) for x in arrays))


def sum_kernel(split, shift_ref, coef_ref, mixed_ref, turned_ref, *refs):
    terms, sec_dev, rows, width = mixed_ref.shape
    targets = coef_ref.shape[0]
    half = width // 2
    mine = refs[0]
    mine[...] = jnp.zeros_like(mine)
    if split:
        theirs, total = refs[1:-1], refs[-1]
        total[...] = jnp.zeros_like(total)

    @pl.loop(0, terms // SUM_TERMS)
    def _(step):
        for t in range(SUM_TERMS):
            k = step * SUM_TERMS + t
            product = jnp.dot(
                mixed_ref[k].reshape(sec_dev * rows, width),
                turned_ref[k],
                preferred_element_type=jnp.float32,
            )
            for s in range(sec_dev):
                target = wrapped(s - shift_ref[k], targets)
                scaled = coef_ref[target, k] * product[s * rows : (s + 1) * rows]
                if split:
                    total[target] += scaled[:, :half]
                    mine[target] += scaled[:, half:]
                else:
                    mine[target] += scaled

    if split:
        for g, out in enumerate(theirs):
            out[...] = total[g * sec_dev : (g + 1) * sec_dev].astype(jnp.bfloat16)


def summed(shift, coef, mixed, turned, split):
    k_dev, sec_dev, rows, width = mixed.shape
    targets = coef.shape[0]
    if split:
        out_shape = [pltpu.VMEM((targets, rows, width // 2), jnp.float32)]
        out_shape += [pltpu.VMEM((sec_dev, rows, width // 2), jnp.bfloat16)] * (targets // sec_dev)
        scratch = [pltpu.VMEM((targets, rows, width // 2), jnp.float32)]
    else:
        out_shape = [pltpu.VMEM((targets, rows, width), jnp.float32)]
        scratch = []
    return pl.pallas_call(
        functools.partial(sum_kernel, split),
        out_shape=out_shape,
        in_specs=[pl.BlockSpec(memory_space=pltpu.SMEM)] * 2
        + [pl.BlockSpec(memory_space=pltpu.VMEM)] * 2,
        out_specs=[pl.BlockSpec(memory_space=pltpu.VMEM)] * len(out_shape),
        scratch_shapes=scratch,
        compiler_params=pltpu.CompilerParams(vmem_limit_bytes=24 * MIB),
        cost_estimate=pl.CostEstimate(
            flops=2 * k_dev * sec_dev * rows * width * width,
            bytes_accessed=2 * (mixed.size + turned.size),
            transcendentals=0,
        ),
    )(
        pltpu.with_memory_space_constraint(shift, pltpu.HBM),
        coef,
        pltpu.with_memory_space_constraint(mixed, pltpu.VMEM),
        pltpu.with_memory_space_constraint(turned, pltpu.VMEM),
    )


def shift_by(value, axis, distance):
    size = lax.axis_size(axis)
    return lax.ppermute(value, axis, [(i, (i + distance) % size) for i in range(size)])


def after(value, other):
    return lax.optimization_barrier((value, other))[0]


def per_device(wavefunction, left_ops, right_ops, site_coef, coupled, sector_shift):
    sec_dev = wavefunction.shape[0]
    devices = lax.axis_size("sector")
    live = jnp.where(coupled.T > 0, site_coef.T, 0.0)
    side = jnp.reshape(lax.axis_index("op"), (1,)).astype(jnp.int32)
    split = lax.axis_size("op") == 2 and devices <= 4

    if split:
        coefs = [live] + [shift_by(live, "sector", -g) for g in range(1, devices)]
        coef = jnp.concatenate(coefs, axis=0)
        mixed, turned = mix(side, wavefunction, left_ops, right_ops, True)
        mine, *theirs = summed(sector_shift, coef, mixed, turned, True)
        mine = [mine[g * sec_dev : (g + 1) * sec_dev] for g in range(devices)]
        order = sorted(range(1, devices), key=lambda g: abs(2 * g - devices))
        crossed = {g: shift_by(theirs[g], "op", 1) for g in order}
        arrived, both = [], None
        for g in order:
            other = crossed[g] if both is None else after(crossed[g], both)
            both = (mine[g] + other.astype(jnp.float32)).astype(jnp.bfloat16)
            if not arrived:
                theirs[0] = after(theirs[0], both)
            arrived.append(shift_by(both, "sector", g))
        sigma = mine[0] + after(shift_by(theirs[0], "op", 1), both).astype(jnp.float32)
        for other in arrived:
            sigma = lax.optimization_barrier(sigma) + other.astype(jnp.float32)
        return sigma

    first = lax.axis_index("sector") * sec_dev
    coef = jnp.roll(lax.all_gather(live, "sector", axis=0, tiled=True), -first, axis=0)
    mixed, turned = mix(side, wavefunction, left_ops, right_ops, False)
    (total,) = summed(sector_shift, coef, mixed, turned, False)
    total = jnp.roll(total, first, axis=0)
    total = lax.psum_scatter(total, "op", scatter_dimension=2, tiled=True)
    return lax.psum_scatter(total, "sector", scatter_dimension=0, tiled=True)


def solution(mesh):
    placed = (
        P(("groups", "sector"), None, None),
        P(("groups", "op"), "rep", None),
        P(("groups", "op"), None, None),
        P(("groups", "op"), "sector"),
        P(("groups", "op"), "sector"),
        P(("groups", "op")),
    )
    return jax.shard_map(
        per_device,
        mesh=mesh,
        in_specs=placed,
        out_specs=P(("groups", "sector"), "rep", "op"),
        check_vma=False,
    )
```

```python
import functools

import jax
import jax.numpy as jnp
from jax import lax
from jax.experimental import pallas as pl
from jax.experimental.pallas import tpu as pltpu
from jax.sharding import PartitionSpec as P

MIX_TERMS = 8
SUM_TERMS = 4
MIB = 1024 * 1024


def wrapped(value, size):
    if size & (size - 1) == 0:
        return value & (size - 1)
    return lax.rem(value + size, size)


def mix_kernel(split, side_ref, wave_ref, left_ref, right_ref, mixed_ref, held_ref, wave, left, sems):
    sec_dev = wave.shape[0]
    terms, rows, width = left.shape
    chunks = terms // MIX_TERMS

    def left_copy(c):
        part = pl.ds(c * MIX_TERMS, MIX_TERMS)
        return pltpu.make_async_copy(left_ref.at[part], left.at[part], sems.at[3 + c])

    wave_copy = pltpu.make_async_copy(wave_ref, wave, sems.at[0])
    wave_copy.start()
    for c in range(chunks):
        left_copy(c).start()
    if split:
        half = width // 2
        mine = pl.multiple_of(side_ref[0] * half, half)
        theirs = pl.multiple_of((1 - side_ref[0]) * half, half)
        right_copies = [
            pltpu.make_async_copy(
                right_ref.at[:, pl.ds(theirs, half)], held_ref.at[:, pl.ds(0, half)], sems.at[1]
            ),
            pltpu.make_async_copy(
                right_ref.at[:, pl.ds(mine, half)], held_ref.at[:, pl.ds(half, half)], sems.at[2]
            ),
        ]
    else:
        right_copies = [pltpu.make_async_copy(right_ref, held_ref, sems.at[1])]
    wave_copy.wait()

    @pl.loop(0, chunks)
    def _(c):
        left_copy(c).wait()

        @pl.when(c == 0)
        def _():
            for copy in right_copies:
                copy.start()

        part = pl.ds(c * MIX_TERMS, MIX_TERMS)
        rows_in = left[part].reshape(MIX_TERMS * rows, width)
        for s in range(sec_dev):
            product = jnp.dot(rows_in, wave[s], preferred_element_type=jnp.float32)
            mixed_ref[part, s] = product.astype(jnp.bfloat16).reshape(MIX_TERMS, rows, width)

    for copy in right_copies:
        copy.wait()


def mix(side, wavefunction, left_ops, right_ops, split):
    k_dev, rows, width = left_ops.shape
    sec_dev = wavefunction.shape[0]
    return pl.pallas_call(
        functools.partial(mix_kernel, split),
        out_shape=[
            pltpu.VMEM((k_dev, sec_dev, rows, width), jnp.bfloat16),
            pltpu.VMEM(right_ops.shape, jnp.bfloat16),
        ],
        in_specs=[pl.BlockSpec(memory_space=pltpu.SMEM)] + [pl.BlockSpec(memory_space=pltpu.HBM)] * 3,
        out_specs=[pl.BlockSpec(memory_space=pltpu.VMEM)] * 2,
        scratch_shapes=[
            pltpu.VMEM(wavefunction.shape, jnp.bfloat16),
            pltpu.VMEM(left_ops.shape, jnp.bfloat16),
            pltpu.SemaphoreType.DMA((3 + k_dev // MIX_TERMS,)),
        ],
        compiler_params=pltpu.CompilerParams(vmem_limit_bytes=24 * MIB),
        cost_estimate=pl.CostEstimate(
            flops=2 * k_dev * sec_dev * rows * width * width,
            bytes_accessed=2 * (left_ops.size + right_ops.size),
            transcendentals=0,
        ),
    )(
        side,
        *(pltpu.with_memory_space_constraint(x, pltpu.HBM) for x in (wavefunction, left_ops, right_ops)),
    )


def sum_kernel(split, shift_ref, coef_ref, mixed_ref, held_ref, *refs):
    terms, sec_dev, rows, width = mixed_ref.shape
    targets = coef_ref.shape[0]
    half = width // 2
    spill = sec_dev - 1
    sums = refs[-2:] if split else refs[-1:]
    outs = refs[: len(refs) - len(sums)]
    for total in sums:
        total[...] = jnp.zeros_like(total)

    @pl.loop(0, terms // SUM_TERMS)
    def _(step):
        for t in range(SUM_TERMS):
            k = step * SUM_TERMS + t
            product = lax.dot_general(
                mixed_ref[k].reshape(sec_dev * rows, width),
                held_ref[k],
                (((1,), (1,)), ((), ())),
                preferred_element_type=jnp.float32,
            ).reshape(sec_dev, rows, width)
            first = wrapped(-shift_ref[k], targets)
            scaled = jnp.stack(
                [coef_ref[wrapped(first + s, targets), k] * product[s] for s in range(sec_dev)]
            )
            place = pl.ds(first, sec_dev)
            if split:
                sums[0][place] += scaled[:, :, :half]
                sums[1][place] += scaled[:, :, half:]
            else:
                sums[0][place] += scaled

    for total in sums:
        total[:spill] += total[targets:]
    if split:
        outs[0][...] = sums[1][:targets]
        for g, out in enumerate(outs[1:]):
            out[...] = sums[0][g * sec_dev : (g + 1) * sec_dev].astype(jnp.bfloat16)
    else:
        outs[0][...] = sums[0][:targets]


def summed(shift, coef, mixed, held, split):
    k_dev, sec_dev, rows, width = mixed.shape
    targets = coef.shape[0]
    columns = width // 2 if split else width
    out_shape = [pltpu.VMEM((targets, rows, columns), jnp.float32)]
    scratch = [pltpu.VMEM((targets + sec_dev - 1, rows, columns), jnp.float32)]
    if split:
        out_shape += [pltpu.VMEM((sec_dev, rows, columns), jnp.bfloat16)] * (targets // sec_dev)
        scratch = scratch * 2
    return pl.pallas_call(
        functools.partial(sum_kernel, split),
        out_shape=out_shape,
        in_specs=[pl.BlockSpec(memory_space=pltpu.SMEM)] * 2
        + [pl.BlockSpec(memory_space=pltpu.VMEM)] * 2,
        out_specs=[pl.BlockSpec(memory_space=pltpu.VMEM)] * len(out_shape),
        scratch_shapes=scratch,
        compiler_params=pltpu.CompilerParams(vmem_limit_bytes=24 * MIB),
        cost_estimate=pl.CostEstimate(
            flops=2 * k_dev * sec_dev * rows * width * width,
            bytes_accessed=2 * (mixed.size + held.size),
            transcendentals=0,
        ),
    )(
        pltpu.with_memory_space_constraint(shift, pltpu.HBM),
        coef,
        pltpu.with_memory_space_constraint(mixed, pltpu.VMEM),
        pltpu.with_memory_space_constraint(held, pltpu.VMEM),
    )


def shift_by(value, axis, distance):
    size = lax.axis_size(axis)
    return lax.ppermute(value, axis, [(i, (i + distance) % size) for i in range(size)])


def after(value, other):
    return lax.optimization_barrier((value, other))[0]


def per_device(wavefunction, left_ops, right_ops, site_coef, coupled, sector_shift):
    sec_dev = wavefunction.shape[0]
    devices = lax.axis_size("sector")
    live = jnp.where(coupled.T > 0, site_coef.T, 0.0)
    side = jnp.reshape(lax.axis_index("op"), (1,)).astype(jnp.int32)
    split = lax.axis_size("op") == 2 and devices <= 4

    if split:
        coefs = [live] + [shift_by(live, "sector", -g) for g in range(1, devices)]
        coef = jnp.concatenate(coefs, axis=0)
        mixed, held = mix(side, wavefunction, left_ops, right_ops, True)
        mine, *theirs = summed(sector_shift, coef, mixed, held, True)
        mine = [mine[g * sec_dev : (g + 1) * sec_dev] for g in range(devices)]
        order = sorted(range(1, devices), key=lambda g: abs(2 * g - devices))
        crossed = {g: shift_by(theirs[g], "op", 1) for g in order}
        arrived, both = [], None
        for g in order:
            other = crossed[g] if both is None else after(crossed[g], both)
            both = (mine[g] + other.astype(jnp.float32)).astype(jnp.bfloat16)
            if not arrived:
                theirs[0] = after(theirs[0], both)
            arrived.append(shift_by(both, "sector", g))
        sigma = mine[0] + after(shift_by(theirs[0], "op", 1), both).astype(jnp.float32)
        for other in arrived:
            sigma = lax.optimization_barrier(sigma) + other.astype(jnp.float32)
        return sigma

    first = lax.axis_index("sector") * sec_dev
    coef = jnp.roll(lax.all_gather(live, "sector", axis=0, tiled=True), -first, axis=0)
    mixed, held = mix(side, wavefunction, left_ops, right_ops, False)
    (total,) = summed(sector_shift, coef, mixed, held, False)
    total = jnp.roll(total, first, axis=0)
    total = lax.psum_scatter(total, "op", scatter_dimension=2, tiled=True)
    return lax.psum_scatter(total, "sector", scatter_dimension=0, tiled=True)


def solution(mesh):
    placed = (
        P(("groups", "sector"), None, None),
        P(("groups", "op"), "rep", None),
        P(("groups", "op"), None, None),
        P(("groups", "op"), "sector"),
        P(("groups", "op"), "sector"),
        P(("groups", "op")),
    )
    return jax.shard_map(
        per_device,
        mesh=mesh,
        in_specs=placed,
        out_specs=P(("groups", "sector"), "rep", "op"),
        check_vma=False,
    )
```

```python
import functools

import jax
import jax.numpy as jnp
from jax import lax
from jax.experimental import pallas as pl
from jax.experimental.pallas import tpu as pltpu
from jax.sharding import PartitionSpec as P

MIX_TERMS = 8
SUM_TERMS = 8
MIB = 1024 * 1024


def wrapped(value, size):
    if size & (size - 1) == 0:
        return value & (size - 1)
    return lax.rem(value + size, size)


def mix_kernel(split, side_ref, wave_ref, left_ref, right_ref, mixed_ref, held_ref, wave, left, sems):
    sec_dev = wave.shape[0]
    terms, rows, width = left.shape
    chunks = terms // MIX_TERMS

    def left_copy(c):
        part = pl.ds(c * MIX_TERMS, MIX_TERMS)
        return pltpu.make_async_copy(left_ref.at[part], left.at[part], sems.at[3 + c])

    wave_copy = pltpu.make_async_copy(wave_ref, wave, sems.at[0])
    wave_copy.start()
    for c in range(chunks):
        left_copy(c).start()
    if split:
        half = width // 2
        mine = pl.multiple_of(side_ref[0] * half, half)
        theirs = pl.multiple_of((1 - side_ref[0]) * half, half)
        right_copies = [
            pltpu.make_async_copy(
                right_ref.at[:, pl.ds(theirs, half)], held_ref.at[:, pl.ds(0, half)], sems.at[1]
            ),
            pltpu.make_async_copy(
                right_ref.at[:, pl.ds(mine, half)], held_ref.at[:, pl.ds(half, half)], sems.at[2]
            ),
        ]
    else:
        right_copies = [pltpu.make_async_copy(right_ref, held_ref, sems.at[1])]
    wave_copy.wait()

    @pl.loop(0, chunks)
    def _(c):
        left_copy(c).wait()

        @pl.when(c == 0)
        def _():
            for copy in right_copies:
                copy.start()

        part = pl.ds(c * MIX_TERMS, MIX_TERMS)
        rows_in = left[part].reshape(MIX_TERMS * rows, width)
        for s in range(sec_dev):
            product = jnp.dot(rows_in, wave[s], preferred_element_type=jnp.float32)
            mixed_ref[part, s] = product.astype(jnp.bfloat16).reshape(MIX_TERMS, rows, width)

    for copy in right_copies:
        copy.wait()


def mix(side, wavefunction, left_ops, right_ops, split):
    k_dev, rows, width = left_ops.shape
    sec_dev = wavefunction.shape[0]
    return pl.pallas_call(
        functools.partial(mix_kernel, split),
        out_shape=[
            pltpu.VMEM((k_dev, sec_dev, rows, width), jnp.bfloat16),
            pltpu.VMEM(right_ops.shape, jnp.bfloat16),
        ],
        in_specs=[pl.BlockSpec(memory_space=pltpu.SMEM)] + [pl.BlockSpec(memory_space=pltpu.HBM)] * 3,
        out_specs=[pl.BlockSpec(memory_space=pltpu.VMEM)] * 2,
        scratch_shapes=[
            pltpu.VMEM(wavefunction.shape, jnp.bfloat16),
            pltpu.VMEM(left_ops.shape, jnp.bfloat16),
            pltpu.SemaphoreType.DMA((3 + k_dev // MIX_TERMS,)),
        ],
        compiler_params=pltpu.CompilerParams(vmem_limit_bytes=24 * MIB),
        cost_estimate=pl.CostEstimate(
            flops=2 * k_dev * sec_dev * rows * width * width,
            bytes_accessed=2 * (left_ops.size + right_ops.size),
            transcendentals=0,
        ),
    )(
        side,
        *(pltpu.with_memory_space_constraint(x, pltpu.HBM) for x in (wavefunction, left_ops, right_ops)),
    )


def sum_kernel(theirs, at, shift_ref, coef_ref, mixed_ref, held_ref, *refs):
    terms, sec_dev, rows, width = mixed_ref.shape
    targets = coef_ref.shape[0]
    total = refs[-1]
    columns = total.shape[2]
    total[...] = jnp.zeros_like(total)

    @pl.loop(0, terms // SUM_TERMS)
    def _(step):
        for t in range(SUM_TERMS):
            k = step * SUM_TERMS + t
            product = lax.dot_general(
                mixed_ref[k].reshape(sec_dev * rows, width),
                held_ref[k, at * columns : (at + 1) * columns],
                (((1,), (1,)), ((), ())),
                preferred_element_type=jnp.float32,
            )
            for s in range(sec_dev):
                target = wrapped(s - shift_ref[k], targets)
                total[target] += coef_ref[target, k] * product[s * rows : (s + 1) * rows]

    if theirs:
        for g, out in enumerate(refs[:-1]):
            out[...] = total[g * sec_dev : (g + 1) * sec_dev].astype(jnp.bfloat16)


def summed(shift, coef, mixed, held, parts, at, theirs):
    k_dev, sec_dev, rows, width = mixed.shape
    targets = coef.shape[0]
    shape = (targets, rows, width // parts)
    if theirs:
        group = (sec_dev, rows, width // parts)
        out_shape = [pltpu.VMEM(group, jnp.bfloat16)] * (targets // sec_dev)
        scratch = [pltpu.VMEM(shape, jnp.float32)]
    else:
        out_shape = [pltpu.VMEM(shape, jnp.float32)]
        scratch = []
    return pl.pallas_call(
        functools.partial(sum_kernel, theirs, at),
        out_shape=out_shape,
        in_specs=[pl.BlockSpec(memory_space=pltpu.SMEM)] * 2
        + [pl.BlockSpec(memory_space=pltpu.VMEM)] * 2,
        out_specs=[pl.BlockSpec(memory_space=pltpu.VMEM)] * len(out_shape),
        scratch_shapes=scratch,
        compiler_params=pltpu.CompilerParams(vmem_limit_bytes=24 * MIB),
        cost_estimate=pl.CostEstimate(
            flops=2 * k_dev * sec_dev * rows * width * width // parts,
            bytes_accessed=2 * (mixed.size + held.size),
            transcendentals=0,
        ),
    )(
        pltpu.with_memory_space_constraint(shift, pltpu.HBM),
        coef,
        pltpu.with_memory_space_constraint(mixed, pltpu.VMEM),
        pltpu.with_memory_space_constraint(held, pltpu.VMEM),
    )


def shift_by(value, axis, distance):
    size = lax.axis_size(axis)
    return lax.ppermute(value, axis, [(i, (i + distance) % size) for i in range(size)])


def after(value, other):
    return lax.optimization_barrier((value, other))[0]


def per_device(wavefunction, left_ops, right_ops, site_coef, coupled, sector_shift):
    sec_dev = wavefunction.shape[0]
    devices = lax.axis_size("sector")
    live = jnp.where(coupled.T > 0, site_coef.T, 0.0)
    side = jnp.reshape(lax.axis_index("op"), (1,)).astype(jnp.int32)
    split = lax.axis_size("op") == 2 and devices <= 4

    if split:
        coefs = [live] + [shift_by(live, "sector", -g) for g in range(1, devices)]
        coef = jnp.concatenate(coefs, axis=0)
        mixed, held = mix(side, wavefunction, left_ops, right_ops, True)
        theirs = summed(sector_shift, coef, mixed, held, 2, 0, True)
        far, *near = sorted(range(1, devices), key=lambda g: abs(2 * g - devices))
        crossed = shift_by(theirs[far], "op", 1)
        (mine,) = summed(sector_shift, after(coef, theirs[far]), mixed, held, 2, 1, False)
        mine = [mine[g * sec_dev : (g + 1) * sec_dev] for g in range(devices)]
        both = (mine[far] + crossed.astype(jnp.float32)).astype(jnp.bfloat16)
        arrived = [shift_by(both, "sector", far)]
        crossed = {g: shift_by(after(theirs[g], both), "op", 1) for g in near + [0]}
        for g in near:
            both = (mine[g] + after(crossed[g], both).astype(jnp.float32)).astype(jnp.bfloat16)
            arrived.append(shift_by(both, "sector", g))
        sigma = mine[0] + after(crossed[0], both).astype(jnp.float32)
        for other in arrived:
            sigma = lax.optimization_barrier(sigma) + other.astype(jnp.float32)
        return sigma

    first = lax.axis_index("sector") * sec_dev
    coef = jnp.roll(lax.all_gather(live, "sector", axis=0, tiled=True), -first, axis=0)
    mixed, held = mix(side, wavefunction, left_ops, right_ops, False)
    (total,) = summed(sector_shift, coef, mixed, held, 1, 0, False)
    total = jnp.roll(total, first, axis=0)
    total = lax.psum_scatter(total, "op", scatter_dimension=2, tiled=True)
    return lax.psum_scatter(total, "sector", scatter_dimension=0, tiled=True)


def solution(mesh):
    placed = (
        P(("groups", "sector"), None, None),
        P(("groups", "op"), "rep", None),
        P(("groups", "op"), None, None),
        P(("groups", "op"), "sector"),
        P(("groups", "op"), "sector"),
        P(("groups", "op")),
    )
    return jax.shard_map(
        per_device,
        mesh=mesh,
        in_specs=placed,
        out_specs=P(("groups", "sector"), "rep", "op"),
        check_vma=False,
    )
```

```python
import functools

import jax
import jax.numpy as jnp
from jax import lax
from jax.experimental import pallas as pl
from jax.experimental.pallas import tpu as pltpu
from jax.sharding import PartitionSpec as P

MIX_TERMS = 8
SUM_TERMS = 8
MIB = 1024 * 1024


def wrapped(value, size):
    if size & (size - 1) == 0:
        return value & (size - 1)
    return lax.rem(value + size, size)


def mix_kernel(split, side_ref, wave_ref, left_ref, right_ref, mixed_ref, held_ref, wave, left, sems):
    sec_dev = wave.shape[0]
    terms, rows, width = left.shape
    chunks = terms // MIX_TERMS

    def left_copy(c):
        part = pl.ds(c * MIX_TERMS, MIX_TERMS)
        return pltpu.make_async_copy(left_ref.at[part], left.at[part], sems.at[3 + c])

    wave_copy = pltpu.make_async_copy(wave_ref, wave, sems.at[0])
    wave_copy.start()
    for c in range(chunks):
        left_copy(c).start()
    if split:
        half = width // 2
        mine = pl.multiple_of(side_ref[0] * half, half)
        theirs = pl.multiple_of((1 - side_ref[0]) * half, half)
        right_copies = [
            pltpu.make_async_copy(
                right_ref.at[:, pl.ds(theirs, half)], held_ref.at[:, pl.ds(0, half)], sems.at[1]
            ),
            pltpu.make_async_copy(
                right_ref.at[:, pl.ds(mine, half)], held_ref.at[:, pl.ds(half, half)], sems.at[2]
            ),
        ]
    else:
        right_copies = [pltpu.make_async_copy(right_ref, held_ref, sems.at[1])]
    wave_copy.wait()

    @pl.loop(0, chunks)
    def _(c):
        left_copy(c).wait()

        @pl.when(c == 0)
        def _():
            for copy in right_copies:
                copy.start()

        part = pl.ds(c * MIX_TERMS, MIX_TERMS)
        rows_in = left[part].reshape(MIX_TERMS * rows, width)
        for s in range(sec_dev):
            product = jnp.dot(rows_in, wave[s], preferred_element_type=jnp.float32)
            mixed_ref[part, s] = product.astype(jnp.bfloat16).reshape(MIX_TERMS, rows, width)

    for copy in right_copies:
        copy.wait()


def mix(side, wavefunction, left_ops, right_ops, split):
    k_dev, rows, width = left_ops.shape
    sec_dev = wavefunction.shape[0]
    return pl.pallas_call(
        functools.partial(mix_kernel, split),
        out_shape=[
            pltpu.VMEM((k_dev, sec_dev, rows, width), jnp.bfloat16),
            pltpu.VMEM(right_ops.shape, jnp.bfloat16),
        ],
        in_specs=[pl.BlockSpec(memory_space=pltpu.SMEM)] + [pl.BlockSpec(memory_space=pltpu.HBM)] * 3,
        out_specs=[pl.BlockSpec(memory_space=pltpu.VMEM)] * 2,
        scratch_shapes=[
            pltpu.VMEM(wavefunction.shape, jnp.bfloat16),
            pltpu.VMEM(left_ops.shape, jnp.bfloat16),
            pltpu.SemaphoreType.DMA((3 + k_dev // MIX_TERMS,)),
        ],
        compiler_params=pltpu.CompilerParams(vmem_limit_bytes=24 * MIB),
        cost_estimate=pl.CostEstimate(
            flops=2 * k_dev * sec_dev * rows * width * width,
            bytes_accessed=2 * (left_ops.size + right_ops.size),
            transcendentals=0,
        ),
    )(
        side,
        *(pltpu.with_memory_space_constraint(x, pltpu.HBM) for x in (wavefunction, left_ops, right_ops)),
    )


def sum_kernel(split, shift_ref, coef_ref, mixed_ref, held_ref, *refs):
    terms, sec_dev, rows, width = mixed_ref.shape
    targets = coef_ref.shape[0]
    half = width // 2
    mine = refs[0]
    mine[...] = jnp.zeros_like(mine)
    if split:
        theirs, total = refs[1:-1], refs[-1]
        total[...] = jnp.zeros_like(total)

    def add(k, s, product):
        target = wrapped(s - shift_ref[k], targets)
        scaled = coef_ref[target, k] * product
        if split:
            total[target] += scaled[:, :half]
            mine[target] += scaled[:, half:]
        else:
            mine[target] += scaled

    @pl.loop(0, terms // SUM_TERMS)
    def _(step):
        waiting = None
        for t in range(SUM_TERMS):
            k = step * SUM_TERMS + t
            for s in range(sec_dev):
                product = lax.dot_general(
                    mixed_ref[k, s],
                    held_ref[k],
                    (((1,), (1,)), ((), ())),
                    preferred_element_type=jnp.float32,
                )
                if waiting is not None:
                    add(*waiting)
                waiting = (k, s, product)
        add(*waiting)

    if split:
        for g, out in enumerate(theirs):
            out[...] = total[g * sec_dev : (g + 1) * sec_dev].astype(jnp.bfloat16)


def summed(shift, coef, mixed, held, split):
    k_dev, sec_dev, rows, width = mixed.shape
    targets = coef.shape[0]
    columns = width // 2 if split else width
    out_shape = [pltpu.VMEM((targets, rows, columns), jnp.float32)]
    scratch = []
    if split:
        out_shape += [pltpu.VMEM((sec_dev, rows, columns), jnp.bfloat16)] * (targets // sec_dev)
        scratch = [pltpu.VMEM((targets, rows, columns), jnp.float32)]
    return pl.pallas_call(
        functools.partial(sum_kernel, split),
        out_shape=out_shape,
        in_specs=[pl.BlockSpec(memory_space=pltpu.SMEM)] * 2
        + [pl.BlockSpec(memory_space=pltpu.VMEM)] * 2,
        out_specs=[pl.BlockSpec(memory_space=pltpu.VMEM)] * len(out_shape),
        scratch_shapes=scratch,
        compiler_params=pltpu.CompilerParams(vmem_limit_bytes=24 * MIB),
        cost_estimate=pl.CostEstimate(
            flops=2 * k_dev * sec_dev * rows * width * width,
            bytes_accessed=2 * (mixed.size + held.size),
            transcendentals=0,
        ),
    )(
        pltpu.with_memory_space_constraint(shift, pltpu.HBM),
        coef,
        pltpu.with_memory_space_constraint(mixed, pltpu.VMEM),
        pltpu.with_memory_space_constraint(held, pltpu.VMEM),
    )


def shift_by(value, axis, distance):
    size = lax.axis_size(axis)
    return lax.ppermute(value, axis, [(i, (i + distance) % size) for i in range(size)])


def after(value, other):
    return lax.optimization_barrier((value, other))[0]


def per_device(wavefunction, left_ops, right_ops, site_coef, coupled, sector_shift):
    sec_dev = wavefunction.shape[0]
    devices = lax.axis_size("sector")
    live = jnp.where(coupled.T > 0, site_coef.T, 0.0)
    side = jnp.reshape(lax.axis_index("op"), (1,)).astype(jnp.int32)
    split = lax.axis_size("op") == 2 and devices <= 4

    if split:
        coefs = [live] + [shift_by(live, "sector", -g) for g in range(1, devices)]
        coef = jnp.concatenate(coefs, axis=0)
        mixed, held = mix(side, wavefunction, left_ops, right_ops, True)
        mine, *theirs = summed(sector_shift, coef, mixed, held, True)
        mine = [mine[g * sec_dev : (g + 1) * sec_dev] for g in range(devices)]
        order = sorted(range(1, devices), key=lambda g: abs(2 * g - devices))
        crossed = {g: shift_by(theirs[g], "op", 1) for g in order}
        arrived, both = [], None
        for g in order:
            other = crossed[g] if both is None else after(crossed[g], both)
            both = (mine[g] + other.astype(jnp.float32)).astype(jnp.bfloat16)
            if not arrived:
                theirs[0] = after(theirs[0], both)
            arrived.append(shift_by(both, "sector", g))
        sigma = mine[0] + after(shift_by(theirs[0], "op", 1), both).astype(jnp.float32)
        for other in arrived:
            sigma = lax.optimization_barrier(sigma) + other.astype(jnp.float32)
        return sigma

    first = lax.axis_index("sector") * sec_dev
    coef = jnp.roll(lax.all_gather(live, "sector", axis=0, tiled=True), -first, axis=0)
    mixed, held = mix(side, wavefunction, left_ops, right_ops, False)
    (total,) = summed(sector_shift, coef, mixed, held, False)
    total = jnp.roll(total, first, axis=0)
    total = lax.psum_scatter(total, "op", scatter_dimension=2, tiled=True)
    return lax.psum_scatter(total, "sector", scatter_dimension=0, tiled=True)


def solution(mesh):
    placed = (
        P(("groups", "sector"), None, None),
        P(("groups", "op"), "rep", None),
        P(("groups", "op"), None, None),
        P(("groups", "op"), "sector"),
        P(("groups", "op"), "sector"),
        P(("groups", "op")),
    )
    return jax.shard_map(
        per_device,
        mesh=mesh,
        in_specs=placed,
        out_specs=P(("groups", "sector"), "rep", "op"),
        check_vma=False,
    )
```

```python
import functools

import jax
import jax.numpy as jnp
from jax import lax
from jax.experimental import pallas as pl
from jax.experimental.pallas import tpu as pltpu
from jax.sharding import PartitionSpec as P

MIX_TERMS = 8
SUM_TERMS = 4
MIB = 1024 * 1024


def wrapped(value, size):
    if size & (size - 1) == 0:
        return value & (size - 1)
    return lax.rem(value + size, size)


def mix_kernel(split, side_ref, wave_ref, left_ref, right_ref, mixed_ref, held_ref, wave, left, sems):
    sec_dev = wave.shape[0]
    terms, rows, width = left.shape
    chunks = terms // MIX_TERMS

    def left_copy(c):
        part = pl.ds(c * MIX_TERMS, MIX_TERMS)
        return pltpu.make_async_copy(left_ref.at[part], left.at[part], sems.at[3 + c])

    wave_copy = pltpu.make_async_copy(wave_ref, wave, sems.at[0])
    wave_copy.start()
    for c in range(chunks):
        left_copy(c).start()
    if split:
        half = width // 2
        mine = pl.multiple_of(side_ref[0] * half, half)
        theirs = pl.multiple_of((1 - side_ref[0]) * half, half)
        right_copies = [
            pltpu.make_async_copy(
                right_ref.at[:, pl.ds(theirs, half)], held_ref.at[:, pl.ds(0, half)], sems.at[1]
            ),
            pltpu.make_async_copy(
                right_ref.at[:, pl.ds(mine, half)], held_ref.at[:, pl.ds(half, half)], sems.at[2]
            ),
        ]
    else:
        right_copies = [pltpu.make_async_copy(right_ref, held_ref, sems.at[1])]
    wave_copy.wait()

    @pl.loop(0, chunks)
    def _(c):
        left_copy(c).wait()

        @pl.when(c == 0)
        def _():
            for copy in right_copies:
                copy.start()

        part = pl.ds(c * MIX_TERMS, MIX_TERMS)
        rows_in = left[part].reshape(MIX_TERMS * rows, width)
        for s in range(sec_dev):
            product = jnp.dot(rows_in, wave[s], preferred_element_type=jnp.float32)
            mixed_ref[part, s] = product.astype(jnp.bfloat16).reshape(MIX_TERMS, rows, width)

    for copy in right_copies:
        copy.wait()


def mix(side, wavefunction, left_ops, right_ops, split):
    k_dev, rows, width = left_ops.shape
    sec_dev = wavefunction.shape[0]
    return pl.pallas_call(
        functools.partial(mix_kernel, split),
        out_shape=[
            pltpu.VMEM((k_dev, sec_dev, rows, width), jnp.bfloat16),
            pltpu.VMEM(right_ops.shape, jnp.bfloat16),
        ],
        in_specs=[pl.BlockSpec(memory_space=pltpu.SMEM)] + [pl.BlockSpec(memory_space=pltpu.HBM)] * 3,
        out_specs=[pl.BlockSpec(memory_space=pltpu.VMEM)] * 2,
        scratch_shapes=[
            pltpu.VMEM(wavefunction.shape, jnp.bfloat16),
            pltpu.VMEM(left_ops.shape, jnp.bfloat16),
            pltpu.SemaphoreType.DMA((3 + k_dev // MIX_TERMS,)),
        ],
        compiler_params=pltpu.CompilerParams(vmem_limit_bytes=24 * MIB),
        cost_estimate=pl.CostEstimate(
            flops=2 * k_dev * sec_dev * rows * width * width,
            bytes_accessed=2 * (left_ops.size + right_ops.size),
            transcendentals=0,
        ),
    )(
        side,
        *(pltpu.with_memory_space_constraint(x, pltpu.HBM) for x in (wavefunction, left_ops, right_ops)),
    )


def sum_kernel(split, me_ref, shift_ref, coef_ref, mixed_ref, held_ref, *refs):
    terms, sec_dev, rows, width = mixed_ref.shape
    targets = coef_ref.shape[0]
    half = width // 2
    first = me_ref[0] * sec_dev
    mine = refs[0]
    mine[...] = jnp.zeros_like(mine)
    if split:
        theirs, total = refs[1:-1], refs[-1]
        total[...] = jnp.zeros_like(total)

    @pl.loop(0, terms // SUM_TERMS)
    def _(step):
        for t in range(SUM_TERMS):
            k = step * SUM_TERMS + t
            product = lax.dot_general(
                mixed_ref[k].reshape(sec_dev * rows, width),
                held_ref[k],
                (((1,), (1,)), ((), ())),
                preferred_element_type=jnp.float32,
            )
            for s in range(sec_dev):
                target = wrapped(first + s - shift_ref[k], targets)
                if split:
                    slot = target ^ first
                    scaled = coef_ref[slot, k] * product[s * rows : (s + 1) * rows]
                    total[slot] += scaled[:, :half]
                    mine[slot] += scaled[:, half:]
                else:
                    mine[target] += coef_ref[target, k] * product[s * rows : (s + 1) * rows]

    if split:
        for g, out in enumerate(theirs):
            out[...] = total[g * sec_dev : (g + 1) * sec_dev].astype(jnp.bfloat16)


def summed(me, shift, coef, mixed, held, split):
    k_dev, sec_dev, rows, width = mixed.shape
    targets = coef.shape[0]
    columns = width // 2 if split else width
    out_shape = [pltpu.VMEM((targets, rows, columns), jnp.float32)]
    scratch = []
    if split:
        out_shape += [pltpu.VMEM((sec_dev, rows, columns), jnp.bfloat16)] * (targets // sec_dev)
        scratch = [pltpu.VMEM((targets, rows, columns), jnp.float32)]
    return pl.pallas_call(
        functools.partial(sum_kernel, split),
        out_shape=out_shape,
        in_specs=[pl.BlockSpec(memory_space=pltpu.SMEM)] * 3
        + [pl.BlockSpec(memory_space=pltpu.VMEM)] * 2,
        out_specs=[pl.BlockSpec(memory_space=pltpu.VMEM)] * len(out_shape),
        scratch_shapes=scratch,
        compiler_params=pltpu.CompilerParams(vmem_limit_bytes=24 * MIB),
        cost_estimate=pl.CostEstimate(
            flops=2 * k_dev * sec_dev * rows * width * width,
            bytes_accessed=2 * (mixed.size + held.size),
            transcendentals=0,
        ),
    )(
        me,
        pltpu.with_memory_space_constraint(shift, pltpu.HBM),
        coef,
        pltpu.with_memory_space_constraint(mixed, pltpu.VMEM),
        pltpu.with_memory_space_constraint(held, pltpu.VMEM),
    )


def swap(value, axis, mask):
    return lax.ppermute(value, axis, [(i, i ^ mask) for i in range(lax.axis_size(axis))])


def after(value, other):
    return lax.optimization_barrier((value, other))[0]


def per_device(wavefunction, left_ops, right_ops, site_coef, coupled, sector_shift):
    sec_dev = wavefunction.shape[0]
    devices = lax.axis_size("sector")
    live = jnp.where(coupled.T > 0, site_coef.T, 0.0)
    side = jnp.reshape(lax.axis_index("op"), (1,)).astype(jnp.int32)
    me = jnp.reshape(lax.axis_index("sector"), (1,)).astype(jnp.int32)
    split = lax.axis_size("op") == 2 and devices == 4 and sec_dev & (sec_dev - 1) == 0
    mixed, held = mix(side, wavefunction, left_ops, right_ops, split)

    if split:
        coef = jnp.concatenate([live] + [swap(live, "sector", g) for g in (1, 2, 3)], axis=0)
        mine, *theirs = summed(me, sector_shift, coef, mixed, held, True)
        mine = [mine[g * sec_dev : (g + 1) * sec_dev] for g in range(4)]
        crossed = {g: swap(theirs[g], "op", 1) for g in (3, 2)}
        third = (mine[3] + crossed[3].astype(jnp.float32)).astype(jnp.bfloat16)
        relayed = swap(third, "sector", 1)
        crossed |= {g: swap(after(theirs[g], third), "op", 1) for g in (1, 0)}
        second = mine[2] + after(crossed[2], third).astype(jnp.float32)
        second = lax.optimization_barrier(second) + relayed.astype(jnp.float32)
        second = second.astype(jnp.bfloat16)
        far = swap(second, "sector", 2)
        first = (mine[1] + after(crossed[1], second).astype(jnp.float32)).astype(jnp.bfloat16)
        near = swap(first, "sector", 1)
        sigma = mine[0] + after(crossed[0], first).astype(jnp.float32)
        sigma = lax.optimization_barrier(sigma) + near.astype(jnp.float32)
        return lax.optimization_barrier(sigma) + far.astype(jnp.float32)

    coef = lax.all_gather(live, "sector", axis=0, tiled=True)
    (total,) = summed(me, sector_shift, coef, mixed, held, False)
    total = lax.psum_scatter(total, "op", scatter_dimension=2, tiled=True)
    return lax.psum_scatter(total, "sector", scatter_dimension=0, tiled=True)


def solution(mesh):
    placed = (
        P(("groups", "sector"), None, None),
        P(("groups", "op"), "rep", None),
        P(("groups", "op"), None, None),
        P(("groups", "op"), "sector"),
        P(("groups", "op"), "sector"),
        P(("groups", "op")),
    )
    return jax.shard_map(
        per_device,
        mesh=mesh,
        in_specs=placed,
        out_specs=P(("groups", "sector"), "rep", "op"),
        check_vma=False,
    )
```

```python
import functools

import jax
import jax.numpy as jnp
from jax import lax
from jax.experimental import pallas as pl
from jax.experimental.pallas import tpu as pltpu
from jax.sharding import PartitionSpec as P

MIX_TERMS = 8
SUM_TERMS = 4
MIB = 1024 * 1024


def wrapped(value, size):
    if size & (size - 1) == 0:
        return value & (size - 1)
    return lax.rem(value + size, size)


def mix_kernel(split, side_ref, wave_ref, left_ref, right_ref, mixed_ref, held_ref, wave, left, sems):
    sec_dev = wave.shape[0]
    terms, rows, width = left.shape
    chunks = terms // MIX_TERMS

    def left_copy(c):
        part = pl.ds(c * MIX_TERMS, MIX_TERMS)
        return pltpu.make_async_copy(left_ref.at[part], left.at[part], sems.at[3 + c])

    wave_copy = pltpu.make_async_copy(wave_ref, wave, sems.at[0])
    wave_copy.start()
    for c in range(chunks):
        left_copy(c).start()
    if split:
        half = width // 2
        mine = pl.multiple_of(side_ref[0] * half, half)
        theirs = pl.multiple_of((1 - side_ref[0]) * half, half)
        right_copies = [
            pltpu.make_async_copy(
                right_ref.at[:, pl.ds(theirs, half)], held_ref.at[:, pl.ds(0, half)], sems.at[1]
            ),
            pltpu.make_async_copy(
                right_ref.at[:, pl.ds(mine, half)], held_ref.at[:, pl.ds(half, half)], sems.at[2]
            ),
        ]
    else:
        right_copies = [pltpu.make_async_copy(right_ref, held_ref, sems.at[1])]
    wave_copy.wait()

    @pl.loop(0, chunks)
    def _(c):
        left_copy(c).wait()

        @pl.when(c == 0)
        def _():
            for copy in right_copies:
                copy.start()

        part = pl.ds(c * MIX_TERMS, MIX_TERMS)
        rows_in = left[part].reshape(MIX_TERMS * rows, width)
        for s in range(sec_dev):
            product = jnp.dot(rows_in, wave[s], preferred_element_type=jnp.float32)
            mixed_ref[part, s] = product.astype(jnp.bfloat16).reshape(MIX_TERMS, rows, width)

    for copy in right_copies:
        copy.wait()


def mix(side, wavefunction, left_ops, right_ops, split):
    k_dev, rows, width = left_ops.shape
    sec_dev = wavefunction.shape[0]
    return pl.pallas_call(
        functools.partial(mix_kernel, split),
        out_shape=[
            pltpu.VMEM((k_dev, sec_dev, rows, width), jnp.bfloat16),
            pltpu.VMEM(right_ops.shape, jnp.bfloat16),
        ],
        in_specs=[pl.BlockSpec(memory_space=pltpu.SMEM)] + [pl.BlockSpec(memory_space=pltpu.HBM)] * 3,
        out_specs=[pl.BlockSpec(memory_space=pltpu.VMEM)] * 2,
        scratch_shapes=[
            pltpu.VMEM(wavefunction.shape, jnp.bfloat16),
            pltpu.VMEM(left_ops.shape, jnp.bfloat16),
            pltpu.SemaphoreType.DMA((3 + k_dev // MIX_TERMS,)),
        ],
        compiler_params=pltpu.CompilerParams(vmem_limit_bytes=16 * MIB),
        cost_estimate=pl.CostEstimate(
            flops=2 * k_dev * sec_dev * rows * width * width,
            bytes_accessed=2 * (left_ops.size + right_ops.size),
            transcendentals=0,
        ),
    )(
        side,
        *(pltpu.with_memory_space_constraint(x, pltpu.HBM) for x in (wavefunction, left_ops, right_ops)),
    )


def sum_kernel(low, order, shift_ref, coef_ref, mixed_ref, held_ref, *refs):
    terms, sec_dev, _, width = mixed_ref.shape
    targets = coef_ref.shape[0]
    half = width // 2
    if order:
        *before, mine = refs[: -1 - len(order)]
        theirs, total = refs[-1 - len(order) : -1], refs[-1]
        total[...] = jnp.zeros_like(total)
    else:
        (mine,) = refs
    rows = mine.shape[1]
    mine[...] = jnp.zeros_like(mine)

    @pl.loop(0, terms // SUM_TERMS)
    def _(step):
        for t in range(SUM_TERMS):
            k = step * SUM_TERMS + t
            product = lax.dot_general(
                mixed_ref[k, :, low : low + rows].reshape(sec_dev * rows, width),
                held_ref[k],
                (((1,), (1,)), ((), ())),
                preferred_element_type=jnp.float32,
            )
            for s in range(sec_dev):
                target = wrapped(s - shift_ref[k], targets)
                scaled = coef_ref[target, k] * product[s * rows : (s + 1) * rows]
                if order:
                    total[target] += scaled[:, :half]
                    mine[target] += scaled[:, half:]
                else:
                    mine[target] += scaled

    for out, groups in zip(theirs if order else (), order):
        for at, g in enumerate(groups):
            sums = total[g * sec_dev : (g + 1) * sec_dev].astype(jnp.bfloat16)
            out[at * sec_dev : (at + 1) * sec_dev, out.shape[1] - rows :] = sums
    if order and before:
        theirs[-1][:, :low] = before[0][...]


def summed(shift, coef, mixed, held, low, rows, order, before=()):
    k_dev, sec_dev, _, width = mixed.shape
    targets = coef.shape[0]
    columns = width // 2 if order else width
    shape = (targets, rows, columns)
    out_shape = [pltpu.VMEM(shape, jnp.float32)]
    for number, groups in enumerate(order):
        height = low + rows if before and number == len(order) - 1 else rows
        out_shape.append(pltpu.VMEM((len(groups) * sec_dev, height, columns), jnp.bfloat16))
    held_in_vmem = (mixed, held, *before)
    return pl.pallas_call(
        functools.partial(sum_kernel, low, order),
        out_shape=out_shape,
        in_specs=[pl.BlockSpec(memory_space=pltpu.SMEM)] * 2
        + [pl.BlockSpec(memory_space=pltpu.VMEM)] * len(held_in_vmem),
        out_specs=[pl.BlockSpec(memory_space=pltpu.VMEM)] * len(out_shape),
        scratch_shapes=[pltpu.VMEM(shape, jnp.float32)] if order else [],
        compiler_params=pltpu.CompilerParams(vmem_limit_bytes=16 * MIB),
        cost_estimate=pl.CostEstimate(
            flops=2 * k_dev * sec_dev * rows * width * width,
            bytes_accessed=2 * (mixed.size + held.size),
            transcendentals=0,
        ),
    )(
        pltpu.with_memory_space_constraint(shift, pltpu.HBM),
        coef,
        *(pltpu.with_memory_space_constraint(x, pltpu.VMEM) for x in held_in_vmem),
    )


def shift_by(value, axis, distance):
    size = lax.axis_size(axis)
    return lax.ppermute(value, axis, [(i, (i + distance) % size) for i in range(size)])


def after(value, other):
    return lax.optimization_barrier((value, other))[0]


def per_device(wavefunction, left_ops, right_ops, site_coef, coupled, sector_shift):
    sec_dev = wavefunction.shape[0]
    devices = lax.axis_size("sector")
    live = jnp.where(coupled.T > 0, site_coef.T, 0.0)
    side = jnp.reshape(lax.axis_index("op"), (1,)).astype(jnp.int32)
    split = lax.axis_size("op") == 2 and devices <= 4

    if split:
        coefs = [live] + [shift_by(live, "sector", -g) for g in range(1, devices)]
        coef = jnp.concatenate(coefs, axis=0)
        mixed, held = mix(side, wavefunction, left_ops, right_ops, True)
        far, *near = sorted(range(1, devices), key=lambda g: abs(2 * g - devices))
        order = ((far,), tuple(near), (0,))
        rows = left_ops.shape[1] // 2

        def own(mine, g):
            return mine[g * sec_dev : (g + 1) * sec_dev]

        mine, *theirs = summed(sector_shift, coef, mixed, held, 0, rows, order)
        crossed = [shift_by(x, "op", 1) for x in theirs[:2]]
        lower, *rest = summed(sector_shift, coef, mixed, held, rows, rows, order, theirs[2:])

        def pass_on(mine, crossed, last):
            arrived = []
            for at, g in enumerate([far, *near]):
                other = crossed[0] if at == 0 else own(crossed[1], at - 1)
                other = other if last is None else after(other, last)
                last = (own(mine, g) + other.astype(jnp.float32)).astype(jnp.bfloat16)
                arrived.append(shift_by(last, "sector", g))
                if at == 0:
                    first = last
            return arrived, first, last

        upper_arrived, first, last = pass_on(mine, crossed, None)
        crossed = [shift_by(after(x, first), "op", 1) for x in rest[:2]]
        whole = shift_by(after(rest[2], last), "op", 1)
        lower_arrived, _, last = pass_on(lower, crossed, last)
        whole = after(whole, last).astype(jnp.float32)
        parts = []
        for own_sums, arrived, other in (
            (mine, upper_arrived, whole[:, :rows]),
            (lower, lower_arrived, whole[:, rows:]),
        ):
            sigma = own(own_sums, 0) + other
            for other in arrived:
                sigma = lax.optimization_barrier(sigma) + other.astype(jnp.float32)
            parts.append(sigma)
        return jnp.concatenate(parts, axis=1)

    first = lax.axis_index("sector") * sec_dev
    coef = jnp.roll(lax.all_gather(live, "sector", axis=0, tiled=True), -first, axis=0)
    mixed, held = mix(side, wavefunction, left_ops, right_ops, False)
    (total,) = summed(sector_shift, coef, mixed, held, 0, left_ops.shape[1], ())
    total = jnp.roll(total, first, axis=0)
    total = lax.psum_scatter(total, "op", scatter_dimension=2, tiled=True)
    return lax.psum_scatter(total, "sector", scatter_dimension=0, tiled=True)


def solution(mesh):
    placed = (
        P(("groups", "sector"), None, None),
        P(("groups", "op"), "rep", None),
        P(("groups", "op"), None, None),
        P(("groups", "op"), "sector"),
        P(("groups", "op"), "sector"),
        P(("groups", "op")),
    )
    return jax.shard_map(
        per_device,
        mesh=mesh,
        in_specs=placed,
        out_specs=P(("groups", "sector"), "rep", "op"),
        check_vma=False,
    )
```

```python
import functools

import jax
import jax.numpy as jnp
from jax import lax
from jax.experimental import pallas as pl
from jax.experimental.pallas import tpu as pltpu
from jax.sharding import PartitionSpec as P

MIX_TERMS = 8
SUM_TERMS = 4
MIB = 1024 * 1024


def wrapped(value, size):
    if size & (size - 1) == 0:
        return value & (size - 1)
    return lax.rem(value + size, size)


def mix_kernel(split, wave_ref, left_ref, right_ref, mixed_ref, held_ref, wave, left, sems):
    sec_dev = wave.shape[0]
    terms, rows, width = left.shape
    chunks = terms // MIX_TERMS

    def left_copy(c):
        part = pl.ds(c * MIX_TERMS, MIX_TERMS)
        return pltpu.make_async_copy(left_ref.at[part], left.at[part], sems.at[3 + c])

    wave_copy = pltpu.make_async_copy(wave_ref, wave, sems.at[0])
    wave_copy.start()
    for c in range(chunks):
        left_copy(c).start()
    if split:
        half = width // 2
        side = lax.axis_index("op")
        mine = pl.multiple_of(side * half, half)
        theirs = pl.multiple_of((1 - side) * half, half)
        right_copies = [
            pltpu.make_async_copy(
                right_ref.at[:, pl.ds(theirs, half)], held_ref.at[:, pl.ds(0, half)], sems.at[1]
            ),
            pltpu.make_async_copy(
                right_ref.at[:, pl.ds(mine, half)], held_ref.at[:, pl.ds(half, half)], sems.at[2]
            ),
        ]
    else:
        right_copies = [pltpu.make_async_copy(right_ref, held_ref, sems.at[1])]
    for copy in right_copies:
        copy.start()
    wave_copy.wait()

    @pl.loop(0, chunks)
    def _(c):
        left_copy(c).wait()
        part = pl.ds(c * MIX_TERMS, MIX_TERMS)
        rows_in = left[part].reshape(MIX_TERMS * rows, width)
        for s in range(sec_dev):
            product = jnp.dot(rows_in, wave[s], preferred_element_type=jnp.float32)
            mixed_ref[part, s] = product.astype(jnp.bfloat16).reshape(MIX_TERMS, rows, width)

    for copy in right_copies:
        copy.wait()


def mix(wavefunction, left_ops, right_ops, split):
    k_dev, rows, width = left_ops.shape
    sec_dev = wavefunction.shape[0]
    return pl.pallas_call(
        functools.partial(mix_kernel, split),
        out_shape=[
            pltpu.VMEM((k_dev, sec_dev, rows, width), jnp.bfloat16),
            pltpu.VMEM(right_ops.shape, jnp.bfloat16),
        ],
        in_specs=[pl.BlockSpec(memory_space=pltpu.HBM)] * 3,
        out_specs=[pl.BlockSpec(memory_space=pltpu.VMEM)] * 2,
        scratch_shapes=[
            pltpu.VMEM(wavefunction.shape, jnp.bfloat16),
            pltpu.VMEM(left_ops.shape, jnp.bfloat16),
            pltpu.SemaphoreType.DMA((3 + k_dev // MIX_TERMS,)),
        ],
        compiler_params=pltpu.CompilerParams(vmem_limit_bytes=24 * MIB),
        cost_estimate=pl.CostEstimate(
            flops=2 * k_dev * sec_dev * rows * width * width,
            bytes_accessed=2 * (left_ops.size + right_ops.size),
            transcendentals=0,
        ),
    )(*(pltpu.with_memory_space_constraint(x, pltpu.HBM) for x in (wavefunction, left_ops, right_ops)))


def reaches(shift, group, sec_dev, targets):
    return wrapped(-shift - group * sec_dev + sec_dev - 1, targets) < 2 * sec_dev - 1


def sum_kernel(far, stage, shift_ref, coef_ref, mixed_ref, held_ref, *refs):
    terms, sec_dev, rows, width = mixed_ref.shape
    targets = coef_ref.shape[0]
    groups = targets // sec_dev
    half = width // 2
    picked = refs[-1]

    def pick(k, count):
        picked[count] = k
        if stage is None:
            return count + 1
        wanted = reaches(shift_ref[k], far, sec_dev, targets) == (stage == 0)
        return count + jnp.where(wanted, 1, 0)

    count = lax.fori_loop(0, terms, pick, 0)
    for i in range(SUM_TERMS):
        picked[count + i] = 0

    if stage is None:
        sums = refs[:1]
    elif stage == 0:
        sums, rounded = refs[:2], refs[2]
    else:
        before, sums, rounded = refs[:2], (refs[2], refs[-2]), refs[3:-2]
    for total in sums:
        total[...] = jnp.zeros_like(total)

    @pl.loop(0, lax.div(count + SUM_TERMS - 1, SUM_TERMS))
    def _(step):
        for t in range(SUM_TERMS):
            at = step * SUM_TERMS + t
            k = picked[at]
            product = lax.dot_general(
                mixed_ref[k].reshape(sec_dev * rows, width),
                held_ref[k],
                (((1,), (1,)), ((), ())),
                preferred_element_type=jnp.float32,
            )
            for s in range(sec_dev):
                target = wrapped(s - shift_ref[k], targets)
                weight = jnp.where(at < count, coef_ref[target, k], 0.0)
                scaled = weight * product[s * rows : (s + 1) * rows]
                if stage is None:
                    sums[0][target] += scaled
                else:
                    sums[0][target] += scaled[:, half:]
                    sums[1][target] += scaled[:, :half]

    def part(ref, g):
        return ref[g * sec_dev : (g + 1) * sec_dev]

    if stage == 0:
        rounded[...] = part(sums[1], far).astype(jnp.bfloat16)
    elif stage == 1:
        near = [g for g in range(1, groups) if g != far]
        for g in near:
            sums[0][g * sec_dev : (g + 1) * sec_dev] += part(before[0], g)
        for g, out in zip([0] + near, rounded):
            theirs = part(sums[1], g)
            out[...] = (theirs if g == 0 else theirs + part(before[1], g)).astype(jnp.bfloat16)


def summed(shift, coef, mixed, held, far, stage, before=()):
    k_dev, sec_dev, rows, width = mixed.shape
    targets = coef.shape[0]
    columns = width if stage is None else width // 2
    whole = pltpu.VMEM((targets, rows, columns), jnp.float32)
    rounded = pltpu.VMEM((sec_dev, rows, columns), jnp.bfloat16)
    scratch = [pltpu.SMEM((k_dev + SUM_TERMS,), jnp.int32)]
    out_shape = [whole]
    if stage == 0:
        out_shape = [whole, whole, rounded]
    elif stage == 1:
        out_shape = [whole] + [rounded] * (targets // sec_dev - 1)
        scratch = [whole] + scratch
    in_vmem = (mixed, held, *before)
    return pl.pallas_call(
        functools.partial(sum_kernel, far, stage),
        out_shape=out_shape,
        in_specs=[pl.BlockSpec(memory_space=pltpu.SMEM)] * 2
        + [pl.BlockSpec(memory_space=pltpu.VMEM)] * len(in_vmem),
        out_specs=[pl.BlockSpec(memory_space=pltpu.VMEM)] * len(out_shape),
        scratch_shapes=scratch,
        compiler_params=pltpu.CompilerParams(vmem_limit_bytes=24 * MIB),
        cost_estimate=pl.CostEstimate(
            flops=k_dev * sec_dev * rows * width * width,
            bytes_accessed=mixed.size + held.size,
            transcendentals=0,
        ),
    )(
        pltpu.with_memory_space_constraint(shift, pltpu.HBM),
        coef,
        *(pltpu.with_memory_space_constraint(x, pltpu.VMEM) for x in in_vmem),
    )


def shift_by(value, axis, distance):
    size = lax.axis_size(axis)
    return lax.ppermute(value, axis, [(i, (i + distance) % size) for i in range(size)])


def after(value, other):
    return lax.optimization_barrier((value, other))[0]


def per_device(wavefunction, left_ops, right_ops, site_coef, coupled, sector_shift):
    sec_dev = wavefunction.shape[0]
    devices = lax.axis_size("sector")
    live = jnp.where(coupled.T > 0, site_coef.T, 0.0)
    split = lax.axis_size("op") == 2 and devices == 4
    mixed, held = mix(wavefunction, left_ops, right_ops, split)

    if split:
        coefs = [live] + [shift_by(live, "sector", -g) for g in range(1, devices)]
        coef = jnp.concatenate(coefs, axis=0)
        far, near = 2, (1, 3)

        def own(sums, g):
            return sums[g * sec_dev : (g + 1) * sec_dev]

        *first, theirs = summed(sector_shift, coef, mixed, held, far, 0)
        crossed = shift_by(theirs, "op", 1)
        mine, *theirs = summed(sector_shift, coef, mixed, held, far, 1, first)
        other = after(crossed, mine).astype(jnp.float32)
        both = (own(first[0], far) + other).astype(jnp.bfloat16)
        arrived = [shift_by(both, "sector", far)]
        crossed = {g: shift_by(after(theirs[at], both), "op", 1) for at, g in enumerate(near, 1)}
        for g in near:
            if g == near[1]:
                crossed[0] = shift_by(after(theirs[0], both), "op", 1)
            other = after(crossed[g], both).astype(jnp.float32)
            both = (own(mine, g) + other).astype(jnp.bfloat16)
            arrived.append(shift_by(both, "sector", g))
        sigma = own(mine, 0) + after(crossed[0], both).astype(jnp.float32)
        for other in arrived:
            sigma = lax.optimization_barrier(sigma) + other.astype(jnp.float32)
        return sigma

    first = lax.axis_index("sector") * sec_dev
    coef = jnp.roll(lax.all_gather(live, "sector", axis=0, tiled=True), -first, axis=0)
    (total,) = summed(sector_shift, coef, mixed, held, None, None)
    total = jnp.roll(total, first, axis=0)
    total = lax.psum_scatter(total, "op", scatter_dimension=2, tiled=True)
    return lax.psum_scatter(total, "sector", scatter_dimension=0, tiled=True)


def solution(mesh):
    placed = (
        P(("groups", "sector"), None, None),
        P(("groups", "op"), "rep", None),
        P(("groups", "op"), None, None),
        P(("groups", "op"), "sector"),
        P(("groups", "op"), "sector"),
        P(("groups", "op")),
    )
    return jax.shard_map(
        per_device,
        mesh=mesh,
        in_specs=placed,
        out_specs=P(("groups", "sector"), "rep", "op"),
        check_vma=False,
    )
```

```python
import functools

import jax
import jax.numpy as jnp
from jax import lax
from jax.experimental import pallas as pl
from jax.experimental.pallas import tpu as pltpu
from jax.sharding import PartitionSpec as P

MIX_TERMS = 16
SUM_TERMS = 4
MIB = 1024 * 1024


def wrapped(value, size):
    if size & (size - 1) == 0:
        return value & (size - 1)
    return lax.rem(value + size, size)


def mix_kernel(split, wave_ref, left_ref, right_ref, mixed_ref, held_ref, wave, left, sems):
    sec_dev = wave.shape[0]
    terms, rows, width = left.shape
    chunks = terms // MIX_TERMS

    def left_copy(c):
        part = pl.ds(c * MIX_TERMS, MIX_TERMS)
        return pltpu.make_async_copy(left_ref.at[part], left.at[part], sems.at[3 + c])

    wave_copy = pltpu.make_async_copy(wave_ref, wave, sems.at[0])
    wave_copy.start()
    for c in range(chunks):
        left_copy(c).start()
    if split:
        half = width // 2
        side = lax.axis_index("op")
        mine = pl.multiple_of(side * half, half)
        theirs = pl.multiple_of((1 - side) * half, half)
        right_copies = [
            pltpu.make_async_copy(
                right_ref.at[:, pl.ds(theirs, half)], held_ref.at[:, pl.ds(0, half)], sems.at[1]
            ),
            pltpu.make_async_copy(
                right_ref.at[:, pl.ds(mine, half)], held_ref.at[:, pl.ds(half, half)], sems.at[2]
            ),
        ]
    else:
        right_copies = [pltpu.make_async_copy(right_ref, held_ref, sems.at[1])]
    for copy in right_copies:
        copy.start()
    wave_copy.wait()

    @pl.loop(0, chunks)
    def _(c):
        left_copy(c).wait()
        part = pl.ds(c * MIX_TERMS, MIX_TERMS)
        rows_in = left[part].reshape(MIX_TERMS * rows, width)
        for s in range(sec_dev):
            product = jnp.dot(rows_in, wave[s], preferred_element_type=jnp.float32)
            mixed_ref[part, s] = product.astype(jnp.bfloat16).reshape(MIX_TERMS, rows, width)

    for copy in right_copies:
        copy.wait()


def mix(wavefunction, left_ops, right_ops, split):
    k_dev, rows, width = left_ops.shape
    sec_dev = wavefunction.shape[0]
    return pl.pallas_call(
        functools.partial(mix_kernel, split),
        out_shape=[
            pltpu.VMEM((k_dev, sec_dev, rows, width), jnp.bfloat16),
            pltpu.VMEM(right_ops.shape, jnp.bfloat16),
        ],
        in_specs=[pl.BlockSpec(memory_space=pltpu.HBM)] * 3,
        out_specs=[pl.BlockSpec(memory_space=pltpu.VMEM)] * 2,
        scratch_shapes=[
            pltpu.VMEM(wavefunction.shape, jnp.bfloat16),
            pltpu.VMEM(left_ops.shape, jnp.bfloat16),
            pltpu.SemaphoreType.DMA((3 + k_dev // MIX_TERMS,)),
        ],
        compiler_params=pltpu.CompilerParams(vmem_limit_bytes=24 * MIB),
        cost_estimate=pl.CostEstimate(
            flops=2 * k_dev * sec_dev * rows * width * width,
            bytes_accessed=2 * (left_ops.size + right_ops.size),
            transcendentals=0,
        ),
    )(*(pltpu.with_memory_space_constraint(x, pltpu.HBM) for x in (wavefunction, left_ops, right_ops)))


def reaches(shift, group, sec_dev, targets):
    return wrapped(-shift - group * sec_dev + sec_dev - 1, targets) < 2 * sec_dev - 1


def sum_kernel(order, stage, shift_ref, coef_ref, mixed_ref, held_ref, *refs):
    terms, sec_dev, rows, width = mixed_ref.shape
    targets = coef_ref.shape[0]
    half = width // 2
    picked = refs[-1]

    def pick(k, count):
        picked[count] = k
        if stage is None:
            return count + 1
        wanted = True
        for at, groups in enumerate(order[: stage + 1]):
            if at < stage:
                wanted &= ~reaches(shift_ref[k], groups[0], sec_dev, targets)
            elif at < len(order) - 1:
                wanted &= reaches(shift_ref[k], groups[0], sec_dev, targets)
        return count + jnp.where(wanted, 1, 0)

    count = lax.fori_loop(0, terms, pick, 0)
    for i in range(SUM_TERMS):
        picked[count + i] = 0

    if stage is None:
        sums = refs[:1]
    elif stage == 0:
        sums, outs = refs[:2], refs[2:-1]
    else:
        sums, outs = refs[2:4], refs[4:-1]
    if not stage:
        for total in sums:
            total[...] = jnp.zeros_like(total)

    @pl.loop(0, lax.div(count + SUM_TERMS - 1, SUM_TERMS))
    def _(step):
        for t in range(SUM_TERMS):
            at = step * SUM_TERMS + t
            k = picked[at]
            product = lax.dot_general(
                mixed_ref[k].reshape(sec_dev * rows, width),
                held_ref[k],
                (((1,), (1,)), ((), ())),
                preferred_element_type=jnp.float32,
            )
            for s in range(sec_dev):
                target = wrapped(s - shift_ref[k], targets)
                weight = jnp.where(at < count, coef_ref[target, k], 0.0)
                scaled = weight * product[s * rows : (s + 1) * rows]
                if stage is None:
                    sums[0][target] += scaled
                else:
                    sums[0][target] += scaled[:, half:]
                    sums[1][target] += scaled[:, :half]

    if stage is not None:
        for at, g in enumerate(order[stage]):
            part = slice(g * sec_dev, (g + 1) * sec_dev)
            outs[2 * at][...] = sums[0][part]
            outs[2 * at + 1][...] = sums[1][part].astype(jnp.bfloat16)


def summed(shift, coef, mixed, held, order, stage, sums=()):
    k_dev, sec_dev, rows, width = mixed.shape
    targets = coef.shape[0]
    columns = width if stage is None else width // 2
    whole = pltpu.VMEM((targets, rows, columns), jnp.float32)
    out_shape = [whole]
    if stage is not None:
        out_shape = [whole] * 2
        for _ in order[stage]:
            for dtype in (jnp.float32, jnp.bfloat16):
                out_shape.append(pltpu.VMEM((sec_dev, rows, columns), dtype))
    in_vmem = (mixed, held, *sums)
    return pl.pallas_call(
        functools.partial(sum_kernel, order, stage),
        out_shape=out_shape,
        in_specs=[pl.BlockSpec(memory_space=pltpu.SMEM)] * 2
        + [pl.BlockSpec(memory_space=pltpu.VMEM)] * len(in_vmem),
        out_specs=[pl.BlockSpec(memory_space=pltpu.VMEM)] * len(out_shape),
        input_output_aliases={4 + i: i for i in range(len(sums))},
        scratch_shapes=[pltpu.SMEM((k_dev + SUM_TERMS,), jnp.int32)],
        compiler_params=pltpu.CompilerParams(vmem_limit_bytes=24 * MIB),
        cost_estimate=pl.CostEstimate(
            flops=k_dev * sec_dev * rows * width * width,
            bytes_accessed=mixed.size + held.size,
            transcendentals=0,
        ),
    )(
        pltpu.with_memory_space_constraint(shift, pltpu.HBM),
        coef,
        *(pltpu.with_memory_space_constraint(x, pltpu.VMEM) for x in in_vmem),
    )


def shift_by(value, axis, distance):
    size = lax.axis_size(axis)
    return lax.ppermute(value, axis, [(i, (i + distance) % size) for i in range(size)])


def after(value, other):
    return lax.optimization_barrier((value, other))[0]


def per_device(wavefunction, left_ops, right_ops, site_coef, coupled, sector_shift):
    sec_dev = wavefunction.shape[0]
    devices = lax.axis_size("sector")
    live = jnp.where(coupled.T > 0, site_coef.T, 0.0)
    split = lax.axis_size("op") == 2 and devices == 4
    mixed, held = mix(wavefunction, left_ops, right_ops, split)

    if split:
        coefs = [live] + [shift_by(live, "sector", -g) for g in range(1, devices)]
        coef = jnp.concatenate(coefs, axis=0)
        order = ((2,), (3,), (1, 0))
        *sums, mine_2, theirs_2 = summed(sector_shift, coef, mixed, held, order, 0)
        crossed_2 = shift_by(theirs_2, "op", 1)
        *sums, mine_3, theirs_3 = summed(sector_shift, coef, mixed, held, order, 1, sums)
        crossed_3 = shift_by(theirs_3, "op", 1)
        both_2 = (mine_2 + after(crossed_2, mine_3).astype(jnp.float32)).astype(jnp.bfloat16)
        arrived_2 = shift_by(both_2, "sector", 2)
        _, _, mine_1, theirs_1, mine_0, theirs_0 = summed(
            sector_shift, after(coef, both_2), mixed, held, order, 2, sums
        )
        crossed_1 = shift_by(theirs_1, "op", 1)
        both_3 = (mine_3 + after(crossed_3, mine_1).astype(jnp.float32)).astype(jnp.bfloat16)
        arrived_3 = shift_by(both_3, "sector", 3)
        crossed_0 = shift_by(after(theirs_0, both_3), "op", 1)
        both_1 = (mine_1 + after(crossed_1, both_3).astype(jnp.float32)).astype(jnp.bfloat16)
        arrived_1 = shift_by(both_1, "sector", 1)
        sigma = mine_0 + after(crossed_0, both_1).astype(jnp.float32)
        for other in (arrived_2, arrived_3, arrived_1):
            sigma = lax.optimization_barrier(sigma) + other.astype(jnp.float32)
        return sigma

    first = lax.axis_index("sector") * sec_dev
    coef = jnp.roll(lax.all_gather(live, "sector", axis=0, tiled=True), -first, axis=0)
    (total,) = summed(sector_shift, coef, mixed, held, (), None)
    total = jnp.roll(total, first, axis=0)
    total = lax.psum_scatter(total, "op", scatter_dimension=2, tiled=True)
    return lax.psum_scatter(total, "sector", scatter_dimension=0, tiled=True)


def solution(mesh):
    placed = (
        P(("groups", "sector"), None, None),
        P(("groups", "op"), "rep", None),
        P(("groups", "op"), None, None),
        P(("groups", "op"), "sector"),
        P(("groups", "op"), "sector"),
        P(("groups", "op")),
    )
    return jax.shard_map(
        per_device,
        mesh=mesh,
        in_specs=placed,
        out_specs=P(("groups", "sector"), "rep", "op"),
        check_vma=False,
    )
```

```python
import functools

import jax
import jax.numpy as jnp
from jax import lax
from jax.experimental import pallas as pl
from jax.experimental.pallas import tpu as pltpu
from jax.sharding import PartitionSpec as P

MIX_TERMS = 16
SUM_TERMS = 4
MIB = 1024 * 1024


def wrapped(value, size):
    if size & (size - 1) == 0:
        return value & (size - 1)
    return lax.rem(value + size, size)


def mix_kernel(split, wave_ref, left_ref, right_ref, mixed_ref, held_ref, wave, left, sems):
    sec_dev = wave.shape[0]
    terms, rows, width = left.shape
    chunks = terms // MIX_TERMS

    def left_copy(c):
        part = pl.ds(c * MIX_TERMS, MIX_TERMS)
        return pltpu.make_async_copy(left_ref.at[part], left.at[part], sems.at[3 + c])

    wave_copy = pltpu.make_async_copy(wave_ref, wave, sems.at[0])
    wave_copy.start()
    for c in range(chunks):
        left_copy(c).start()
    if split:
        half = width // 2
        side = lax.axis_index("op")
        mine = pl.multiple_of(side * half, half)
        theirs = pl.multiple_of((1 - side) * half, half)
        right_copies = [
            pltpu.make_async_copy(
                right_ref.at[:, pl.ds(theirs, half)], held_ref.at[:, pl.ds(0, half)], sems.at[1]
            ),
            pltpu.make_async_copy(
                right_ref.at[:, pl.ds(mine, half)], held_ref.at[:, pl.ds(half, half)], sems.at[2]
            ),
        ]
    else:
        right_copies = [pltpu.make_async_copy(right_ref, held_ref, sems.at[1])]
    for copy in right_copies:
        copy.start()
    wave_copy.wait()

    @pl.loop(0, chunks)
    def _(c):
        left_copy(c).wait()
        part = pl.ds(c * MIX_TERMS, MIX_TERMS)
        rows_in = left[part].reshape(MIX_TERMS * rows, width)
        for s in range(sec_dev):
            product = jnp.dot(rows_in, wave[s], preferred_element_type=jnp.float32)
            mixed_ref[part, s] = product.astype(jnp.bfloat16).reshape(MIX_TERMS, rows, width)

    for copy in right_copies:
        copy.wait()


def mix(wavefunction, left_ops, right_ops, split):
    k_dev, rows, width = left_ops.shape
    sec_dev = wavefunction.shape[0]
    return pl.pallas_call(
        functools.partial(mix_kernel, split),
        out_shape=[
            pltpu.VMEM((k_dev, sec_dev, rows, width), jnp.bfloat16),
            pltpu.VMEM(right_ops.shape, jnp.bfloat16),
        ],
        in_specs=[pl.BlockSpec(memory_space=pltpu.HBM)] * 3,
        out_specs=[pl.BlockSpec(memory_space=pltpu.VMEM)] * 2,
        scratch_shapes=[
            pltpu.VMEM(wavefunction.shape, jnp.bfloat16),
            pltpu.VMEM(left_ops.shape, jnp.bfloat16),
            pltpu.SemaphoreType.DMA((3 + k_dev // MIX_TERMS,)),
        ],
        compiler_params=pltpu.CompilerParams(vmem_limit_bytes=24 * MIB),
        cost_estimate=pl.CostEstimate(
            flops=2 * k_dev * sec_dev * rows * width * width,
            bytes_accessed=2 * (left_ops.size + right_ops.size),
            transcendentals=0,
        ),
    )(*(pltpu.with_memory_space_constraint(x, pltpu.HBM) for x in (wavefunction, left_ops, right_ops)))


def reaches(shift, group, sec_dev, targets):
    return wrapped(-shift - group * sec_dev + sec_dev - 1, targets) < 2 * sec_dev - 1


def sum_kernel(order, stage, shift_ref, coef_ref, mixed_ref, held_ref, *refs):
    terms, sec_dev, rows, width = mixed_ref.shape
    targets = coef_ref.shape[0]
    half = width // 2
    picked = refs[-1]

    def pick(k, count):
        picked[count] = k
        if stage is None:
            return count + 1
        wanted = True
        for at, groups in enumerate(order[: stage + 1]):
            if at < stage:
                wanted &= ~reaches(shift_ref[k], groups[0], sec_dev, targets)
            elif at < len(order) - 1:
                wanted &= reaches(shift_ref[k], groups[0], sec_dev, targets)
        return count + jnp.where(wanted, 1, 0)

    count = lax.fori_loop(0, terms, pick, 0)
    for i in range(SUM_TERMS):
        picked[count + i] = 0

    if stage is None:
        sums = refs[:1]
    elif stage == 0:
        sums, outs = refs[:2], refs[2:-1]
    else:
        sums, outs = refs[2:4], refs[4:-1]
    if not stage:
        for total in sums:
            total[...] = jnp.zeros_like(total)

    @pl.loop(0, lax.div(count + SUM_TERMS - 1, SUM_TERMS))
    def _(step):
        for t in range(SUM_TERMS):
            at = step * SUM_TERMS + t
            k = picked[at]
            product = lax.dot_general(
                mixed_ref[k].reshape(sec_dev * rows, width),
                held_ref[k],
                (((1,), (1,)), ((), ())),
                preferred_element_type=jnp.float32,
            )
            for s in range(sec_dev):
                target = wrapped(s - shift_ref[k], targets)
                weight = jnp.where(at < count, coef_ref[target, k], 0.0)
                scaled = weight * product[s * rows : (s + 1) * rows]
                if stage is None:
                    sums[0][target] += scaled
                else:
                    sums[0][target] += scaled[:, half:]
                    sums[1][target] += scaled[:, :half]

    if stage is not None:
        for at, g in enumerate(order[stage]):
            part = slice(g * sec_dev, (g + 1) * sec_dev)
            outs[2 * at][...] = sums[0][part]
            outs[2 * at + 1][...] = sums[1][part].astype(jnp.bfloat16)


def summed(shift, coef, mixed, held, order, stage, sums=()):
    k_dev, sec_dev, rows, width = mixed.shape
    targets = coef.shape[0]
    columns = width if stage is None else width // 2
    whole = pltpu.VMEM((targets, rows, columns), jnp.float32)
    out_shape = [whole]
    if stage is not None:
        out_shape = [whole] * 2
        for _ in order[stage]:
            for dtype in (jnp.float32, jnp.bfloat16):
                out_shape.append(pltpu.VMEM((sec_dev, rows, columns), dtype))
    in_vmem = (mixed, held, *sums)
    return pl.pallas_call(
        functools.partial(sum_kernel, order, stage),
        out_shape=out_shape,
        in_specs=[pl.BlockSpec(memory_space=pltpu.SMEM)] * 2
        + [pl.BlockSpec(memory_space=pltpu.VMEM)] * len(in_vmem),
        out_specs=[pl.BlockSpec(memory_space=pltpu.VMEM)] * len(out_shape),
        input_output_aliases={4 + i: i for i in range(len(sums))},
        scratch_shapes=[pltpu.SMEM((k_dev + SUM_TERMS,), jnp.int32)],
        compiler_params=pltpu.CompilerParams(vmem_limit_bytes=24 * MIB),
        cost_estimate=pl.CostEstimate(
            flops=k_dev * sec_dev * rows * width * width,
            bytes_accessed=mixed.size + held.size,
            transcendentals=0,
        ),
    )(
        pltpu.with_memory_space_constraint(shift, pltpu.HBM),
        coef,
        *(pltpu.with_memory_space_constraint(x, pltpu.VMEM) for x in in_vmem),
    )


def shift_by(value, axis, distance):
    size = lax.axis_size(axis)
    return lax.ppermute(value, axis, [(i, (i + distance) % size) for i in range(size)])


def after(value, other):
    return lax.optimization_barrier((value, other))[0]


def per_device(wavefunction, left_ops, right_ops, site_coef, coupled, sector_shift):
    sec_dev = wavefunction.shape[0]
    devices = lax.axis_size("sector")
    live = jnp.where(coupled.T > 0, site_coef.T, 0.0)
    split = lax.axis_size("op") == 2 and devices == 4
    mixed, held = mix(wavefunction, left_ops, right_ops, split)

    if split:
        coefs = [live] + [shift_by(live, "sector", -g) for g in range(1, devices)]
        coef = jnp.concatenate(coefs, axis=0)
        order = ((2,), (1, 3, 0))
        *sums, mine_2, theirs_2 = summed(sector_shift, coef, mixed, held, order, 0)
        crossed_2 = shift_by(theirs_2, "op", 1)
        _, _, mine_1, theirs_1, mine_3, theirs_3, mine_0, theirs_0 = summed(
            sector_shift, after(coef, theirs_2), mixed, held, order, 1, sums
        )
        both_2 = (mine_2 + after(crossed_2, mine_1).astype(jnp.float32)).astype(jnp.bfloat16)
        arrived_2 = shift_by(both_2, "sector", 2)
        crossed_1 = shift_by(after(theirs_1, both_2), "op", 1)
        crossed_3 = shift_by(after(theirs_3, both_2), "op", 1)
        both_1 = (mine_1 + after(crossed_1, both_2).astype(jnp.float32)).astype(jnp.bfloat16)
        arrived_1 = shift_by(both_1, "sector", 1)
        crossed_0 = shift_by(after(theirs_0, both_1), "op", 1)
        both_3 = (mine_3 + after(crossed_3, both_1).astype(jnp.float32)).astype(jnp.bfloat16)
        arrived_3 = shift_by(both_3, "sector", 3)
        sigma = mine_0 + after(crossed_0, both_3).astype(jnp.float32)
        for other in (arrived_2, arrived_1, arrived_3):
            sigma = lax.optimization_barrier(sigma) + other.astype(jnp.float32)
        return sigma

    first = lax.axis_index("sector") * sec_dev
    coef = jnp.roll(lax.all_gather(live, "sector", axis=0, tiled=True), -first, axis=0)
    (total,) = summed(sector_shift, coef, mixed, held, (), None)
    total = jnp.roll(total, first, axis=0)
    total = lax.psum_scatter(total, "op", scatter_dimension=2, tiled=True)
    return lax.psum_scatter(total, "sector", scatter_dimension=0, tiled=True)


def solution(mesh):
    placed = (
        P(("groups", "sector"), None, None),
        P(("groups", "op"), "rep", None),
        P(("groups", "op"), None, None),
        P(("groups", "op"), "sector"),
        P(("groups", "op"), "sector"),
        P(("groups", "op")),
    )
    return jax.shard_map(
        per_device,
        mesh=mesh,
        in_specs=placed,
        out_specs=P(("groups", "sector"), "rep", "op"),
        check_vma=False,
    )
```

```python
import functools

import jax
import jax.numpy as jnp
from jax import lax
from jax.experimental import pallas as pl
from jax.experimental.pallas import tpu as pltpu
from jax.sharding import PartitionSpec as P

MIX_TERMS = 16
SUM_TERMS = 4
MIB = 1024 * 1024


def wrapped(value, size):
    if size & (size - 1) == 0:
        return value & (size - 1)
    return lax.rem(value + size, size)


def mix_kernel(split, wave_ref, left_ref, right_ref, mixed_ref, held_ref, wave, left, sems):
    sec_dev = wave.shape[0]
    terms, rows, width = left.shape
    chunks = terms // MIX_TERMS

    def left_copy(c):
        part = pl.ds(c * MIX_TERMS, MIX_TERMS)
        return pltpu.make_async_copy(left_ref.at[part], left.at[part], sems.at[3 + c])

    wave_copy = pltpu.make_async_copy(wave_ref, wave, sems.at[0])
    wave_copy.start()
    for c in range(chunks):
        left_copy(c).start()
    if split:
        half = width // 2
        side = lax.axis_index("op")
        mine = pl.multiple_of(side * half, half)
        theirs = pl.multiple_of((1 - side) * half, half)
        right_copies = [
            pltpu.make_async_copy(
                right_ref.at[:, pl.ds(theirs, half)], held_ref.at[:, pl.ds(0, half)], sems.at[1]
            ),
            pltpu.make_async_copy(
                right_ref.at[:, pl.ds(mine, half)], held_ref.at[:, pl.ds(half, half)], sems.at[2]
            ),
        ]
    else:
        right_copies = [pltpu.make_async_copy(right_ref, held_ref, sems.at[1])]
    for copy in right_copies:
        copy.start()
    wave_copy.wait()

    @pl.loop(0, chunks)
    def _(c):
        left_copy(c).wait()
        part = pl.ds(c * MIX_TERMS, MIX_TERMS)
        rows_in = left[part].reshape(MIX_TERMS * rows, width)
        for s in range(sec_dev):
            product = jnp.dot(rows_in, wave[s], preferred_element_type=jnp.float32)
            mixed_ref[part, s] = product.astype(jnp.bfloat16).reshape(MIX_TERMS, rows, width)

    for copy in right_copies:
        copy.wait()


def mix(wavefunction, left_ops, right_ops, split):
    k_dev, rows, width = left_ops.shape
    sec_dev = wavefunction.shape[0]
    return pl.pallas_call(
        functools.partial(mix_kernel, split),
        out_shape=[
            pltpu.VMEM((k_dev, sec_dev, rows, width), jnp.bfloat16),
            pltpu.VMEM(right_ops.shape, jnp.bfloat16),
        ],
        in_specs=[pl.BlockSpec(memory_space=pltpu.HBM)] * 3,
        out_specs=[pl.BlockSpec(memory_space=pltpu.VMEM)] * 2,
        scratch_shapes=[
            pltpu.VMEM(wavefunction.shape, jnp.bfloat16),
            pltpu.VMEM(left_ops.shape, jnp.bfloat16),
            pltpu.SemaphoreType.DMA((3 + k_dev // MIX_TERMS,)),
        ],
        compiler_params=pltpu.CompilerParams(vmem_limit_bytes=24 * MIB),
        cost_estimate=pl.CostEstimate(
            flops=2 * k_dev * sec_dev * rows * width * width,
            bytes_accessed=2 * (left_ops.size + right_ops.size),
            transcendentals=0,
        ),
    )(*(pltpu.with_memory_space_constraint(x, pltpu.HBM) for x in (wavefunction, left_ops, right_ops)))


def sum_kernel(order, stage, shift_ref, coef_ref, mixed_ref, held_ref, *refs):
    terms, sec_dev, rows, width = mixed_ref.shape
    targets = coef_ref.shape[0]
    half = width // 2
    picked = refs[-1]
    first = lax.axis_index("sector") * sec_dev

    def reaches(k, group):
        start = (first ^ (group * sec_dev)) - first
        return wrapped(sec_dev - 1 - start - shift_ref[k], targets) < 2 * sec_dev - 1

    def pick(k, count):
        picked[count] = k
        if stage is None:
            return count + 1
        wanted = functools.reduce(jnp.logical_or, [reaches(k, group) for group in order[0]])
        return count + jnp.where(wanted == (stage == 0), 1, 0)

    count = lax.fori_loop(0, terms, pick, 0)
    for i in range(SUM_TERMS):
        picked[count + i] = 0

    if stage is None:
        sums = refs[:1]
    elif stage == 0:
        sums, outs = refs[:2], refs[2:-1]
    else:
        sums, outs = refs[2:4], refs[4:-1]
    if not stage:
        for total in sums:
            total[...] = jnp.zeros_like(total)

    @pl.loop(0, lax.div(count + SUM_TERMS - 1, SUM_TERMS))
    def _(step):
        for t in range(SUM_TERMS):
            at = step * SUM_TERMS + t
            k = picked[at]
            product = lax.dot_general(
                mixed_ref[k].reshape(sec_dev * rows, width),
                held_ref[k],
                (((1,), (1,)), ((), ())),
                preferred_element_type=jnp.float32,
            )
            for s in range(sec_dev):
                slot = wrapped(first + s - shift_ref[k], targets)
                if stage is not None:
                    slot ^= first
                weight = jnp.where(at < count, coef_ref[slot, k], 0.0)
                scaled = weight * product[s * rows : (s + 1) * rows]
                if stage is None:
                    sums[0][slot] += scaled
                else:
                    sums[0][slot] += scaled[:, half:]
                    sums[1][slot] += scaled[:, :half]

    if stage is not None:
        for at, g in enumerate(order[stage]):
            part = slice(g * sec_dev, (g + 1) * sec_dev)
            outs[2 * at][...] = sums[0][part]
            outs[2 * at + 1][...] = sums[1][part].astype(jnp.bfloat16)


def summed(shift, coef, mixed, held, order, stage, sums=()):
    k_dev, sec_dev, rows, width = mixed.shape
    targets = coef.shape[0]
    columns = width if stage is None else width // 2
    whole = pltpu.VMEM((targets, rows, columns), jnp.float32)
    out_shape = [whole]
    if stage is not None:
        out_shape = [whole] * 2
        for _ in order[stage]:
            for dtype in (jnp.float32, jnp.bfloat16):
                out_shape.append(pltpu.VMEM((sec_dev, rows, columns), dtype))
    in_vmem = (mixed, held, *sums)
    return pl.pallas_call(
        functools.partial(sum_kernel, order, stage),
        out_shape=out_shape,
        in_specs=[pl.BlockSpec(memory_space=pltpu.SMEM)] * 2
        + [pl.BlockSpec(memory_space=pltpu.VMEM)] * len(in_vmem),
        out_specs=[pl.BlockSpec(memory_space=pltpu.VMEM)] * len(out_shape),
        input_output_aliases={4 + i: i for i in range(len(sums))},
        scratch_shapes=[pltpu.SMEM((k_dev + SUM_TERMS,), jnp.int32)],
        compiler_params=pltpu.CompilerParams(vmem_limit_bytes=24 * MIB),
        cost_estimate=pl.CostEstimate(
            flops=k_dev * sec_dev * rows * width * width,
            bytes_accessed=mixed.size + held.size,
            transcendentals=0,
        ),
    )(
        pltpu.with_memory_space_constraint(shift, pltpu.HBM),
        coef,
        *(pltpu.with_memory_space_constraint(x, pltpu.VMEM) for x in in_vmem),
    )


def swap(value, axis, mask):
    return lax.ppermute(value, axis, [(i, i ^ mask) for i in range(lax.axis_size(axis))])


def after(value, other):
    return lax.optimization_barrier((value, other))[0]


def per_device(wavefunction, left_ops, right_ops, site_coef, coupled, sector_shift):
    sec_dev = wavefunction.shape[0]
    devices = lax.axis_size("sector")
    live = jnp.where(coupled.T > 0, site_coef.T, 0.0)
    split = lax.axis_size("op") == 2 and devices == 4 and sec_dev & (sec_dev - 1) == 0
    mixed, held = mix(wavefunction, left_ops, right_ops, split)

    if split:
        pair = jnp.concatenate([live, swap(live, "sector", 1)], axis=0)
        coef = jnp.concatenate([pair, swap(pair, "sector", 2)], axis=0)
        order = ((3, 2), (1, 0))
        *sums, mine_3, theirs_3, mine_2, theirs_2 = summed(
            sector_shift, coef, mixed, held, order, 0
        )
        crossed_3 = swap(theirs_3, "op", 1)
        crossed_2 = swap(theirs_2, "op", 1)
        _, _, mine_1, theirs_1, mine_0, theirs_0 = summed(
            sector_shift, after(coef, theirs_3), mixed, held, order, 1, sums
        )
        both_3 = mine_3 + after(crossed_3, mine_1).astype(jnp.float32)
        both_3 = both_3.astype(jnp.bfloat16)
        relayed = swap(both_3, "sector", 1)
        crossed_1 = swap(after(theirs_1, both_3), "op", 1)
        both_2 = lax.optimization_barrier(mine_2 + after(crossed_2, both_3).astype(jnp.float32))
        crossed_0 = swap(after(theirs_0, both_2), "op", 1)
        both_2 = (both_2 + relayed.astype(jnp.float32)).astype(jnp.bfloat16)
        far = swap(both_2, "sector", 2)
        both_1 = mine_1 + after(crossed_1, both_2).astype(jnp.float32)
        both_1 = both_1.astype(jnp.bfloat16)
        near = swap(both_1, "sector", 1)
        sigma = mine_0 + after(crossed_0, both_1).astype(jnp.float32)
        for other in (near, far):
            sigma = lax.optimization_barrier(sigma) + other.astype(jnp.float32)
        return sigma

    coef = lax.all_gather(live, "sector", axis=0, tiled=True)
    (total,) = summed(sector_shift, coef, mixed, held, (), None)
    total = lax.psum_scatter(total, "op", scatter_dimension=2, tiled=True)
    return lax.psum_scatter(total, "sector", scatter_dimension=0, tiled=True)


def solution(mesh):
    placed = (
        P(("groups", "sector"), None, None),
        P(("groups", "op"), "rep", None),
        P(("groups", "op"), None, None),
        P(("groups", "op"), "sector"),
        P(("groups", "op"), "sector"),
        P(("groups", "op")),
    )
    return jax.shard_map(
        per_device,
        mesh=mesh,
        in_specs=placed,
        out_specs=P(("groups", "sector"), "rep", "op"),
        check_vma=False,
    )
```

```python
import functools

import jax
import jax.numpy as jnp
from jax import lax
from jax.experimental import pallas as pl
from jax.experimental.pallas import tpu as pltpu
from jax.sharding import PartitionSpec as P

MIX_TERMS = 16
SUM_TERMS = 4
MIB = 1024 * 1024


def wrapped(value, size):
    if size & (size - 1) == 0:
        return value & (size - 1)
    return lax.rem(value + size, size)


def mix_kernel(split, wave_ref, left_ref, right_ref, mixed_ref, held_ref, wave, left, sems):
    sec_dev = wave.shape[0]
    terms, rows, width = left.shape
    chunks = terms // MIX_TERMS

    def left_copy(c):
        part = pl.ds(c * MIX_TERMS, MIX_TERMS)
        return pltpu.make_async_copy(left_ref.at[part], left.at[part], sems.at[3 + c])

    wave_copy = pltpu.make_async_copy(wave_ref, wave, sems.at[0])
    wave_copy.start()
    for c in range(chunks):
        left_copy(c).start()
    if split:
        half = width // 2
        side = lax.axis_index("op")
        mine = pl.multiple_of(side * half, half)
        theirs = pl.multiple_of((1 - side) * half, half)
        right_copies = [
            pltpu.make_async_copy(
                right_ref.at[:, pl.ds(theirs, half)], held_ref.at[:, pl.ds(0, half)], sems.at[1]
            ),
            pltpu.make_async_copy(
                right_ref.at[:, pl.ds(mine, half)], held_ref.at[:, pl.ds(half, half)], sems.at[2]
            ),
        ]
    else:
        right_copies = [pltpu.make_async_copy(right_ref, held_ref, sems.at[1])]
    for copy in right_copies:
        copy.start()
    wave_copy.wait()

    @pl.loop(0, chunks)
    def _(c):
        left_copy(c).wait()
        part = pl.ds(c * MIX_TERMS, MIX_TERMS)
        rows_in = left[part].reshape(MIX_TERMS * rows, width)
        for s in range(sec_dev):
            product = jnp.dot(rows_in, wave[s], preferred_element_type=jnp.float32)
            mixed_ref[part, s] = product.astype(jnp.bfloat16).reshape(MIX_TERMS, rows, width)

    for copy in right_copies:
        copy.wait()


def mix(wavefunction, left_ops, right_ops, split):
    k_dev, rows, width = left_ops.shape
    sec_dev = wavefunction.shape[0]
    return pl.pallas_call(
        functools.partial(mix_kernel, split),
        out_shape=[
            pltpu.VMEM((k_dev, sec_dev, rows, width), jnp.bfloat16),
            pltpu.VMEM(right_ops.shape, jnp.bfloat16),
        ],
        in_specs=[pl.BlockSpec(memory_space=pltpu.HBM)] * 3,
        out_specs=[pl.BlockSpec(memory_space=pltpu.VMEM)] * 2,
        scratch_shapes=[
            pltpu.VMEM(wavefunction.shape, jnp.bfloat16),
            pltpu.VMEM(left_ops.shape, jnp.bfloat16),
            pltpu.SemaphoreType.DMA((3 + k_dev // MIX_TERMS,)),
        ],
        compiler_params=pltpu.CompilerParams(vmem_limit_bytes=24 * MIB),
        cost_estimate=pl.CostEstimate(
            flops=2 * k_dev * sec_dev * rows * width * width,
            bytes_accessed=2 * (left_ops.size + right_ops.size),
            transcendentals=0,
        ),
    )(*(pltpu.with_memory_space_constraint(x, pltpu.HBM) for x in (wavefunction, left_ops, right_ops)))


def reaches(shift, group, sec_dev, targets):
    return wrapped(-shift - group * sec_dev + sec_dev - 1, targets) < 2 * sec_dev - 1


def sum_kernel(order, stage, shift_ref, coef_ref, mixed_ref, held_ref, *refs):
    terms, sec_dev, rows, width = mixed_ref.shape
    targets = coef_ref.shape[0]
    half = width // 2
    picked = refs[-1]
    first = lax.axis_index("sector") * sec_dev

    def pick(k, count):
        picked[count] = k
        if stage is None:
            return count + 1
        wanted = True
        for at, groups in enumerate(order[: stage + 1]):
            if at < stage:
                wanted &= ~reaches(shift_ref[k], groups[0], sec_dev, targets)
            elif at < len(order) - 1:
                wanted &= reaches(shift_ref[k], groups[0], sec_dev, targets)
        return count + jnp.where(wanted, 1, 0)

    count = lax.fori_loop(0, terms, pick, 0)
    for i in range(SUM_TERMS):
        picked[count + i] = 0

    if stage is None:
        sums = refs[:1]
    elif stage == 0:
        sums, outs = refs[:2], refs[2:-1]
    else:
        sums, outs = refs[2:4], refs[4:-1]
    if not stage:
        for total in sums:
            total[...] = jnp.zeros_like(total)

    @pl.loop(0, lax.div(count + SUM_TERMS - 1, SUM_TERMS))
    def _(step):
        for t in range(SUM_TERMS):
            at = step * SUM_TERMS + t
            k = picked[at]
            product = lax.dot_general(
                mixed_ref[k].reshape(sec_dev * rows, width),
                held_ref[k],
                (((1,), (1,)), ((), ())),
                preferred_element_type=jnp.float32,
            )
            for s in range(sec_dev):
                target = wrapped(s - shift_ref[k], targets)
                sector = wrapped(first + s - shift_ref[k], targets)
                weight = jnp.where(at < count, coef_ref[sector, k], 0.0)
                scaled = weight * product[s * rows : (s + 1) * rows]
                if stage is None:
                    sums[0][target] += scaled
                else:
                    sums[0][target] += scaled[:, half:]
                    sums[1][target] += scaled[:, :half]

    if stage is not None:
        for at, g in enumerate(order[stage]):
            part = slice(g * sec_dev, (g + 1) * sec_dev)
            outs[2 * at][...] = sums[0][part]
            outs[2 * at + 1][...] = sums[1][part].astype(jnp.bfloat16)


def summed(shift, coef, mixed, held, order, stage, sums=()):
    k_dev, sec_dev, rows, width = mixed.shape
    targets = coef.shape[0]
    columns = width if stage is None else width // 2
    whole = pltpu.VMEM((targets, rows, columns), jnp.float32)
    out_shape = [whole]
    if stage is not None:
        out_shape = [whole] * 2
        for _ in order[stage]:
            for dtype in (jnp.float32, jnp.bfloat16):
                out_shape.append(pltpu.VMEM((sec_dev, rows, columns), dtype))
    in_vmem = (mixed, held, *sums)
    return pl.pallas_call(
        functools.partial(sum_kernel, order, stage),
        out_shape=out_shape,
        in_specs=[pl.BlockSpec(memory_space=pltpu.SMEM)] * 2
        + [pl.BlockSpec(memory_space=pltpu.VMEM)] * len(in_vmem),
        out_specs=[pl.BlockSpec(memory_space=pltpu.VMEM)] * len(out_shape),
        input_output_aliases={4 + i: i for i in range(len(sums))},
        scratch_shapes=[pltpu.SMEM((k_dev + SUM_TERMS,), jnp.int32)],
        compiler_params=pltpu.CompilerParams(vmem_limit_bytes=24 * MIB),
        cost_estimate=pl.CostEstimate(
            flops=k_dev * sec_dev * rows * width * width,
            bytes_accessed=mixed.size + held.size,
            transcendentals=0,
        ),
    )(
        pltpu.with_memory_space_constraint(shift, pltpu.HBM),
        coef,
        *(pltpu.with_memory_space_constraint(x, pltpu.VMEM) for x in in_vmem),
    )


def shift_by(value, axis, distance):
    size = lax.axis_size(axis)
    return lax.ppermute(value, axis, [(i, (i + distance) % size) for i in range(size)])


def after(value, other):
    return lax.optimization_barrier((value, other))[0]


def per_device(wavefunction, left_ops, right_ops, site_coef, coupled, sector_shift):
    sec_dev = wavefunction.shape[0]
    devices = lax.axis_size("sector")
    live = jnp.where(coupled.T > 0, site_coef.T, 0.0)
    split = lax.axis_size("op") == 2 and devices == 4
    mixed, held = mix(wavefunction, left_ops, right_ops, split)

    if split:
        coef = lax.all_to_all(jnp.tile(live, (devices, 1)), "sector", 0, 0, tiled=True)
        order = ((2,), (1, 3, 0))
        *sums, mine_2, theirs_2 = summed(sector_shift, coef, mixed, held, order, 0)
        crossed_2 = shift_by(theirs_2, "op", 1)
        _, _, mine_1, theirs_1, mine_3, theirs_3, mine_0, theirs_0 = summed(
            sector_shift, after(coef, theirs_2), mixed, held, order, 1, sums
        )
        both_2 = (mine_2 + after(crossed_2, mine_1).astype(jnp.float32)).astype(jnp.bfloat16)
        arrived_2 = shift_by(both_2, "sector", 2)
        crossed_1 = shift_by(after(theirs_1, both_2), "op", 1)
        crossed_3 = shift_by(after(theirs_3, both_2), "op", 1)
        both_1 = (mine_1 + after(crossed_1, both_2).astype(jnp.float32)).astype(jnp.bfloat16)
        arrived_1 = shift_by(both_1, "sector", 1)
        crossed_0 = shift_by(after(theirs_0, both_1), "op", 1)
        both_3 = (mine_3 + after(crossed_3, both_1).astype(jnp.float32)).astype(jnp.bfloat16)
        arrived_3 = shift_by(both_3, "sector", 3)
        sigma = mine_0 + after(crossed_0, both_3).astype(jnp.float32)
        for other in (arrived_2, arrived_1, arrived_3):
            sigma = lax.optimization_barrier(sigma) + other.astype(jnp.float32)
        return sigma

    first = lax.axis_index("sector") * sec_dev
    coef = lax.all_gather(live, "sector", axis=0, tiled=True)
    (total,) = summed(sector_shift, coef, mixed, held, (), None)
    total = jnp.roll(total, first, axis=0)
    total = lax.psum_scatter(total, "op", scatter_dimension=2, tiled=True)
    return lax.psum_scatter(total, "sector", scatter_dimension=0, tiled=True)


def solution(mesh):
    placed = (
        P(("groups", "sector"), None, None),
        P(("groups", "op"), "rep", None),
        P(("groups", "op"), None, None),
        P(("groups", "op"), "sector"),
        P(("groups", "op"), "sector"),
        P(("groups", "op")),
    )
    return jax.shard_map(
        per_device,
        mesh=mesh,
        in_specs=placed,
        out_specs=P(("groups", "sector"), "rep", "op"),
        check_vma=False,
    )
```

```python
import functools

import jax
import jax.numpy as jnp
from jax import lax
from jax.experimental import pallas as pl
from jax.experimental.pallas import tpu as pltpu
from jax.sharding import PartitionSpec as P

MIX_TERMS = 16
SUM_TERMS = 4
MIB = 1024 * 1024


def wrapped(value, size):
    if size & (size - 1) == 0:
        return value & (size - 1)
    return lax.rem(value + size, size)


def mix_kernel(split, wave_ref, left_ref, right_ref, mixed_ref, held_ref, wave, left, sems):
    sec_dev = wave.shape[0]
    terms, rows, width = left.shape
    chunks = terms // MIX_TERMS

    def left_copy(c):
        part = pl.ds(c * MIX_TERMS, MIX_TERMS)
        return pltpu.make_async_copy(left_ref.at[part], left.at[part], sems.at[3 + c])

    wave_copy = pltpu.make_async_copy(wave_ref, wave, sems.at[0])
    wave_copy.start()
    for c in range(chunks):
        left_copy(c).start()
    if split:
        half = width // 2
        side = lax.axis_index("op")
        mine = pl.multiple_of(side * half, half)
        theirs = pl.multiple_of((1 - side) * half, half)
        right_copies = [
            pltpu.make_async_copy(
                right_ref.at[:, pl.ds(theirs, half)], held_ref.at[:, pl.ds(0, half)], sems.at[1]
            ),
            pltpu.make_async_copy(
                right_ref.at[:, pl.ds(mine, half)], held_ref.at[:, pl.ds(half, half)], sems.at[2]
            ),
        ]
    else:
        right_copies = [pltpu.make_async_copy(right_ref, held_ref, sems.at[1])]
    for copy in right_copies:
        copy.start()
    wave_copy.wait()

    @pl.loop(0, chunks)
    def _(c):
        left_copy(c).wait()
        part = pl.ds(c * MIX_TERMS, MIX_TERMS)
        rows_in = left[part].reshape(MIX_TERMS * rows, width)
        for s in range(sec_dev):
            product = jnp.dot(rows_in, wave[s], preferred_element_type=jnp.float32)
            mixed_ref[part, s] = product.astype(jnp.bfloat16).reshape(MIX_TERMS, rows, width)

    for copy in right_copies:
        copy.wait()


def mix(wavefunction, left_ops, right_ops, split):
    k_dev, rows, width = left_ops.shape
    sec_dev = wavefunction.shape[0]
    return pl.pallas_call(
        functools.partial(mix_kernel, split),
        out_shape=[
            pltpu.VMEM((k_dev, sec_dev, rows, width), jnp.bfloat16),
            pltpu.VMEM(right_ops.shape, jnp.bfloat16),
        ],
        in_specs=[pl.BlockSpec(memory_space=pltpu.HBM)] * 3,
        out_specs=[pl.BlockSpec(memory_space=pltpu.VMEM)] * 2,
        scratch_shapes=[
            pltpu.VMEM(wavefunction.shape, jnp.bfloat16),
            pltpu.VMEM(left_ops.shape, jnp.bfloat16),
            pltpu.SemaphoreType.DMA((3 + k_dev // MIX_TERMS,)),
        ],
        compiler_params=pltpu.CompilerParams(vmem_limit_bytes=24 * MIB),
        cost_estimate=pl.CostEstimate(
            flops=2 * k_dev * sec_dev * rows * width * width,
            bytes_accessed=2 * (left_ops.size + right_ops.size),
            transcendentals=0,
        ),
    )(*(pltpu.with_memory_space_constraint(x, pltpu.HBM) for x in (wavefunction, left_ops, right_ops)))


def sum_kernel(order, stage, shift_ref, coef_ref, mixed_ref, held_ref, *refs):
    terms, sec_dev, rows, width = mixed_ref.shape
    targets = coef_ref.shape[0]
    half = width // 2
    picked = refs[-1]
    first = lax.axis_index("sector") * sec_dev

    def reaches(k, group):
        start = (first ^ (group * sec_dev)) - first
        return wrapped(sec_dev - 1 - start - shift_ref[k], targets) < 2 * sec_dev - 1

    def pick(k, count):
        picked[count] = k
        if stage is None:
            return count + 1
        wanted = functools.reduce(jnp.logical_or, [reaches(k, group) for group in order[0]])
        return count + jnp.where(wanted == (stage == 0), 1, 0)

    count = lax.fori_loop(0, terms, pick, 0)
    for i in range(SUM_TERMS):
        picked[count + i] = 0

    if stage is None:
        sums = refs[:1]
    elif stage == 0:
        sums, outs = refs[:2], refs[2:-1]
    else:
        sums, outs = refs[2:4], refs[4:-1]
    if not stage:
        for total in sums:
            total[...] = jnp.zeros_like(total)

    @pl.loop(0, lax.div(count + SUM_TERMS - 1, SUM_TERMS))
    def _(step):
        for t in range(SUM_TERMS):
            at = step * SUM_TERMS + t
            k = picked[at]
            product = lax.dot_general(
                mixed_ref[k].reshape(sec_dev * rows, width),
                held_ref[k],
                (((1,), (1,)), ((), ())),
                preferred_element_type=jnp.float32,
            )
            for s in range(sec_dev):
                slot = wrapped(first + s - shift_ref[k], targets)
                if stage is not None:
                    slot ^= first
                weight = jnp.where(at < count, coef_ref[slot, k], 0.0)
                scaled = weight * product[s * rows : (s + 1) * rows]
                if stage is None:
                    sums[0][slot] += scaled
                else:
                    sums[0][slot] += scaled[:, half:]
                    sums[1][slot] += scaled[:, :half]

    if stage is not None:
        for at, g in enumerate(order[stage]):
            part = slice(g * sec_dev, (g + 1) * sec_dev)
            outs[2 * at][...] = sums[0][part]
            outs[2 * at + 1][...] = sums[1][part].astype(jnp.bfloat16)


def summed(shift, coef, mixed, held, order, stage, sums=()):
    k_dev, sec_dev, rows, width = mixed.shape
    targets = coef.shape[0]
    columns = width if stage is None else width // 2
    whole = pltpu.VMEM((targets, rows, columns), jnp.float32)
    out_shape = [whole]
    if stage is not None:
        out_shape = [whole] * 2
        for _ in order[stage]:
            for dtype in (jnp.float32, jnp.bfloat16):
                out_shape.append(pltpu.VMEM((sec_dev, rows, columns), dtype))
    in_vmem = (mixed, held, *sums)
    return pl.pallas_call(
        functools.partial(sum_kernel, order, stage),
        out_shape=out_shape,
        in_specs=[pl.BlockSpec(memory_space=pltpu.SMEM)] * 2
        + [pl.BlockSpec(memory_space=pltpu.VMEM)] * len(in_vmem),
        out_specs=[pl.BlockSpec(memory_space=pltpu.VMEM)] * len(out_shape),
        input_output_aliases={4 + i: i for i in range(len(sums))},
        scratch_shapes=[pltpu.SMEM((k_dev + SUM_TERMS,), jnp.int32)],
        compiler_params=pltpu.CompilerParams(vmem_limit_bytes=24 * MIB),
        cost_estimate=pl.CostEstimate(
            flops=k_dev * sec_dev * rows * width * width,
            bytes_accessed=mixed.size + held.size,
            transcendentals=0,
        ),
    )(
        pltpu.with_memory_space_constraint(shift, pltpu.HBM),
        coef,
        *(pltpu.with_memory_space_constraint(x, pltpu.VMEM) for x in in_vmem),
    )


def swap(value, axis, mask):
    return lax.ppermute(value, axis, [(i, i ^ mask) for i in range(lax.axis_size(axis))])


def after(value, other):
    return lax.optimization_barrier((value, other))[0]


def per_device(wavefunction, left_ops, right_ops, site_coef, coupled, sector_shift):
    sec_dev = wavefunction.shape[0]
    devices = lax.axis_size("sector")
    live = jnp.where(coupled.T > 0, site_coef.T, 0.0)
    split = lax.axis_size("op") == 2 and devices == 4 and sec_dev & (sec_dev - 1) == 0
    mixed, held = mix(wavefunction, left_ops, right_ops, split)

    if split:
        coef = jnp.concatenate([live] + [swap(live, "sector", g) for g in (1, 2, 3)], axis=0)
        order = ((2,), (3, 1, 0))
        *sums, mine_2, theirs_2 = summed(sector_shift, coef, mixed, held, order, 0)
        crossed_2 = swap(theirs_2, "op", 1)
        _, _, mine_3, theirs_3, mine_1, theirs_1, mine_0, theirs_0 = summed(
            sector_shift, after(coef, theirs_2), mixed, held, order, 1, sums
        )
        both_2 = (mine_2 + after(crossed_2, mine_3).astype(jnp.float32)).astype(jnp.bfloat16)
        arrived_2 = swap(both_2, "sector", 2)
        crossed_3 = swap(after(theirs_3, both_2), "op", 1)
        crossed_1 = swap(after(theirs_1, both_2), "op", 1)
        both_3 = (mine_3 + after(crossed_3, both_2).astype(jnp.float32)).astype(jnp.bfloat16)
        arrived_3 = swap(both_3, "sector", 3)
        crossed_0 = swap(after(theirs_0, both_3), "op", 1)
        both_1 = (mine_1 + after(crossed_1, both_3).astype(jnp.float32)).astype(jnp.bfloat16)
        arrived_1 = swap(both_1, "sector", 1)
        sigma = mine_0 + after(crossed_0, both_1).astype(jnp.float32)
        for other in (arrived_2, arrived_3, arrived_1):
            sigma = lax.optimization_barrier(sigma) + other.astype(jnp.float32)
        return sigma

    coef = lax.all_gather(live, "sector", axis=0, tiled=True)
    (total,) = summed(sector_shift, coef, mixed, held, (), None)
    total = lax.psum_scatter(total, "op", scatter_dimension=2, tiled=True)
    return lax.psum_scatter(total, "sector", scatter_dimension=0, tiled=True)


def solution(mesh):
    placed = (
        P(("groups", "sector"), None, None),
        P(("groups", "op"), "rep", None),
        P(("groups", "op"), None, None),
        P(("groups", "op"), "sector"),
        P(("groups", "op"), "sector"),
        P(("groups", "op")),
    )
    return jax.shard_map(
        per_device,
        mesh=mesh,
        in_specs=placed,
        out_specs=P(("groups", "sector"), "rep", "op"),
        check_vma=False,
    )
```

```python
import functools

import jax
import jax.numpy as jnp
from jax import lax
from jax.experimental import pallas as pl
from jax.experimental.pallas import tpu as pltpu
from jax.sharding import PartitionSpec as P

MIX_TERMS = 16
SUM_TERMS = 4
MIB = 1024 * 1024


def wrapped(value, size):
    if size & (size - 1) == 0:
        return value & (size - 1)
    return lax.rem(value + size, size)


def mix_kernel(split, wave_ref, left_ref, right_ref, mixed_ref, held_ref, wave, left, sems):
    sec_dev = wave.shape[0]
    terms, rows, width = left.shape
    chunks = terms // MIX_TERMS

    def left_copy(c):
        part = pl.ds(c * MIX_TERMS, MIX_TERMS)
        return pltpu.make_async_copy(left_ref.at[part], left.at[part], sems.at[3 + c])

    wave_copy = pltpu.make_async_copy(wave_ref, wave, sems.at[0])
    wave_copy.start()
    for c in range(chunks):
        left_copy(c).start()
    if split:
        half = width // 2
        side = lax.axis_index("op")
        mine = pl.multiple_of(side * half, half)
        theirs = pl.multiple_of((1 - side) * half, half)
        right_copies = [
            pltpu.make_async_copy(
                right_ref.at[:, pl.ds(theirs, half)], held_ref.at[:, pl.ds(0, half)], sems.at[1]
            ),
            pltpu.make_async_copy(
                right_ref.at[:, pl.ds(mine, half)], held_ref.at[:, pl.ds(half, half)], sems.at[2]
            ),
        ]
    else:
        right_copies = [pltpu.make_async_copy(right_ref, held_ref, sems.at[1])]
    for copy in right_copies:
        copy.start()
    wave_copy.wait()

    @pl.loop(0, chunks)
    def _(c):
        left_copy(c).wait()
        part = pl.ds(c * MIX_TERMS, MIX_TERMS)
        rows_in = left[part].reshape(MIX_TERMS * rows, width)
        for s in range(sec_dev):
            product = jnp.dot(rows_in, wave[s], preferred_element_type=jnp.float32)
            mixed_ref[part, s] = product.astype(jnp.bfloat16).reshape(MIX_TERMS, rows, width)

    for copy in right_copies:
        copy.wait()


def mix(wavefunction, left_ops, right_ops, split):
    k_dev, rows, width = left_ops.shape
    sec_dev = wavefunction.shape[0]
    return pl.pallas_call(
        functools.partial(mix_kernel, split),
        out_shape=[
            pltpu.VMEM((k_dev, sec_dev, rows, width), jnp.bfloat16),
            pltpu.VMEM(right_ops.shape, jnp.bfloat16),
        ],
        in_specs=[pl.BlockSpec(memory_space=pltpu.HBM)] * 3,
        out_specs=[pl.BlockSpec(memory_space=pltpu.VMEM)] * 2,
        scratch_shapes=[
            pltpu.VMEM(wavefunction.shape, jnp.bfloat16),
            pltpu.VMEM(left_ops.shape, jnp.bfloat16),
            pltpu.SemaphoreType.DMA((3 + k_dev // MIX_TERMS,)),
        ],
        compiler_params=pltpu.CompilerParams(vmem_limit_bytes=24 * MIB),
        cost_estimate=pl.CostEstimate(
            flops=2 * k_dev * sec_dev * rows * width * width,
            bytes_accessed=2 * (left_ops.size + right_ops.size),
            transcendentals=0,
        ),
    )(*(pltpu.with_memory_space_constraint(x, pltpu.HBM) for x in (wavefunction, left_ops, right_ops)))


def reaches(shift, group, sec_dev, targets):
    return wrapped(-shift - group * sec_dev + sec_dev - 1, targets) < 2 * sec_dev - 1


def sum_kernel(order, stage, shift_ref, coef_ref, mixed_ref, held_ref, *refs):
    terms, sec_dev, rows, width = mixed_ref.shape
    targets = coef_ref.shape[0]
    half = width // 2
    picked = refs[-1]
    first = lax.axis_index("sector") * sec_dev

    def pick(k, count):
        picked[count] = k
        if stage is None:
            return count + 1
        wanted = True
        for at, groups in enumerate(order[: stage + 1]):
            if at < stage:
                wanted &= ~reaches(shift_ref[k], groups[0], sec_dev, targets)
            elif at < len(order) - 1:
                wanted &= reaches(shift_ref[k], groups[0], sec_dev, targets)
        return count + jnp.where(wanted, 1, 0)

    count = lax.fori_loop(0, terms, pick, 0)
    for i in range(SUM_TERMS):
        picked[count + i] = 0

    if stage is None:
        sums = refs[:1]
    elif stage == 0:
        sums, outs = refs[:2], refs[2:-1]
    else:
        sums, outs = refs[2:4], refs[4:-1]
    if not stage:
        for total in sums:
            total[...] = jnp.zeros_like(total)

    @pl.loop(0, lax.div(count + SUM_TERMS - 1, SUM_TERMS))
    def _(step):
        for t in range(SUM_TERMS):
            at = step * SUM_TERMS + t
            k = picked[at]
            product = lax.dot_general(
                mixed_ref[k].reshape(sec_dev * rows, width),
                held_ref[k],
                (((1,), (1,)), ((), ())),
                preferred_element_type=jnp.float32,
            )
            for s in range(sec_dev):
                target = wrapped(s - shift_ref[k], targets)
                sector = wrapped(first + s - shift_ref[k], targets)
                weight = jnp.where(at < count, coef_ref[sector, k], 0.0)
                scaled = weight * product[s * rows : (s + 1) * rows]
                if stage is None:
                    sums[0][target] += scaled
                else:
                    sums[0][target] += scaled[:, half:]
                    sums[1][target] += scaled[:, :half]

    if stage is not None:
        for at, g in enumerate(order[stage]):
            part = slice(g * sec_dev, (g + 1) * sec_dev)
            outs[2 * at][...] = sums[0][part]
            outs[2 * at + 1][...] = sums[1][part].astype(jnp.bfloat16)


def summed(shift, coef, mixed, held, order, stage, sums=()):
    k_dev, sec_dev, rows, width = mixed.shape
    targets = coef.shape[0]
    columns = width if stage is None else width // 2
    whole = pltpu.VMEM((targets, rows, columns), jnp.float32)
    out_shape = [whole]
    if stage is not None:
        out_shape = [whole] * 2
        for _ in order[stage]:
            for dtype in (jnp.float32, jnp.bfloat16):
                out_shape.append(pltpu.VMEM((sec_dev, rows, columns), dtype))
    in_vmem = (mixed, held, *sums)
    return pl.pallas_call(
        functools.partial(sum_kernel, order, stage),
        out_shape=out_shape,
        in_specs=[pl.BlockSpec(memory_space=pltpu.SMEM)] * 2
        + [pl.BlockSpec(memory_space=pltpu.VMEM)] * len(in_vmem),
        out_specs=[pl.BlockSpec(memory_space=pltpu.VMEM)] * len(out_shape),
        input_output_aliases={4 + i: i for i in range(len(sums))},
        scratch_shapes=[pltpu.SMEM((k_dev + SUM_TERMS,), jnp.int32)],
        compiler_params=pltpu.CompilerParams(vmem_limit_bytes=24 * MIB),
        cost_estimate=pl.CostEstimate(
            flops=k_dev * sec_dev * rows * width * width,
            bytes_accessed=mixed.size + held.size,
            transcendentals=0,
        ),
    )(
        pltpu.with_memory_space_constraint(shift, pltpu.HBM),
        coef,
        *(pltpu.with_memory_space_constraint(x, pltpu.VMEM) for x in in_vmem),
    )


def shift_by(value, axis, distance):
    size = lax.axis_size(axis)
    return lax.ppermute(value, axis, [(i, (i + distance) % size) for i in range(size)])


def after(value, other):
    return lax.optimization_barrier((value, other))[0]


def per_device(wavefunction, left_ops, right_ops, site_coef, coupled, sector_shift):
    sec_dev = wavefunction.shape[0]
    devices = lax.axis_size("sector")
    live = jnp.where(coupled.T > 0, site_coef.T, 0.0)
    split = lax.axis_size("op") == 2 and devices == 4
    mixed, held = mix(wavefunction, left_ops, right_ops, split)

    if split:
        coef = lax.all_gather(live, "sector", axis=0, tiled=True)
        order = ((2,), (1, 3, 0))
        *sums, mine_2, theirs_2 = summed(sector_shift, coef, mixed, held, order, 0)
        crossed_2 = shift_by(theirs_2, "op", 1)
        _, _, mine_1, theirs_1, mine_3, theirs_3, mine_0, theirs_0 = summed(
            sector_shift, after(coef, theirs_2), mixed, held, order, 1, sums
        )
        both_2 = (mine_2 + after(crossed_2, mine_1).astype(jnp.float32)).astype(jnp.bfloat16)
        arrived_2 = shift_by(both_2, "sector", 2)
        crossed_1 = shift_by(after(theirs_1, both_2), "op", 1)
        crossed_3 = shift_by(after(theirs_3, both_2), "op", 1)
        both_1 = (mine_1 + after(crossed_1, both_2).astype(jnp.float32)).astype(jnp.bfloat16)
        arrived_1 = shift_by(both_1, "sector", 1)
        crossed_0 = shift_by(after(theirs_0, both_1), "op", 1)
        both_3 = (mine_3 + after(crossed_3, both_1).astype(jnp.float32)).astype(jnp.bfloat16)
        arrived_3 = shift_by(both_3, "sector", 3)
        sigma = mine_0 + after(crossed_0, both_3).astype(jnp.float32)
        for other in (arrived_2, arrived_1, arrived_3):
            sigma = lax.optimization_barrier(sigma) + other.astype(jnp.float32)
        return sigma

    first = lax.axis_index("sector") * sec_dev
    coef = lax.all_gather(live, "sector", axis=0, tiled=True)
    (total,) = summed(sector_shift, coef, mixed, held, (), None)
    total = jnp.roll(total, first, axis=0)
    total = lax.psum_scatter(total, "op", scatter_dimension=2, tiled=True)
    return lax.psum_scatter(total, "sector", scatter_dimension=0, tiled=True)


def solution(mesh):
    placed = (
        P(("groups", "sector"), None, None),
        P(("groups", "op"), "rep", None),
        P(("groups", "op"), None, None),
        P(("groups", "op"), "sector"),
        P(("groups", "op"), "sector"),
        P(("groups", "op")),
    )
    return jax.shard_map(
        per_device,
        mesh=mesh,
        in_specs=placed,
        out_specs=P(("groups", "sector"), "rep", "op"),
        check_vma=False,
    )
```

```python
import functools

import jax
import jax.numpy as jnp
from jax import lax
from jax.experimental import pallas as pl
from jax.experimental.pallas import tpu as pltpu
from jax.sharding import PartitionSpec as P

MIX_TERMS = 16
SUM_TERMS = 4
MIB = 1024 * 1024


def wrapped(value, size):
    if size & (size - 1) == 0:
        return value & (size - 1)
    return lax.rem(value + size, size)


def mix_kernel(split, wave_ref, left_ref, right_ref, mixed_ref, held_ref, wave, left, sems):
    sec_dev = wave.shape[0]
    terms, rows, width = left.shape
    chunks = terms // MIX_TERMS

    def left_copy(c):
        part = pl.ds(c * MIX_TERMS, MIX_TERMS)
        return pltpu.make_async_copy(left_ref.at[part], left.at[part], sems.at[3 + c])

    wave_copy = pltpu.make_async_copy(wave_ref, wave, sems.at[0])
    wave_copy.start()
    for c in range(chunks):
        left_copy(c).start()
    if split:
        half = width // 2
        side = lax.axis_index("op")
        mine = pl.multiple_of(side * half, half)
        theirs = pl.multiple_of((1 - side) * half, half)
        right_copies = [
            pltpu.make_async_copy(
                right_ref.at[:, pl.ds(theirs, half)], held_ref.at[:, pl.ds(0, half)], sems.at[1]
            ),
            pltpu.make_async_copy(
                right_ref.at[:, pl.ds(mine, half)], held_ref.at[:, pl.ds(half, half)], sems.at[2]
            ),
        ]
    else:
        right_copies = [pltpu.make_async_copy(right_ref, held_ref, sems.at[1])]
    for copy in right_copies:
        copy.start()
    wave_copy.wait()

    @pl.loop(0, chunks)
    def _(c):
        left_copy(c).wait()
        part = pl.ds(c * MIX_TERMS, MIX_TERMS)
        rows_in = left[part].reshape(MIX_TERMS * rows, width)
        for s in range(sec_dev):
            product = jnp.dot(rows_in, wave[s], preferred_element_type=jnp.float32)
            mixed_ref[part, s] = product.astype(jnp.bfloat16).reshape(MIX_TERMS, rows, width)

    for copy in right_copies:
        copy.wait()


def mix(wavefunction, left_ops, right_ops, split):
    k_dev, rows, width = left_ops.shape
    sec_dev = wavefunction.shape[0]
    return pl.pallas_call(
        functools.partial(mix_kernel, split),
        out_shape=[
            pltpu.VMEM((k_dev, sec_dev, rows, width), jnp.bfloat16),
            pltpu.VMEM(right_ops.shape, jnp.bfloat16),
        ],
        in_specs=[pl.BlockSpec(memory_space=pltpu.HBM)] * 3,
        out_specs=[pl.BlockSpec(memory_space=pltpu.VMEM)] * 2,
        scratch_shapes=[
            pltpu.VMEM(wavefunction.shape, jnp.bfloat16),
            pltpu.VMEM(left_ops.shape, jnp.bfloat16),
            pltpu.SemaphoreType.DMA((3 + k_dev // MIX_TERMS,)),
        ],
        compiler_params=pltpu.CompilerParams(vmem_limit_bytes=24 * MIB),
        cost_estimate=pl.CostEstimate(
            flops=2 * k_dev * sec_dev * rows * width * width,
            bytes_accessed=2 * (left_ops.size + right_ops.size),
            transcendentals=0,
        ),
    )(*(pltpu.with_memory_space_constraint(x, pltpu.HBM) for x in (wavefunction, left_ops, right_ops)))


def sum_kernel(order, stage, shift_ref, coef_ref, mixed_ref, held_ref, *refs):
    terms, sec_dev, rows, width = mixed_ref.shape
    targets = coef_ref.shape[0]
    half = width // 2
    picked = refs[-1]
    first = lax.axis_index("sector") * sec_dev

    def reaches(k, group):
        start = (first ^ (group * sec_dev)) - first
        return wrapped(sec_dev - 1 - start - shift_ref[k], targets) < 2 * sec_dev - 1

    def pick(wanted):
        def body(k, count):
            picked[count] = k
            found = functools.reduce(jnp.logical_or, [reaches(k, group) for group in order[0]])
            return count + jnp.where(found == wanted, 1, 0)

        return body

    if stage is None:
        low, high = 0, terms // SUM_TERMS
    else:
        count = lax.fori_loop(0, terms, pick(True), 0)
        lax.fori_loop(0, terms, pick(False), count)
        steps = lax.div(jnp.maximum(count, terms // 2) + SUM_TERMS - 1, SUM_TERMS)
        low, high = (0, steps) if stage == 0 else (steps, terms // SUM_TERMS)

    if stage is None:
        sums = refs[:1]
    elif stage == 0:
        sums, outs = refs[:2], refs[2:-1]
    else:
        sums, outs = refs[2:4], refs[4:-1]
    if not stage:
        for total in sums:
            total[...] = jnp.zeros_like(total)

    @pl.loop(low, high)
    def _(step):
        for t in range(SUM_TERMS):
            k = step * SUM_TERMS + t
            if stage is not None:
                k = picked[k]
            product = lax.dot_general(
                mixed_ref[k].reshape(sec_dev * rows, width),
                held_ref[k],
                (((1,), (1,)), ((), ())),
                preferred_element_type=jnp.float32,
            )
            for s in range(sec_dev):
                slot = wrapped(first + s - shift_ref[k], targets)
                if stage is not None:
                    slot ^= first
                scaled = coef_ref[slot, k] * product[s * rows : (s + 1) * rows]
                if stage is None:
                    sums[0][slot] += scaled
                else:
                    sums[0][slot] += scaled[:, half:]
                    sums[1][slot] += scaled[:, :half]

    if stage is not None:
        for at, g in enumerate(order[stage]):
            part = slice(g * sec_dev, (g + 1) * sec_dev)
            outs[2 * at][...] = sums[0][part]
            outs[2 * at + 1][...] = sums[1][part].astype(jnp.bfloat16)


def summed(shift, coef, mixed, held, order, stage, sums=()):
    k_dev, sec_dev, rows, width = mixed.shape
    targets = coef.shape[0]
    columns = width if stage is None else width // 2
    whole = pltpu.VMEM((targets, rows, columns), jnp.float32)
    out_shape = [whole]
    if stage is not None:
        out_shape = [whole] * 2
        for _ in order[stage]:
            for dtype in (jnp.float32, jnp.bfloat16):
                out_shape.append(pltpu.VMEM((sec_dev, rows, columns), dtype))
    in_vmem = (mixed, held, *sums)
    return pl.pallas_call(
        functools.partial(sum_kernel, order, stage),
        out_shape=out_shape,
        in_specs=[pl.BlockSpec(memory_space=pltpu.SMEM)] * 2
        + [pl.BlockSpec(memory_space=pltpu.VMEM)] * len(in_vmem),
        out_specs=[pl.BlockSpec(memory_space=pltpu.VMEM)] * len(out_shape),
        input_output_aliases={4 + i: i for i in range(len(sums))},
        scratch_shapes=[pltpu.SMEM((k_dev + SUM_TERMS,), jnp.int32)],
        compiler_params=pltpu.CompilerParams(vmem_limit_bytes=24 * MIB),
        cost_estimate=pl.CostEstimate(
            flops=k_dev * sec_dev * rows * width * width,
            bytes_accessed=mixed.size + held.size,
            transcendentals=0,
        ),
    )(
        pltpu.with_memory_space_constraint(shift, pltpu.HBM),
        coef,
        *(pltpu.with_memory_space_constraint(x, pltpu.VMEM) for x in in_vmem),
    )


def swap(value, axis, mask):
    return lax.ppermute(value, axis, [(i, i ^ mask) for i in range(lax.axis_size(axis))])


def after(value, other):
    return lax.optimization_barrier((value, other))[0]


def per_device(wavefunction, left_ops, right_ops, site_coef, coupled, sector_shift):
    sec_dev = wavefunction.shape[0]
    devices = lax.axis_size("sector")
    live = jnp.where(coupled.T > 0, site_coef.T, 0.0)
    split = lax.axis_size("op") == 2 and devices == 4 and sec_dev & (sec_dev - 1) == 0
    mixed, held = mix(wavefunction, left_ops, right_ops, split)

    if split:
        coef = jnp.concatenate([live] + [swap(live, "sector", g) for g in (1, 2, 3)], axis=0)
        order = ((2,), (3, 1, 0))
        *sums, mine_2, theirs_2 = summed(sector_shift, coef, mixed, held, order, 0)
        crossed_2 = swap(theirs_2, "op", 1)
        _, _, mine_3, theirs_3, mine_1, theirs_1, mine_0, theirs_0 = summed(
            sector_shift, after(coef, theirs_2), mixed, held, order, 1, sums
        )
        both_2 = (mine_2 + after(crossed_2, mine_3).astype(jnp.float32)).astype(jnp.bfloat16)
        arrived_2 = swap(both_2, "sector", 2)
        crossed_3 = swap(after(theirs_3, both_2), "op", 1)
        crossed_1 = swap(after(theirs_1, both_2), "op", 1)
        both_3 = (mine_3 + after(crossed_3, both_2).astype(jnp.float32)).astype(jnp.bfloat16)
        arrived_3 = swap(both_3, "sector", 3)
        crossed_0 = swap(after(theirs_0, both_3), "op", 1)
        both_1 = (mine_1 + after(crossed_1, both_3).astype(jnp.float32)).astype(jnp.bfloat16)
        arrived_1 = swap(both_1, "sector", 1)
        sigma = mine_0 + after(crossed_0, both_1).astype(jnp.float32)
        for other in (arrived_2, arrived_3, arrived_1):
            sigma = lax.optimization_barrier(sigma) + other.astype(jnp.float32)
        return sigma

    coef = lax.all_gather(live, "sector", axis=0, tiled=True)
    (total,) = summed(sector_shift, coef, mixed, held, (), None)
    total = lax.psum_scatter(total, "op", scatter_dimension=2, tiled=True)
    return lax.psum_scatter(total, "sector", scatter_dimension=0, tiled=True)


def solution(mesh):
    placed = (
        P(("groups", "sector"), None, None),
        P(("groups", "op"), "rep", None),
        P(("groups", "op"), None, None),
        P(("groups", "op"), "sector"),
        P(("groups", "op"), "sector"),
        P(("groups", "op")),
    )
    return jax.shard_map(
        per_device,
        mesh=mesh,
        in_specs=placed,
        out_specs=P(("groups", "sector"), "rep", "op"),
        check_vma=False,
    )
```

```python
import functools

import jax
import jax.numpy as jnp
from jax import lax
from jax.experimental import pallas as pl
from jax.experimental.pallas import tpu as pltpu
from jax.sharding import PartitionSpec as P

PAIRS_A_STEP = 8
BLOCKS = 64
MIB = 1024 * 1024


def wrapped(value, size):
    if size & (size - 1) == 0:
        return value & (size - 1)
    return lax.rem(value + size, size)


def divided(value, size):
    if size & (size - 1) == 0:
        return value >> (size.bit_length() - 1)
    return lax.div(value, size)


def list_words(terms, sec_dev):
    return terms * sec_dev + 2 * PAIRS_A_STEP


def load_kernel(split, total_sectors, coef_ref, coupled_ref, shift_ref, wave_ref, left_ref, right_ref, *refs):
    wave, left, right, lists, weights, sems = refs
    terms, width = right.shape[:2]
    sec_dev = coef_ref.shape[0]
    groups = 2 if split else 1
    words = list_words(terms, sec_dev)
    half = width // 2
    first = lax.axis_index("sector") * sec_dev
    copies = [
        pltpu.make_async_copy(wave_ref, wave, sems.at[0]),
        pltpu.make_async_copy(left_ref, left, sems.at[1]),
    ]
    if split:
        op, rep = lax.axis_index("op"), lax.axis_index("rep")
        for at, side in enumerate((1 - op, op)):
            source = right_ref.at[:, pl.ds(pl.multiple_of(side * half, half), half)]
            target = right.at[:, pl.ds(at * half, half)]
            copies.append(pltpu.make_async_copy(source, target, sems.at[2 + at]))
    else:
        copies.append(pltpu.make_async_copy(right_ref, right, sems.at[2]))
    for copy in copies:
        copy.start()

    def add_term(k, counts):
        counts = list(counts)
        for t in range(sec_dev):
            sector = wrapped(first + t + shift_ref[k], total_sectors)
            block, group, at = sector, 0, counts[0]
            if split:
                apart = divided(sector ^ first, sec_dev)
                block = wrapped(sector, sec_dev)
                core, side = (block & 1) ^ rep, (block >> 1) ^ op
                other = core * 4 + side * 2 + apart - 1
                other = jnp.where(apart == 3, 8 + core * 2 + side, other)
                block = jnp.where(apart == 0, block, other)
                group = jnp.where(apart == 0, 0, 1)
                at = jnp.where(apart == 0, at, words + counts[1])
            weight = jnp.where(coupled_ref[t, k] > 0, coef_ref[t, k], 0.0)
            lists[at] = (k * BLOCKS + block) * sec_dev + t
            weights[at] = weight
            live = jnp.where(weight != 0.0, 1, 0)
            for g in range(groups):
                counts[g] = counts[g] + jnp.where(group == g, live, 0)
        return tuple(counts)

    counts = lax.fori_loop(0, terms, add_term, (jnp.int32(0),) * groups)
    for g, count in enumerate(counts):
        lists[(g + 1) * words - 1] = count
        for i in range(PAIRS_A_STEP):
            lists[g * words + count + i] = 0
            weights[g * words + count + i] = 0.0
    for copy in copies:
        copy.wait()


def load(coef, coupled, shift, wave, left, right, total_sectors, split):
    sec_dev, terms = coef.shape
    words = list_words(terms, sec_dev) * (2 if split else 1)
    arrays = (coef, coupled, shift, wave, left, right)
    return pl.pallas_call(
        functools.partial(load_kernel, split, total_sectors),
        out_shape=[pltpu.VMEM(x.shape, x.dtype) for x in (wave, left, right)]
        + [jax.ShapeDtypeStruct((words,), dtype) for dtype in (jnp.int32, jnp.float32)],
        in_specs=[pl.BlockSpec(memory_space=pltpu.SMEM)] * 3
        + [pl.BlockSpec(memory_space=pltpu.HBM)] * 3,
        out_specs=[pl.BlockSpec(memory_space=pltpu.VMEM)] * 3
        + [pl.BlockSpec(memory_space=pltpu.SMEM)] * 2,
        scratch_shapes=[pltpu.SemaphoreType.DMA((4,))],
        compiler_params=pltpu.CompilerParams(vmem_limit_bytes=24 * MIB),
        cost_estimate=pl.CostEstimate(
            flops=0, bytes_accessed=4 * (left.size + right.size), transcendentals=0
        ),
    )(*(pltpu.with_memory_space_constraint(x, pltpu.HBM) for x in arrays))


def group_kernel(group, last, lists_ref, weights_ref, wave_ref, left_ref, right_ref, *refs):
    terms, rows, width = left_ref.shape
    sums = refs[:2] if group == 0 else refs[2:4]
    sec_dev = sums[0].shape[0]
    half = width // 2
    words = list_words(terms, sec_dev)
    if group == 0:
        for total in sums:
            total[...] = jnp.zeros_like(total)
    count = lists_ref[(group + 1) * words - 1]

    @pl.loop(0, lax.div(count + PAIRS_A_STEP - 1, PAIRS_A_STEP))
    def _(step):
        start = group * words + step * PAIRS_A_STEP
        triples = [lists_ref[start + i] for i in range(PAIRS_A_STEP)]
        ks = [divided(triple, BLOCKS * sec_dev) for triple in triples]
        mixed = [
            jnp.dot(
                left_ref[k],
                wave_ref[wrapped(divided(triple, sec_dev), BLOCKS)],
                preferred_element_type=jnp.float32,
            ).astype(jnp.bfloat16)
            for triple, k in zip(triples, ks)
        ]
        for i, (triple, k) in enumerate(zip(triples, ks)):
            product = lax.dot_general(
                mixed[i],
                right_ref[k],
                (((1,), (1,)), ((), ())),
                preferred_element_type=jnp.float32,
            )
            scaled = weights_ref[start + i] * product
            target = wrapped(triple, sec_dev)
            sums[0][target] += scaled[:, :half]
            sums[1][target] += scaled[:, half:]

    if last:
        refs[-1][...] = sums[0][...].astype(refs[-1].dtype)


def group_sum(group, last, sec_dev, lists, weights, wave, left, right, sums=()):
    terms, rows, width = left.shape
    shape = (sec_dev, rows, width // 2)
    out_shape = [pltpu.VMEM(shape, jnp.float32)] * 2
    if last:
        out_shape.append(pltpu.VMEM(shape, last))
    in_vmem = (wave, left, right, *sums)
    return pl.pallas_call(
        functools.partial(group_kernel, group, bool(last)),
        out_shape=out_shape,
        in_specs=[pl.BlockSpec(memory_space=pltpu.SMEM)] * 2
        + [pl.BlockSpec(memory_space=pltpu.VMEM)] * len(in_vmem),
        out_specs=[pl.BlockSpec(memory_space=pltpu.VMEM)] * len(out_shape),
        input_output_aliases={5 + i: i for i in range(len(sums))},
        compiler_params=pltpu.CompilerParams(vmem_limit_bytes=24 * MIB),
        cost_estimate=pl.CostEstimate(
            flops=terms * rows * width * width * 4,
            bytes_accessed=left.size + right.size,
            transcendentals=0,
        ),
    )(lists, weights, *(pltpu.with_memory_space_constraint(x, pltpu.VMEM) for x in in_vmem))


def swap(value, axis, mask):
    return lax.ppermute(value, axis, [(i, i ^ mask) for i in range(lax.axis_size(axis))])


def after(value, other):
    return lax.optimization_barrier((value, other))[0]


def per_device(wavefunction, left_ops, right_ops, site_coef, coupled, sector_shift):
    sec_dev = wavefunction.shape[0]
    devices = lax.axis_size("sector")
    op, rep = lax.axis_index("op"), lax.axis_index("rep")
    tables = (site_coef.T, coupled.T, sector_shift)
    four = lax.axis_size("op") == 2 and lax.axis_size("rep") == 2
    if four and devices == 4 and sec_dev == 4:
        own = lax.dynamic_slice_in_dim(wavefunction, op * 2 + rep, 1, 0)
        got = {g: swap(own, "sector", g) for g in (1, 2, 3)}
        wave, left, right, lists, weights = load(
            *tables, wavefunction, left_ops, right_ops, devices * sec_dev, True
        )

        crossed = {g: swap(got[g], "op", 1) for g in (1, 2, 3)}

        def gathered(groups):
            pieces = jnp.concatenate([x[g] for x in (got, crossed) for g in groups], axis=0)
            return [pieces, swap(pieces, "rep", 1)]

        sums = group_sum(0, None, sec_dev, lists, weights, wave, left, right)
        others = jnp.concatenate(gathered((1, 2)) + gathered((3,)), axis=0)
        _, mine, theirs = group_sum(
            1, jnp.bfloat16, sec_dev, lists, weights, others, left, right, sums
        )
        return mine + swap(theirs, "op", 1).astype(jnp.float32)

    wave = lax.all_gather(wavefunction, "sector", axis=0, tiled=True)
    wave, left, right, lists, weights = load(
        *tables, wave, left_ops, right_ops, devices * sec_dev, False
    )
    sums = group_sum(0, None, sec_dev, lists, weights, wave, left, right)
    total = jnp.concatenate(sums, axis=2)
    return lax.psum_scatter(total, "op", scatter_dimension=2, tiled=True)


def solution(mesh):
    placed = (
        P(("groups", "sector"), None, None),
        P(("groups", "op"), "rep", None),
        P(("groups", "op"), None, None),
        P(("groups", "op"), "sector"),
        P(("groups", "op"), "sector"),
        P(("groups", "op")),
    )
    return jax.shard_map(
        per_device,
        mesh=mesh,
        in_specs=placed,
        out_specs=P(("groups", "sector"), "rep", "op"),
        check_vma=False,
    )
```

```python
import functools

import jax
import jax.numpy as jnp
from jax import lax
from jax.experimental import pallas as pl
from jax.experimental.pallas import tpu as pltpu
from jax.sharding import PartitionSpec as P

MIX_TERMS = 16
SUM_TERMS = 4
MIB = 1024 * 1024


def wrapped(value, size):
    if size & (size - 1) == 0:
        return value & (size - 1)
    return lax.rem(value + size, size)


def mix_kernel(split, wave_ref, left_ref, right_ref, mixed_ref, held_ref, wave, left, sems):
    sec_dev = wave.shape[0]
    terms, rows, width = left.shape
    chunks = terms // MIX_TERMS

    def left_copy(c):
        part = pl.ds(c * MIX_TERMS, MIX_TERMS)
        return pltpu.make_async_copy(left_ref.at[part], left.at[part], sems.at[3 + c])

    wave_copy = pltpu.make_async_copy(wave_ref, wave, sems.at[0])
    wave_copy.start()
    for c in range(chunks):
        left_copy(c).start()
    if split:
        half = width // 2
        side = lax.axis_index("op")
        mine = pl.multiple_of(side * half, half)
        theirs = pl.multiple_of((1 - side) * half, half)
        right_copies = [
            pltpu.make_async_copy(
                right_ref.at[:, pl.ds(theirs, half)], held_ref.at[:, pl.ds(0, half)], sems.at[1]
            ),
            pltpu.make_async_copy(
                right_ref.at[:, pl.ds(mine, half)], held_ref.at[:, pl.ds(half, half)], sems.at[2]
            ),
        ]
    else:
        right_copies = [pltpu.make_async_copy(right_ref, held_ref, sems.at[1])]
    for copy in right_copies:
        copy.start()
    wave_copy.wait()

    @pl.loop(0, chunks)
    def _(c):
        left_copy(c).wait()
        part = pl.ds(c * MIX_TERMS, MIX_TERMS)
        rows_in = left[part].reshape(MIX_TERMS * rows, width)
        for s in range(sec_dev):
            product = jnp.dot(rows_in, wave[s], preferred_element_type=jnp.float32)
            mixed_ref[part, s] = product.astype(jnp.bfloat16).reshape(MIX_TERMS, rows, width)

    for copy in right_copies:
        copy.wait()


def mix(wavefunction, left_ops, right_ops, split):
    k_dev, rows, width = left_ops.shape
    sec_dev = wavefunction.shape[0]
    return pl.pallas_call(
        functools.partial(mix_kernel, split),
        out_shape=[
            pltpu.VMEM((k_dev, sec_dev, rows, width), jnp.bfloat16),
            pltpu.VMEM(right_ops.shape, jnp.bfloat16),
        ],
        in_specs=[pl.BlockSpec(memory_space=pltpu.HBM)] * 3,
        out_specs=[pl.BlockSpec(memory_space=pltpu.VMEM)] * 2,
        scratch_shapes=[
            pltpu.VMEM(wavefunction.shape, jnp.bfloat16),
            pltpu.VMEM(left_ops.shape, jnp.bfloat16),
            pltpu.SemaphoreType.DMA((3 + k_dev // MIX_TERMS,)),
        ],
        compiler_params=pltpu.CompilerParams(vmem_limit_bytes=24 * MIB),
        cost_estimate=pl.CostEstimate(
            flops=2 * k_dev * sec_dev * rows * width * width,
            bytes_accessed=2 * (left_ops.size + right_ops.size),
            transcendentals=0,
        ),
    )(*(pltpu.with_memory_space_constraint(x, pltpu.HBM) for x in (wavefunction, left_ops, right_ops)))


def sum_kernel(order, stage, shift_ref, coef_ref, mixed_ref, held_ref, *refs):
    terms, sec_dev, rows, width = mixed_ref.shape
    targets = coef_ref.shape[0]
    half = width // 2
    picked = refs[-1]
    first = lax.axis_index("sector") * sec_dev

    def reaches(k, group):
        start = (first ^ (group * sec_dev)) - first
        return wrapped(sec_dev - 1 - start - shift_ref[k], targets) < 2 * sec_dev - 1

    def pick(wanted):
        def body(k, count):
            picked[count] = k
            found = functools.reduce(jnp.logical_or, [reaches(k, group) for group in order[0]])
            return count + jnp.where(found == wanted, 1, 0)

        return body

    if stage is None:
        low, high = 0, terms // SUM_TERMS
    else:
        count = lax.fori_loop(0, terms, pick(True), 0)
        lax.fori_loop(0, terms, pick(False), count)
        steps = lax.div(jnp.maximum(count, terms // 2) + SUM_TERMS - 1, SUM_TERMS)
        low, high = (0, steps) if stage == 0 else (steps, terms // SUM_TERMS)

    if stage is None:
        sums = refs[:1]
    elif stage == 0:
        sums, outs = refs[:2], refs[2:-1]
    else:
        sums, outs = refs[2:4], refs[4:-1]
    if not stage:
        for total in sums:
            total[...] = jnp.zeros_like(total)

    @pl.loop(low, high)
    def _(step):
        for t in range(SUM_TERMS):
            k = step * SUM_TERMS + t
            if stage is not None:
                k = picked[k]
            product = lax.dot_general(
                mixed_ref[k].reshape(sec_dev * rows, width),
                held_ref[k],
                (((1,), (1,)), ((), ())),
                preferred_element_type=jnp.float32,
            )
            for s in range(sec_dev):
                slot = wrapped(first + s - shift_ref[k], targets)
                if stage is not None:
                    slot ^= first
                scaled = coef_ref[slot, k] * product[s * rows : (s + 1) * rows]
                if stage is None:
                    sums[0][slot] += scaled
                else:
                    sums[0][slot] += scaled[:, half:]
                    sums[1][slot] += scaled[:, :half]

    if stage is not None:
        for at, g in enumerate(order[stage]):
            part = slice(g * sec_dev, (g + 1) * sec_dev)
            outs[2 * at][...] = sums[0][part]
            outs[2 * at + 1][...] = sums[1][part].astype(jnp.bfloat16)


def summed(shift, coef, mixed, held, order, stage, sums=()):
    k_dev, sec_dev, rows, width = mixed.shape
    targets = coef.shape[0]
    columns = width if stage is None else width // 2
    whole = pltpu.VMEM((targets, rows, columns), jnp.float32)
    out_shape = [whole]
    if stage is not None:
        out_shape = [whole] * 2
        for _ in order[stage]:
            for dtype in (jnp.float32, jnp.bfloat16):
                out_shape.append(pltpu.VMEM((sec_dev, rows, columns), dtype))
    in_vmem = (mixed, held, *sums)
    return pl.pallas_call(
        functools.partial(sum_kernel, order, stage),
        out_shape=out_shape,
        in_specs=[pl.BlockSpec(memory_space=pltpu.SMEM)] * 2
        + [pl.BlockSpec(memory_space=pltpu.VMEM)] * len(in_vmem),
        out_specs=[pl.BlockSpec(memory_space=pltpu.VMEM)] * len(out_shape),
        input_output_aliases={4 + i: i for i in range(len(sums))},
        scratch_shapes=[pltpu.SMEM((k_dev + SUM_TERMS,), jnp.int32)],
        compiler_params=pltpu.CompilerParams(vmem_limit_bytes=24 * MIB),
        cost_estimate=pl.CostEstimate(
            flops=k_dev * sec_dev * rows * width * width,
            bytes_accessed=mixed.size + held.size,
            transcendentals=0,
        ),
    )(
        pltpu.with_memory_space_constraint(shift, pltpu.HBM),
        coef,
        *(pltpu.with_memory_space_constraint(x, pltpu.VMEM) for x in in_vmem),
    )


def swap(value, axis, mask):
    return lax.ppermute(value, axis, [(i, i ^ mask) for i in range(lax.axis_size(axis))])


def after(value, other):
    return lax.optimization_barrier((value, other))[0]


def per_device(wavefunction, left_ops, right_ops, site_coef, coupled, sector_shift):
    sec_dev = wavefunction.shape[0]
    devices = lax.axis_size("sector")
    live = jnp.where(coupled.T > 0, site_coef.T, 0.0)
    split = lax.axis_size("op") == 2 and devices == 4 and sec_dev & (sec_dev - 1) == 0
    mixed, held = mix(wavefunction, left_ops, right_ops, split)

    if split:
        coef = jnp.concatenate([live] + [swap(live, "sector", g) for g in (1, 2, 3)], axis=0)
        order = ((3,), (2, 1, 0))
        *sums, mine_3, theirs_3 = summed(sector_shift, coef, mixed, held, order, 0)
        crossed_3 = swap(theirs_3, "op", 1)
        _, _, mine_2, theirs_2, mine_1, theirs_1, mine_0, theirs_0 = summed(
            sector_shift, after(coef, theirs_3), mixed, held, order, 1, sums
        )
        both_3 = (mine_3 + after(crossed_3, mine_2).astype(jnp.float32)).astype(jnp.bfloat16)
        relayed = swap(both_3, "sector", 1)
        crossed_2 = swap(after(theirs_2, both_3), "op", 1)
        crossed_1 = swap(after(theirs_1, both_3), "op", 1)
        halfway = lax.optimization_barrier(mine_2 + after(crossed_2, both_3).astype(jnp.float32))
        both_2 = (halfway + relayed.astype(jnp.float32)).astype(jnp.bfloat16)
        far = swap(both_2, "sector", 2)
        both_1 = (mine_1 + after(crossed_1, halfway).astype(jnp.float32)).astype(jnp.bfloat16)
        near = swap(both_1, "sector", 1)
        crossed_0 = swap(after(theirs_0, both_2), "op", 1)
        sigma = mine_0 + after(near, both_1).astype(jnp.float32)
        for other in (crossed_0, far):
            sigma = lax.optimization_barrier(sigma) + other.astype(jnp.float32)
        return sigma

    coef = lax.all_gather(live, "sector", axis=0, tiled=True)
    (total,) = summed(sector_shift, coef, mixed, held, (), None)
    total = lax.psum_scatter(total, "op", scatter_dimension=2, tiled=True)
    return lax.psum_scatter(total, "sector", scatter_dimension=0, tiled=True)


def solution(mesh):
    placed = (
        P(("groups", "sector"), None, None),
        P(("groups", "op"), "rep", None),
        P(("groups", "op"), None, None),
        P(("groups", "op"), "sector"),
        P(("groups", "op"), "sector"),
        P(("groups", "op")),
    )
    return jax.shard_map(
        per_device,
        mesh=mesh,
        in_specs=placed,
        out_specs=P(("groups", "sector"), "rep", "op"),
        check_vma=False,
    )
```

```python
import functools

import jax
import jax.numpy as jnp
from jax import lax
from jax.experimental import pallas as pl
from jax.experimental.pallas import tpu as pltpu
from jax.sharding import PartitionSpec as P

MIX_TERMS = 16
SUM_TERMS = 4
MIB = 1024 * 1024


def wrapped(value, size):
    if size & (size - 1) == 0:
        return value & (size - 1)
    return lax.rem(value + size, size)


def divided(value, size):
    if size & (size - 1) == 0:
        return value >> (size.bit_length() - 1)
    return lax.div(value, size)


def mix_kernel(split, group, targets, shift_ref, wave_ref, left_ref, right_ref, *refs):
    mixed_ref, held_ref, plan, wave, left, shifts, sems = refs
    sec_dev = wave.shape[0]
    terms, rows, width = left.shape
    chunks = terms // MIX_TERMS

    def left_copy(c):
        part = pl.ds(c * MIX_TERMS, MIX_TERMS)
        return pltpu.make_async_copy(left_ref.at[part], left.at[part], sems.at[4 + c])

    wave_copy = pltpu.make_async_copy(wave_ref, wave, sems.at[0])
    wave_copy.start()
    shift_copy = pltpu.make_async_copy(shift_ref, shifts, sems.at[3])
    shift_copy.start()
    for c in range(chunks):
        left_copy(c).start()
    if split:
        half = width // 2
        side = lax.axis_index("op")
        mine = pl.multiple_of(side * half, half)
        theirs = pl.multiple_of((1 - side) * half, half)
        right_copies = [
            pltpu.make_async_copy(
                right_ref.at[:, pl.ds(theirs, half)], held_ref.at[:, pl.ds(0, half)], sems.at[1]
            ),
            pltpu.make_async_copy(
                right_ref.at[:, pl.ds(mine, half)], held_ref.at[:, pl.ds(half, half)], sems.at[2]
            ),
        ]
    else:
        right_copies = [pltpu.make_async_copy(right_ref, held_ref, sems.at[1])]
    for copy in right_copies:
        copy.start()

    first = lax.axis_index("sector") * sec_dev
    start = (first ^ (group * sec_dev)) - first
    shift_copy.wait()

    def pick(wanted):
        def body(k, count):
            shift = shifts[k]
            plan[count] = k * targets + shift
            reaches = wrapped(sec_dev - 1 - start - shift, targets) < 2 * sec_dev - 1
            return count + jnp.where(reaches == wanted, 1, 0)

        return body

    count = lax.fori_loop(0, terms, pick(True), 0)
    lax.fori_loop(0, terms, pick(False), count)
    most = jnp.maximum(count, terms // 2)
    plan[terms + 1] = lax.div(most + SUM_TERMS - 1, SUM_TERMS)
    wave_copy.wait()

    @pl.loop(0, chunks)
    def _(c):
        left_copy(c).wait()
        part = pl.ds(c * MIX_TERMS, MIX_TERMS)
        rows_in = left[part].reshape(MIX_TERMS * rows, width)
        for s in range(sec_dev):
            product = jnp.dot(rows_in, wave[s], preferred_element_type=jnp.float32)
            mixed_ref[part, s] = product.astype(jnp.bfloat16).reshape(MIX_TERMS, rows, width)

    for copy in right_copies:
        copy.wait()


def mix(shift, wavefunction, left_ops, right_ops, group, targets, split):
    k_dev, rows, width = left_ops.shape
    sec_dev = wavefunction.shape[0]
    return pl.pallas_call(
        functools.partial(mix_kernel, split, group, targets),
        out_shape=[
            pltpu.VMEM((k_dev, sec_dev, rows, width), jnp.bfloat16),
            pltpu.VMEM(right_ops.shape, jnp.bfloat16),
            jax.ShapeDtypeStruct((k_dev + 2,), jnp.int32),
        ],
        in_specs=[pl.BlockSpec(memory_space=pltpu.HBM)] * 4,
        out_specs=[pl.BlockSpec(memory_space=pltpu.VMEM)] * 2
        + [pl.BlockSpec(memory_space=pltpu.SMEM)],
        scratch_shapes=[
            pltpu.VMEM(wavefunction.shape, jnp.bfloat16),
            pltpu.VMEM(left_ops.shape, jnp.bfloat16),
            pltpu.SMEM(shift.shape, jnp.int32),
            pltpu.SemaphoreType.DMA((4 + k_dev // MIX_TERMS,)),
        ],
        compiler_params=pltpu.CompilerParams(vmem_limit_bytes=24 * MIB),
        cost_estimate=pl.CostEstimate(
            flops=2 * k_dev * sec_dev * rows * width * width,
            bytes_accessed=2 * (left_ops.size + right_ops.size),
            transcendentals=0,
        ),
    )(
        *(
            pltpu.with_memory_space_constraint(x, pltpu.HBM)
            for x in (shift, wavefunction, left_ops, right_ops)
        )
    )


def sum_kernel(order, stage, plan, coef_ref, mixed_ref, held_ref, *refs):
    terms, sec_dev, rows, width = mixed_ref.shape
    targets = coef_ref.shape[0]
    half = width // 2
    first = lax.axis_index("sector") * sec_dev
    low = plan[terms + 1] if stage == 1 else 0
    high = plan[terms + 1] if stage == 0 else terms // SUM_TERMS

    if stage is None:
        sums = refs[:1]
    elif stage == 0:
        sums, outs = refs[:2], refs[2:]
    else:
        sums, outs = refs[2:4], refs[4:]
    if not stage:
        for total in sums:
            total[...] = jnp.zeros_like(total)

    @pl.loop(low, high)
    def _(step):
        for t in range(SUM_TERMS):
            entry = plan[step * SUM_TERMS + t]
            k, shift = divided(entry, targets), wrapped(entry, targets)
            product = lax.dot_general(
                mixed_ref[k].reshape(sec_dev * rows, width),
                held_ref[k],
                (((1,), (1,)), ((), ())),
                preferred_element_type=jnp.float32,
            )
            for s in range(sec_dev):
                slot = wrapped(first + s - shift, targets)
                if stage is not None:
                    slot ^= first
                scaled = coef_ref[slot, k] * product[s * rows : (s + 1) * rows]
                if stage is None:
                    sums[0][slot] += scaled
                else:
                    sums[0][slot] += scaled[:, half:]
                    sums[1][slot] += scaled[:, :half]

    if stage is not None:
        for at, g in enumerate(order[stage]):
            part = slice(g * sec_dev, (g + 1) * sec_dev)
            outs[2 * at][...] = sums[0][part]
            outs[2 * at + 1][...] = sums[1][part].astype(jnp.bfloat16)


def summed(plan, coef, mixed, held, order, stage, sums=()):
    k_dev, sec_dev, rows, width = mixed.shape
    targets = coef.shape[0]
    columns = width if stage is None else width // 2
    whole = pltpu.VMEM((targets, rows, columns), jnp.float32)
    out_shape = [whole]
    if stage is not None:
        out_shape = [whole] * 2
        for _ in order[stage]:
            for dtype in (jnp.float32, jnp.bfloat16):
                out_shape.append(pltpu.VMEM((sec_dev, rows, columns), dtype))
    in_vmem = (mixed, held, *sums)
    return pl.pallas_call(
        functools.partial(sum_kernel, order, stage),
        out_shape=out_shape,
        in_specs=[pl.BlockSpec(memory_space=pltpu.SMEM)] * 2
        + [pl.BlockSpec(memory_space=pltpu.VMEM)] * len(in_vmem),
        out_specs=[pl.BlockSpec(memory_space=pltpu.VMEM)] * len(out_shape),
        input_output_aliases={4 + i: i for i in range(len(sums))},
        compiler_params=pltpu.CompilerParams(vmem_limit_bytes=24 * MIB),
        cost_estimate=pl.CostEstimate(
            flops=k_dev * sec_dev * rows * width * width,
            bytes_accessed=mixed.size + held.size,
            transcendentals=0,
        ),
    )(
        plan,
        coef,
        *(pltpu.with_memory_space_constraint(x, pltpu.VMEM) for x in in_vmem),
    )


def swap(value, axis, mask):
    return lax.ppermute(value, axis, [(i, i ^ mask) for i in range(lax.axis_size(axis))])


def after(value, other):
    return lax.optimization_barrier((value, other))[0]


def per_device(wavefunction, left_ops, right_ops, site_coef, coupled, sector_shift):
    sec_dev = wavefunction.shape[0]
    devices = lax.axis_size("sector")
    live = jnp.where(coupled.T > 0, site_coef.T, 0.0)
    split = lax.axis_size("op") == 2 and devices == 4 and sec_dev & (sec_dev - 1) == 0
    order = ((2,), (3, 1, 0))
    mixed, held, plan = mix(
        sector_shift, wavefunction, left_ops, right_ops, order[0][0], devices * sec_dev, split
    )

    if split:
        coef = jnp.concatenate([live] + [swap(live, "sector", g) for g in (1, 2, 3)], axis=0)
        *sums, mine_2, theirs_2 = summed(plan, coef, mixed, held, order, 0)
        crossed_2 = swap(theirs_2, "op", 1)
        _, _, mine_3, theirs_3, mine_1, theirs_1, mine_0, theirs_0 = summed(
            plan, after(coef, theirs_2), mixed, held, order, 1, sums
        )
        both_2 = (mine_2 + after(crossed_2, mine_3).astype(jnp.float32)).astype(jnp.bfloat16)
        arrived_2 = swap(both_2, "sector", 2)
        crossed_3 = swap(after(theirs_3, both_2), "op", 1)
        crossed_1 = swap(after(theirs_1, both_2), "op", 1)
        both_3 = (mine_3 + after(crossed_3, both_2).astype(jnp.float32)).astype(jnp.bfloat16)
        arrived_3 = swap(both_3, "sector", 3)
        crossed_0 = swap(after(theirs_0, both_3), "op", 1)
        both_1 = (mine_1 + after(crossed_1, both_3).astype(jnp.float32)).astype(jnp.bfloat16)
        arrived_1 = swap(both_1, "sector", 1)
        sigma = mine_0 + after(crossed_0, both_1).astype(jnp.float32)
        for other in (arrived_2, arrived_3, arrived_1):
            sigma = lax.optimization_barrier(sigma) + other.astype(jnp.float32)
        return sigma

    coef = lax.all_gather(live, "sector", axis=0, tiled=True)
    (total,) = summed(plan, coef, mixed, held, (), None)
    total = lax.psum_scatter(total, "op", scatter_dimension=2, tiled=True)
    return lax.psum_scatter(total, "sector", scatter_dimension=0, tiled=True)


def solution(mesh):
    placed = (
        P(("groups", "sector"), None, None),
        P(("groups", "op"), "rep", None),
        P(("groups", "op"), None, None),
        P(("groups", "op"), "sector"),
        P(("groups", "op"), "sector"),
        P(("groups", "op")),
    )
    return jax.shard_map(
        per_device,
        mesh=mesh,
        in_specs=placed,
        out_specs=P(("groups", "sector"), "rep", "op"),
        check_vma=False,
    )
```

```python
import functools

import jax
import jax.numpy as jnp
from jax import lax
from jax.experimental import pallas as pl
from jax.experimental.pallas import tpu as pltpu
from jax.sharding import PartitionSpec as P

MIX_TERMS = 16
SUM_TERMS = 4
MIB = 1024 * 1024


def wrapped(value, size):
    if size & (size - 1) == 0:
        return value & (size - 1)
    return lax.rem(value + size, size)


def mix_kernel(split, wave_ref, left_ref, right_ref, mixed_ref, held_ref, wave, left, sems):
    sec_dev = wave.shape[0]
    terms, rows, width = left.shape
    chunks = terms // MIX_TERMS

    def left_copy(c):
        part = pl.ds(c * MIX_TERMS, MIX_TERMS)
        return pltpu.make_async_copy(left_ref.at[part], left.at[part], sems.at[3 + c])

    wave_copy = pltpu.make_async_copy(wave_ref, wave, sems.at[0])
    wave_copy.start()
    for c in range(chunks):
        left_copy(c).start()
    if split:
        half = width // 2
        side = lax.axis_index("op")
        mine = pl.multiple_of(side * half, half)
        theirs = pl.multiple_of((1 - side) * half, half)
        right_copies = [
            pltpu.make_async_copy(
                right_ref.at[:, pl.ds(theirs, half)], held_ref.at[:, pl.ds(0, half)], sems.at[1]
            ),
            pltpu.make_async_copy(
                right_ref.at[:, pl.ds(mine, half)], held_ref.at[:, pl.ds(half, half)], sems.at[2]
            ),
        ]
    else:
        right_copies = [pltpu.make_async_copy(right_ref, held_ref, sems.at[1])]
    for copy in right_copies:
        copy.start()
    wave_copy.wait()

    @pl.loop(0, chunks)
    def _(c):
        left_copy(c).wait()
        part = pl.ds(c * MIX_TERMS, MIX_TERMS)
        rows_in = left[part].reshape(MIX_TERMS * rows, width)
        for s in range(sec_dev):
            product = jnp.dot(rows_in, wave[s], preferred_element_type=jnp.float32)
            mixed_ref[part, s] = product.astype(jnp.bfloat16).reshape(MIX_TERMS, rows, width)

    for copy in right_copies:
        copy.wait()


def mix(wavefunction, left_ops, right_ops, split):
    k_dev, rows, width = left_ops.shape
    sec_dev = wavefunction.shape[0]
    return pl.pallas_call(
        functools.partial(mix_kernel, split),
        out_shape=[
            pltpu.VMEM((k_dev, sec_dev, rows, width), jnp.bfloat16),
            pltpu.VMEM(right_ops.shape, jnp.bfloat16),
        ],
        in_specs=[pl.BlockSpec(memory_space=pltpu.HBM)] * 3,
        out_specs=[pl.BlockSpec(memory_space=pltpu.VMEM)] * 2,
        scratch_shapes=[
            pltpu.VMEM(wavefunction.shape, jnp.bfloat16),
            pltpu.VMEM(left_ops.shape, jnp.bfloat16),
            pltpu.SemaphoreType.DMA((3 + k_dev // MIX_TERMS,)),
        ],
        compiler_params=pltpu.CompilerParams(vmem_limit_bytes=24 * MIB),
        cost_estimate=pl.CostEstimate(
            flops=2 * k_dev * sec_dev * rows * width * width,
            bytes_accessed=2 * (left_ops.size + right_ops.size),
            transcendentals=0,
        ),
    )(*(pltpu.with_memory_space_constraint(x, pltpu.HBM) for x in (wavefunction, left_ops, right_ops)))


def sum_kernel(order, stage, shift_ref, coef_ref, mixed_ref, held_ref, *refs):
    terms, sec_dev, rows, width = mixed_ref.shape
    targets = coef_ref.shape[0]
    half = width // 2
    picked = refs[-1]
    first = lax.axis_index("sector") * sec_dev

    def reaches(k, group):
        start = (first ^ (group * sec_dev)) - first
        return wrapped(sec_dev - 1 - start - shift_ref[k], targets) < 2 * sec_dev - 1

    def pick(wanted):
        def body(k, count):
            picked[count] = k
            found = functools.reduce(jnp.logical_or, [reaches(k, group) for group in order[0]])
            return count + jnp.where(found == wanted, 1, 0)

        return body

    if stage is None:
        low, high = 0, terms // SUM_TERMS
    else:
        count = lax.fori_loop(0, terms, pick(True), 0)
        lax.fori_loop(0, terms, pick(False), count)
        steps = lax.div(jnp.maximum(count, terms // 2) + SUM_TERMS - 1, SUM_TERMS)
        low, high = (0, steps) if stage == 0 else (steps, terms // SUM_TERMS)

    if stage is None:
        sums = refs[:1]
    elif stage == 0:
        sums, outs = refs[:2], refs[2:-1]
    else:
        sums, outs = refs[2:4], refs[4:-1]
    if not stage:
        for total in sums:
            total[...] = jnp.zeros_like(total)

    @pl.loop(low, high)
    def _(step):
        for t in range(SUM_TERMS):
            k = step * SUM_TERMS + t
            if stage is not None:
                k = picked[k]
            product = lax.dot_general(
                mixed_ref[k].reshape(sec_dev * rows, width),
                held_ref[k],
                (((1,), (1,)), ((), ())),
                preferred_element_type=jnp.float32,
            )
            for s in range(sec_dev):
                slot = wrapped(first + s - shift_ref[k], targets)
                if stage is not None:
                    slot ^= first
                scaled = coef_ref[slot, k] * product[s * rows : (s + 1) * rows]
                if stage is None:
                    sums[0][slot] += scaled
                else:
                    sums[0][slot] += scaled[:, half:]
                    sums[1][slot] += scaled[:, :half]

    if stage is not None:
        for at, g in enumerate(order[stage]):
            part = slice(g * sec_dev, (g + 1) * sec_dev)
            outs[2 * at][...] = sums[0][part]
            outs[2 * at + 1][...] = sums[1][part].astype(jnp.bfloat16)


def summed(shift, coef, mixed, held, order, stage, sums=()):
    k_dev, sec_dev, rows, width = mixed.shape
    targets = coef.shape[0]
    columns = width if stage is None else width // 2
    whole = pltpu.VMEM((targets, rows, columns), jnp.float32)
    out_shape = [whole]
    if stage is not None:
        out_shape = [whole] * 2
        for _ in order[stage]:
            for dtype in (jnp.float32, jnp.bfloat16):
                out_shape.append(pltpu.VMEM((sec_dev, rows, columns), dtype))
    in_vmem = (mixed, held, *sums)
    return pl.pallas_call(
        functools.partial(sum_kernel, order, stage),
        out_shape=out_shape,
        in_specs=[pl.BlockSpec(memory_space=pltpu.SMEM)] * 2
        + [pl.BlockSpec(memory_space=pltpu.VMEM)] * len(in_vmem),
        out_specs=[pl.BlockSpec(memory_space=pltpu.VMEM)] * len(out_shape),
        input_output_aliases={4 + i: i for i in range(len(sums))},
        scratch_shapes=[pltpu.SMEM((k_dev + SUM_TERMS,), jnp.int32)],
        compiler_params=pltpu.CompilerParams(vmem_limit_bytes=24 * MIB),
        cost_estimate=pl.CostEstimate(
            flops=k_dev * sec_dev * rows * width * width,
            bytes_accessed=mixed.size + held.size,
            transcendentals=0,
        ),
    )(
        pltpu.with_memory_space_constraint(shift, pltpu.HBM),
        coef,
        *(pltpu.with_memory_space_constraint(x, pltpu.VMEM) for x in in_vmem),
    )


def swap(value, axis, mask):
    return lax.ppermute(value, axis, [(i, i ^ mask) for i in range(lax.axis_size(axis))])


def after(value, other):
    return lax.optimization_barrier((value, other))[0]


def per_device(wavefunction, left_ops, right_ops, site_coef, coupled, sector_shift):
    sec_dev = wavefunction.shape[0]
    devices = lax.axis_size("sector")
    live = jnp.where(coupled.T > 0, site_coef.T, 0.0)
    split = lax.axis_size("op") == 2 and devices == 4 and sec_dev & (sec_dev - 1) == 0
    mixed, held = mix(wavefunction, left_ops, right_ops, split)

    if split:
        coef = jnp.concatenate([live] + [swap(live, "sector", g) for g in (1, 2, 3)], axis=0)
        order = ((2,), (3, 1, 0))
        *sums, mine_2, theirs_2 = summed(sector_shift, coef, mixed, held, order, 0)
        crossed_2 = swap(theirs_2, "op", 1)
        _, _, mine_3, theirs_3, mine_1, theirs_1, mine_0, theirs_0 = summed(
            sector_shift, after(coef, theirs_2), mixed, held, order, 1, sums
        )
        crossed_3 = swap(theirs_3, "op", 1)
        both_2 = (mine_2 + after(crossed_2, mine_3).astype(jnp.float32)).astype(jnp.bfloat16)
        arrived_2 = swap(both_2, "sector", 2)
        crossed_1 = swap(after(theirs_1, both_2), "op", 1)
        both_3 = (mine_3 + after(crossed_3, both_2).astype(jnp.float32)).astype(jnp.bfloat16)
        arrived_3 = swap(both_3, "sector", 3)
        crossed_0 = swap(after(theirs_0, both_3), "op", 1)
        both_1 = (mine_1 + after(crossed_1, both_3).astype(jnp.float32)).astype(jnp.bfloat16)
        arrived_1 = swap(both_1, "sector", 1)
        sigma = mine_0 + after(arrived_2, both_1).astype(jnp.float32)
        for other in (crossed_0, arrived_3, arrived_1):
            sigma = lax.optimization_barrier(sigma) + other.astype(jnp.float32)
        return sigma

    coef = lax.all_gather(live, "sector", axis=0, tiled=True)
    (total,) = summed(sector_shift, coef, mixed, held, (), None)
    total = lax.psum_scatter(total, "op", scatter_dimension=2, tiled=True)
    return lax.psum_scatter(total, "sector", scatter_dimension=0, tiled=True)


def solution(mesh):
    placed = (
        P(("groups", "sector"), None, None),
        P(("groups", "op"), "rep", None),
        P(("groups", "op"), None, None),
        P(("groups", "op"), "sector"),
        P(("groups", "op"), "sector"),
        P(("groups", "op")),
    )
    return jax.shard_map(
        per_device,
        mesh=mesh,
        in_specs=placed,
        out_specs=P(("groups", "sector"), "rep", "op"),
        check_vma=False,
    )
```

```python
import functools

import jax
import jax.numpy as jnp
from jax import lax
from jax.experimental import pallas as pl
from jax.experimental.pallas import tpu as pltpu
from jax.sharding import PartitionSpec as P

PAIRS_A_STEP = 8
BLOCKS = 64
MIB = 1024 * 1024


def wrapped(value, size):
    if size & (size - 1) == 0:
        return value & (size - 1)
    return lax.rem(value + size, size)


def divided(value, size):
    if size & (size - 1) == 0:
        return value >> (size.bit_length() - 1)
    return lax.div(value, size)


def list_words(terms, sec_dev):
    return terms * sec_dev + 2 * PAIRS_A_STEP


def add_pairs(group, lists, weights, wave, left, right, sums):
    half = right.shape[1] // 2
    sec_dev = sums[0].shape[0]
    words = list_words(left.shape[0], sec_dev)
    count = lists[(group + 1) * words - 1]

    @pl.loop(0, lax.div(count + PAIRS_A_STEP - 1, PAIRS_A_STEP))
    def _(step):
        start = group * words + step * PAIRS_A_STEP
        triples = [lists[start + i] for i in range(PAIRS_A_STEP)]
        ks = [divided(triple, BLOCKS * sec_dev) for triple in triples]
        mixed = [
            jnp.dot(
                left[k],
                wave[wrapped(divided(triple, sec_dev), BLOCKS)],
                preferred_element_type=jnp.float32,
            ).astype(jnp.bfloat16)
            for triple, k in zip(triples, ks)
        ]
        for i, (triple, k) in enumerate(zip(triples, ks)):
            product = lax.dot_general(
                mixed[i], right[k], (((1,), (1,)), ((), ())), preferred_element_type=jnp.float32
            )
            scaled = weights[start + i] * product
            target = wrapped(triple, sec_dev)
            sums[0][target] += scaled[:, :half]
            sums[1][target] += scaled[:, half:]


def own_kernel(split, total_sectors, coef_ref, coupled_ref, shift_ref, wave_ref, left_ref, right_ref, *refs):
    left, right, lists, weights, *sums = refs[:6]
    wave, sems = refs[6:]
    terms, width = right.shape[:2]
    sec_dev = coef_ref.shape[0]
    groups = 3 if split else 1
    words = list_words(terms, sec_dev)
    half = width // 2
    first = lax.axis_index("sector") * sec_dev
    copies = [
        pltpu.make_async_copy(wave_ref, wave, sems.at[0]),
        pltpu.make_async_copy(left_ref, left, sems.at[1]),
    ]
    if split:
        op, rep = lax.axis_index("op"), lax.axis_index("rep")
        for at, side in enumerate((1 - op, op)):
            source = right_ref.at[:, pl.ds(pl.multiple_of(side * half, half), half)]
            target = right.at[:, pl.ds(at * half, half)]
            copies.append(pltpu.make_async_copy(source, target, sems.at[2 + at]))
    else:
        copies.append(pltpu.make_async_copy(right_ref, right, sems.at[2]))
    for copy in copies:
        copy.start()
    for total in sums:
        total[...] = jnp.zeros_like(total)

    def add_term(k, counts):
        counts = list(counts)
        for t in range(sec_dev):
            block = wrapped(first + t + shift_ref[k], total_sectors)
            group, at = 0, counts[0]
            if split:
                apart = divided(block ^ first, sec_dev)
                block = wrapped(block, sec_dev)
                core, side = (block & 1) ^ rep, (block >> 1) ^ op
                group = jnp.where(apart == 0, 0, jnp.where(apart == 3, 2, 1))
                other = core * 2 + side
                other = jnp.where(apart == 3, other, other * 2 + apart - 1)
                block = jnp.where(apart == 0, block, other)
                at = jnp.where(apart == 0, at, jnp.where(apart == 3, counts[2], counts[1]))
                at = at + group * words
            weight = jnp.where(coupled_ref[t, k] > 0, coef_ref[t, k], 0.0)
            lists[at] = (k * BLOCKS + block) * sec_dev + t
            weights[at] = weight
            live = jnp.where(weight != 0.0, 1, 0)
            for g in range(groups):
                counts[g] = counts[g] + jnp.where(group == g, live, 0)
        return tuple(counts)

    counts = lax.fori_loop(0, terms, add_term, (jnp.int32(0),) * groups)
    for g, count in enumerate(counts):
        lists[(g + 1) * words - 1] = count
        for i in range(PAIRS_A_STEP):
            lists[g * words + count + i] = 0
            weights[g * words + count + i] = 0.0
    for copy in copies:
        copy.wait()
    add_pairs(0, lists, weights, wave, left, right, sums)


def own_sum(coef, coupled, shift, wave, left, right, total_sectors, split):
    sec_dev, terms = coef.shape
    words = list_words(terms, sec_dev) * (3 if split else 1)
    arrays = (coef, coupled, shift, wave, left, right)
    sums = pltpu.VMEM((sec_dev, left.shape[1], left.shape[2] // 2), jnp.float32)
    return pl.pallas_call(
        functools.partial(own_kernel, split, total_sectors),
        out_shape=[pltpu.VMEM(x.shape, x.dtype) for x in (left, right)]
        + [jax.ShapeDtypeStruct((words,), dtype) for dtype in (jnp.int32, jnp.float32)]
        + [sums] * 2,
        in_specs=[pl.BlockSpec(memory_space=pltpu.SMEM)] * 3
        + [pl.BlockSpec(memory_space=pltpu.HBM)] * 3,
        out_specs=[pl.BlockSpec(memory_space=pltpu.VMEM)] * 2
        + [pl.BlockSpec(memory_space=pltpu.SMEM)] * 2
        + [pl.BlockSpec(memory_space=pltpu.VMEM)] * 2,
        scratch_shapes=[pltpu.VMEM(wave.shape, wave.dtype), pltpu.SemaphoreType.DMA((4,))],
        compiler_params=pltpu.CompilerParams(vmem_limit_bytes=32 * MIB),
        cost_estimate=pl.CostEstimate(
            flops=terms * left.shape[1] * left.shape[2] ** 2 * 8,
            bytes_accessed=4 * (left.size + right.size),
            transcendentals=0,
        ),
    )(*(pltpu.with_memory_space_constraint(x, pltpu.HBM) for x in arrays))


def group_kernel(group, last, lists_ref, weights_ref, wave_ref, left_ref, right_ref, *refs):
    sums = refs[2:4]
    add_pairs(group, lists_ref, weights_ref, wave_ref, left_ref, right_ref, sums)
    if last:
        refs[-1][...] = sums[0][...].astype(refs[-1].dtype)


def group_sum(group, last, lists, weights, wave, left, right, sums):
    terms, rows, width = left.shape
    out_shape = [pltpu.VMEM(x.shape, x.dtype) for x in sums]
    if last:
        out_shape.append(pltpu.VMEM(sums[0].shape, jnp.bfloat16))
    in_vmem = (wave, left, right, *sums)
    return pl.pallas_call(
        functools.partial(group_kernel, group, last),
        out_shape=out_shape,
        in_specs=[pl.BlockSpec(memory_space=pltpu.SMEM)] * 2
        + [pl.BlockSpec(memory_space=pltpu.VMEM)] * len(in_vmem),
        out_specs=[pl.BlockSpec(memory_space=pltpu.VMEM)] * len(out_shape),
        input_output_aliases={5 + i: i for i in range(len(sums))},
        compiler_params=pltpu.CompilerParams(vmem_limit_bytes=24 * MIB),
        cost_estimate=pl.CostEstimate(
            flops=terms * rows * width * width * 4,
            bytes_accessed=left.size + right.size,
            transcendentals=0,
        ),
    )(lists, weights, *(pltpu.with_memory_space_constraint(x, pltpu.VMEM) for x in in_vmem))


def swap(value, axis, mask):
    return lax.ppermute(value, axis, [(i, i ^ mask) for i in range(lax.axis_size(axis))])


def after(value, other):
    return lax.optimization_barrier((value, other))[0]


def per_device(wavefunction, left_ops, right_ops, site_coef, coupled, sector_shift):
    sec_dev = wavefunction.shape[0]
    devices = lax.axis_size("sector")
    op, rep = lax.axis_index("op"), lax.axis_index("rep")
    tables = (site_coef.T, coupled.T, sector_shift)
    four = lax.axis_size("op") == 2 and lax.axis_size("rep") == 2
    if four and devices == 4 and sec_dev == 4:
        own = lax.dynamic_slice_in_dim(wavefunction, op * 2 + rep, 1, 0)
        got = {g: swap(own, "sector", g) for g in (1, 2, 3)}
        left, right, lists, weights, *sums = own_sum(
            *tables, wavefunction, left_ops, right_ops, devices * sec_dev, True
        )
        crossed = {g: swap(after(got[g], sums[0]), "op", 1) for g in (1, 2, 3)}

        def pieces(groups):
            return jnp.concatenate([x[g] for x in (got, crossed) for g in groups], axis=0)

        near, far = pieces((1, 2)), pieces((3,))
        beside = swap(far, "rep", 1)
        others = jnp.concatenate([near, swap(near, "rep", 1)], axis=0)
        sums = group_sum(1, False, lists, weights, others, left, right, sums)
        others = jnp.concatenate([far, after(beside, sums[0])], axis=0)
        _, mine, theirs = group_sum(2, True, lists, weights, others, left, right, sums)
        return mine + swap(theirs, "op", 1).astype(jnp.float32)

    wave = lax.all_gather(wavefunction, "sector", axis=0, tiled=True)
    *_, theirs, mine = own_sum(*tables, wave, left_ops, right_ops, devices * sec_dev, False)
    total = jnp.concatenate([theirs, mine], axis=2)
    return lax.psum_scatter(total, "op", scatter_dimension=2, tiled=True)


def solution(mesh):
    placed = (
        P(("groups", "sector"), None, None),
        P(("groups", "op"), "rep", None),
        P(("groups", "op"), None, None),
        P(("groups", "op"), "sector"),
        P(("groups", "op"), "sector"),
        P(("groups", "op")),
    )
    return jax.shard_map(
        per_device,
        mesh=mesh,
        in_specs=placed,
        out_specs=P(("groups", "sector"), "rep", "op"),
        check_vma=False,
    )
```

```python
import functools

import jax
import jax.numpy as jnp
from jax import lax
from jax.experimental import pallas as pl
from jax.experimental.pallas import tpu as pltpu
from jax.sharding import PartitionSpec as P

PAIRS_A_STEP = 8
BLOCKS = 64
MIB = 1024 * 1024


def wrapped(value, size):
    if size & (size - 1) == 0:
        return value & (size - 1)
    return lax.rem(value + size, size)


def divided(value, size):
    if size & (size - 1) == 0:
        return value >> (size.bit_length() - 1)
    return lax.div(value, size)


def list_words(terms, sec_dev):
    return terms * sec_dev + 2 * PAIRS_A_STEP


def add_pairs(group, lists, weights, wave, left, right, sums):
    half = right.shape[1] // 2
    sec_dev = sums[0].shape[0]
    words = list_words(left.shape[0], sec_dev)
    count = lists[(group + 1) * words - 1]

    @pl.loop(0, lax.div(count + PAIRS_A_STEP - 1, PAIRS_A_STEP))
    def _(step):
        start = group * words + step * PAIRS_A_STEP
        triples = [lists[start + i] for i in range(PAIRS_A_STEP)]
        ks = [divided(triple, BLOCKS * sec_dev) for triple in triples]
        mixed = [
            jnp.dot(
                left[k],
                wave[wrapped(divided(triple, sec_dev), BLOCKS)],
                preferred_element_type=jnp.float32,
            ).astype(jnp.bfloat16)
            for triple, k in zip(triples, ks)
        ]
        for i, (triple, k) in enumerate(zip(triples, ks)):
            product = lax.dot_general(
                mixed[i], right[k], (((1,), (1,)), ((), ())), preferred_element_type=jnp.float32
            )
            scaled = weights[start + i] * product
            target = wrapped(triple, sec_dev)
            sums[0][target] += scaled[:, :half]
            sums[1][target] += scaled[:, half:]


def load_kernel(split, total_sectors, coef_ref, coupled_ref, shift_ref, wave_ref, left_ref, right_ref, *refs):
    wave, left, right, lists, weights, sems = refs
    terms, width = right.shape[:2]
    sec_dev = coef_ref.shape[0]
    groups = 3 if split else 1
    words = list_words(terms, sec_dev)
    half = width // 2
    first = lax.axis_index("sector") * sec_dev
    copies = [
        pltpu.make_async_copy(wave_ref, wave, sems.at[0]),
        pltpu.make_async_copy(left_ref, left, sems.at[1]),
    ]
    if split:
        op, rep = lax.axis_index("op"), lax.axis_index("rep")
        for at, side in enumerate((1 - op, op)):
            source = right_ref.at[:, pl.ds(pl.multiple_of(side * half, half), half)]
            target = right.at[:, pl.ds(at * half, half)]
            copies.append(pltpu.make_async_copy(source, target, sems.at[2 + at]))
    else:
        copies.append(pltpu.make_async_copy(right_ref, right, sems.at[2]))
    for copy in copies:
        copy.start()

    def add_term(k, counts):
        counts = list(counts)
        for t in range(sec_dev):
            block = wrapped(first + t + shift_ref[k], total_sectors)
            group, at = 0, counts[0]
            if split:
                apart = divided(block ^ first, sec_dev)
                block = wrapped(block, sec_dev)
                core, side = (block & 1) ^ rep, (block >> 1) ^ op
                group = jnp.where(apart == 0, 0, jnp.where(apart == 3, 2, 1))
                other = core * 2 + side
                other = jnp.where(apart == 3, other, other * 2 + apart - 1)
                block = jnp.where(apart == 0, block, other)
                at = jnp.where(apart == 0, at, jnp.where(apart == 3, counts[2], counts[1]))
                at = at + group * words
            weight = jnp.where(coupled_ref[t, k] > 0, coef_ref[t, k], 0.0)
            lists[at] = (k * BLOCKS + block) * sec_dev + t
            weights[at] = weight
            live = jnp.where(weight != 0.0, 1, 0)
            for g in range(groups):
                counts[g] = counts[g] + jnp.where(group == g, live, 0)
        return tuple(counts)

    counts = lax.fori_loop(0, terms, add_term, (jnp.int32(0),) * groups)
    for g, count in enumerate(counts):
        lists[(g + 1) * words - 1] = count
        for i in range(PAIRS_A_STEP):
            lists[g * words + count + i] = 0
            weights[g * words + count + i] = 0.0
    for copy in copies:
        copy.wait()


def load(coef, coupled, shift, wave, left, right, total_sectors, split):
    sec_dev, terms = coef.shape
    words = list_words(terms, sec_dev) * (3 if split else 1)
    arrays = (coef, coupled, shift, wave, left, right)
    return pl.pallas_call(
        functools.partial(load_kernel, split, total_sectors),
        out_shape=[pltpu.VMEM(x.shape, x.dtype) for x in (wave, left, right)]
        + [jax.ShapeDtypeStruct((words,), dtype) for dtype in (jnp.int32, jnp.float32)],
        in_specs=[pl.BlockSpec(memory_space=pltpu.SMEM)] * 3
        + [pl.BlockSpec(memory_space=pltpu.HBM)] * 3,
        out_specs=[pl.BlockSpec(memory_space=pltpu.VMEM)] * 3
        + [pl.BlockSpec(memory_space=pltpu.SMEM)] * 2,
        scratch_shapes=[pltpu.SemaphoreType.DMA((4,))],
        compiler_params=pltpu.CompilerParams(vmem_limit_bytes=32 * MIB),
        cost_estimate=pl.CostEstimate(
            flops=0,
            bytes_accessed=4 * (left.size + right.size),
            transcendentals=0,
        ),
    )(*(pltpu.with_memory_space_constraint(x, pltpu.HBM) for x in arrays))


def group_kernel(group, last, lists_ref, weights_ref, wave_ref, left_ref, right_ref, *refs):
    sums = refs[2:4] if group else refs[:2]
    if not group:
        for total in sums:
            total[...] = jnp.zeros_like(total)
    add_pairs(group, lists_ref, weights_ref, wave_ref, left_ref, right_ref, sums)
    if last:
        refs[-1][...] = sums[0][...].astype(refs[-1].dtype)


def group_sum(group, last, sec_dev, lists, weights, wave, left, right, sums=()):
    terms, rows, width = left.shape
    shape = (sec_dev, rows, width // 2)
    out_shape = [pltpu.VMEM(shape, jnp.float32)] * 2
    if last:
        out_shape.append(pltpu.VMEM(shape, jnp.bfloat16))
    in_vmem = (wave, left, right, *sums)
    return pl.pallas_call(
        functools.partial(group_kernel, group, last),
        out_shape=out_shape,
        in_specs=[pl.BlockSpec(memory_space=pltpu.SMEM)] * 2
        + [pl.BlockSpec(memory_space=pltpu.VMEM)] * len(in_vmem),
        out_specs=[pl.BlockSpec(memory_space=pltpu.VMEM)] * len(out_shape),
        input_output_aliases={5 + i: i for i in range(len(sums))},
        compiler_params=pltpu.CompilerParams(vmem_limit_bytes=24 * MIB),
        cost_estimate=pl.CostEstimate(
            flops=terms * rows * width * width * 4,
            bytes_accessed=left.size + right.size,
            transcendentals=0,
        ),
    )(lists, weights, *(pltpu.with_memory_space_constraint(x, pltpu.VMEM) for x in in_vmem))


def swap(value, axis, mask):
    return lax.ppermute(value, axis, [(i, i ^ mask) for i in range(lax.axis_size(axis))])


def after(value, other):
    return lax.optimization_barrier((value, other))[0]


def per_device(wavefunction, left_ops, right_ops, site_coef, coupled, sector_shift):
    sec_dev = wavefunction.shape[0]
    devices = lax.axis_size("sector")
    op, rep = lax.axis_index("op"), lax.axis_index("rep")
    tables = (site_coef.T, coupled.T, sector_shift)
    four = lax.axis_size("op") == 2 and lax.axis_size("rep") == 2
    if four and devices == 4 and sec_dev == 4:
        own = lax.dynamic_slice_in_dim(wavefunction, op * 2 + rep, 1, 0)
        got = {g: swap(own, "sector", g) for g in (1, 2, 3)}
        wave, left, right, lists, weights = load(
            *tables, wavefunction, left_ops, right_ops, devices * sec_dev, True
        )
        crossed = {g: swap(after(got[g], lists), "op", 1) for g in (1, 2, 3)}
        held = after(lists, (got[1], got[2], got[3]))
        sums = group_sum(0, False, sec_dev, held, weights, wave, left, right)

        def pieces(groups):
            return jnp.concatenate([x[g] for x in (got, crossed) for g in groups], axis=0)

        crossed[1] = after(crossed[1], sums[0])
        near, far = pieces((1, 2)), pieces((3,))
        beside = swap(far, "rep", 1)
        others = jnp.concatenate([near, swap(near, "rep", 1)], axis=0)
        sums = group_sum(1, False, sec_dev, lists, weights, others, left, right, sums)
        others = jnp.concatenate([far, after(beside, sums[0])], axis=0)
        _, mine, theirs = group_sum(
            2, True, sec_dev, lists, weights, others, left, right, sums
        )
        return mine + swap(theirs, "op", 1).astype(jnp.float32)

    wave = lax.all_gather(wavefunction, "sector", axis=0, tiled=True)
    wave, left, right, lists, weights = load(
        *tables, wave, left_ops, right_ops, devices * sec_dev, False
    )
    sums = group_sum(0, False, sec_dev, lists, weights, wave, left, right)
    total = jnp.concatenate(sums, axis=2)
    return lax.psum_scatter(total, "op", scatter_dimension=2, tiled=True)


def solution(mesh):
    placed = (
        P(("groups", "sector"), None, None),
        P(("groups", "op"), "rep", None),
        P(("groups", "op"), None, None),
        P(("groups", "op"), "sector"),
        P(("groups", "op"), "sector"),
        P(("groups", "op")),
    )
    return jax.shard_map(
        per_device,
        mesh=mesh,
        in_specs=placed,
        out_specs=P(("groups", "sector"), "rep", "op"),
        check_vma=False,
    )
```

```python
import functools

import jax
import jax.numpy as jnp
from jax import lax
from jax.experimental import pallas as pl
from jax.experimental.pallas import tpu as pltpu
from jax.sharding import PartitionSpec as P

MIX_TERMS = 16
SUM_TERMS = 4
MIB = 1024 * 1024


def wrapped(value, size):
    if size & (size - 1) == 0:
        return value & (size - 1)
    return lax.rem(value + size, size)


def mix_kernel(split, wave_ref, left_ref, right_ref, mixed_ref, held_ref, wave, left, sems):
    sec_dev = wave.shape[0]
    terms, rows, width = left.shape
    chunks = terms // MIX_TERMS

    def left_copy(c):
        part = pl.ds(c * MIX_TERMS, MIX_TERMS)
        return pltpu.make_async_copy(left_ref.at[part], left.at[part], sems.at[3 + c])

    wave_copy = pltpu.make_async_copy(wave_ref, wave, sems.at[0])
    wave_copy.start()
    for c in range(chunks):
        left_copy(c).start()
    if split:
        half = width // 2
        side = lax.axis_index("op")
        mine = pl.multiple_of(side * half, half)
        theirs = pl.multiple_of((1 - side) * half, half)
        right_copies = [
            pltpu.make_async_copy(
                right_ref.at[:, pl.ds(theirs, half)], held_ref.at[:, pl.ds(0, half)], sems.at[1]
            ),
            pltpu.make_async_copy(
                right_ref.at[:, pl.ds(mine, half)], held_ref.at[:, pl.ds(half, half)], sems.at[2]
            ),
        ]
    else:
        right_copies = [pltpu.make_async_copy(right_ref, held_ref, sems.at[1])]
    for copy in right_copies:
        copy.start()
    wave_copy.wait()

    @pl.loop(0, chunks)
    def _(c):
        left_copy(c).wait()
        part = pl.ds(c * MIX_TERMS, MIX_TERMS)
        rows_in = left[part].reshape(MIX_TERMS * rows, width)
        for s in range(sec_dev):
            product = jnp.dot(rows_in, wave[s], preferred_element_type=jnp.float32)
            mixed_ref[part, s] = product.astype(jnp.bfloat16).reshape(MIX_TERMS, rows, width)

    for copy in right_copies:
        copy.wait()


def mix(wavefunction, left_ops, right_ops, split):
    k_dev, rows, width = left_ops.shape
    sec_dev = wavefunction.shape[0]
    return pl.pallas_call(
        functools.partial(mix_kernel, split),
        out_shape=[
            pltpu.VMEM((k_dev, sec_dev, rows, width), jnp.bfloat16),
            pltpu.VMEM(right_ops.shape, jnp.bfloat16),
        ],
        in_specs=[pl.BlockSpec(memory_space=pltpu.HBM)] * 3,
        out_specs=[pl.BlockSpec(memory_space=pltpu.VMEM)] * 2,
        scratch_shapes=[
            pltpu.VMEM(wavefunction.shape, jnp.bfloat16),
            pltpu.VMEM(left_ops.shape, jnp.bfloat16),
            pltpu.SemaphoreType.DMA((3 + k_dev // MIX_TERMS,)),
        ],
        compiler_params=pltpu.CompilerParams(vmem_limit_bytes=24 * MIB),
        cost_estimate=pl.CostEstimate(
            flops=2 * k_dev * sec_dev * rows * width * width,
            bytes_accessed=2 * (left_ops.size + right_ops.size),
            transcendentals=0,
        ),
    )(*(pltpu.with_memory_space_constraint(x, pltpu.HBM) for x in (wavefunction, left_ops, right_ops)))


def reaches(shift, group, sec_dev, targets):
    return wrapped(-shift - group * sec_dev + sec_dev - 1, targets) < 2 * sec_dev - 1


def sum_kernel(order, stage, shift_ref, coef_ref, mixed_ref, held_ref, *refs):
    terms, sec_dev, rows, width = mixed_ref.shape
    targets = coef_ref.shape[0]
    half = width // 2
    picked = refs[-1]

    def pick(k, count):
        picked[count] = k
        if stage is None:
            return count + 1
        wanted = True
        for at, groups in enumerate(order[: stage + 1]):
            if at < stage:
                wanted &= ~reaches(shift_ref[k], groups[0], sec_dev, targets)
            elif at < len(order) - 1:
                wanted &= reaches(shift_ref[k], groups[0], sec_dev, targets)
        return count + jnp.where(wanted, 1, 0)

    count = lax.fori_loop(0, terms, pick, 0)
    for i in range(SUM_TERMS):
        picked[count + i] = 0

    if stage is None:
        sums = refs[:1]
    elif stage == 0:
        sums, outs = refs[:2], refs[2:-1]
    else:
        sums, outs = refs[2:4], refs[4:-1]
    if not stage:
        for total in sums:
            total[...] = jnp.zeros_like(total)

    @pl.loop(0, lax.div(count + SUM_TERMS - 1, SUM_TERMS))
    def _(step):
        for t in range(SUM_TERMS):
            at = step * SUM_TERMS + t
            k = picked[at]
            product = lax.dot_general(
                mixed_ref[k].reshape(sec_dev * rows, width),
                held_ref[k],
                (((1,), (1,)), ((), ())),
                preferred_element_type=jnp.float32,
            )
            for s in range(sec_dev):
                target = wrapped(s - shift_ref[k], targets)
                weight = jnp.where(at < count, coef_ref[target, k], 0.0)
                scaled = weight * product[s * rows : (s + 1) * rows]
                if stage is None:
                    sums[0][target] += scaled
                else:
                    sums[0][target] += scaled[:, half:]
                    sums[1][target] += scaled[:, :half]

    if stage is not None:
        for at, g in enumerate(order[stage]):
            part = slice(g * sec_dev, (g + 1) * sec_dev)
            outs[2 * at][...] = sums[0][part]
            outs[2 * at + 1][...] = sums[1][part].astype(jnp.bfloat16)


def summed(shift, coef, mixed, held, order, stage, sums=()):
    k_dev, sec_dev, rows, width = mixed.shape
    targets = coef.shape[0]
    columns = width if stage is None else width // 2
    whole = pltpu.VMEM((targets, rows, columns), jnp.float32)
    out_shape = [whole]
    if stage is not None:
        out_shape = [whole] * 2
        for _ in order[stage]:
            for dtype in (jnp.float32, jnp.bfloat16):
                out_shape.append(pltpu.VMEM((sec_dev, rows, columns), dtype))
    in_vmem = (mixed, held, *sums)
    return pl.pallas_call(
        functools.partial(sum_kernel, order, stage),
        out_shape=out_shape,
        in_specs=[pl.BlockSpec(memory_space=pltpu.SMEM)] * 2
        + [pl.BlockSpec(memory_space=pltpu.VMEM)] * len(in_vmem),
        out_specs=[pl.BlockSpec(memory_space=pltpu.VMEM)] * len(out_shape),
        input_output_aliases={4 + i: i for i in range(len(sums))},
        scratch_shapes=[pltpu.SMEM((k_dev + SUM_TERMS,), jnp.int32)],
        compiler_params=pltpu.CompilerParams(vmem_limit_bytes=24 * MIB),
        cost_estimate=pl.CostEstimate(
            flops=k_dev * sec_dev * rows * width * width,
            bytes_accessed=mixed.size + held.size,
            transcendentals=0,
        ),
    )(
        pltpu.with_memory_space_constraint(shift, pltpu.HBM),
        coef,
        *(pltpu.with_memory_space_constraint(x, pltpu.VMEM) for x in in_vmem),
    )


def shift_by(value, axis, distance):
    size = lax.axis_size(axis)
    return lax.ppermute(value, axis, [(i, (i + distance) % size) for i in range(size)])


def after(value, other):
    return lax.optimization_barrier((value, other))[0]


def per_device(wavefunction, left_ops, right_ops, site_coef, coupled, sector_shift):
    sec_dev = wavefunction.shape[0]
    devices = lax.axis_size("sector")
    live = jnp.where(coupled.T > 0, site_coef.T, 0.0)
    split = lax.axis_size("op") == 2 and devices == 4
    mixed, held = mix(wavefunction, left_ops, right_ops, split)

    if split:
        coefs = [live] + [shift_by(live, "sector", -g) for g in range(1, devices)]
        coef = jnp.concatenate(coefs, axis=0)
        order = ((2,), (1, 3, 0))
        *sums, mine_2, theirs_2 = summed(sector_shift, coef, mixed, held, order, 0)
        crossed_2 = shift_by(theirs_2, "op", 1)
        _, _, mine_1, theirs_1, mine_3, theirs_3, mine_0, theirs_0 = summed(
            sector_shift, after(coef, theirs_2), mixed, held, order, 1, sums
        )
        both_2 = (mine_2 + after(crossed_2, mine_1).astype(jnp.float32)).astype(jnp.bfloat16)
        arrived_2 = shift_by(both_2, "sector", 2)
        crossed = shift_by(jnp.concatenate([theirs_1, theirs_3], axis=0), "op", 1)
        both_1 = (mine_1 + after(crossed, both_2)[:sec_dev].astype(jnp.float32)).astype(jnp.bfloat16)
        arrived_1 = shift_by(both_1, "sector", 1)
        both_3 = (mine_3 + after(crossed, both_1)[sec_dev:].astype(jnp.float32)).astype(jnp.bfloat16)
        crossed_0 = shift_by(after(theirs_0, both_3), "op", 1)
        arrived_3 = shift_by(both_3, "sector", 3)
        sigma = mine_0 + after(arrived_2, both_3).astype(jnp.float32)
        for other in (arrived_1, crossed_0, arrived_3):
            sigma = lax.optimization_barrier(sigma) + other.astype(jnp.float32)
        return sigma

    first = lax.axis_index("sector") * sec_dev
    coef = jnp.roll(lax.all_gather(live, "sector", axis=0, tiled=True), -first, axis=0)
    (total,) = summed(sector_shift, coef, mixed, held, (), None)
    total = jnp.roll(total, first, axis=0)
    total = lax.psum_scatter(total, "op", scatter_dimension=2, tiled=True)
    return lax.psum_scatter(total, "sector", scatter_dimension=0, tiled=True)


def solution(mesh):
    placed = (
        P(("groups", "sector"), None, None),
        P(("groups", "op"), "rep", None),
        P(("groups", "op"), None, None),
        P(("groups", "op"), "sector"),
        P(("groups", "op"), "sector"),
        P(("groups", "op")),
    )
    return jax.shard_map(
        per_device,
        mesh=mesh,
        in_specs=placed,
        out_specs=P(("groups", "sector"), "rep", "op"),
        check_vma=False,
    )
```

```python
import functools

import jax
import jax.numpy as jnp
from jax import lax
from jax.experimental import pallas as pl
from jax.experimental.pallas import tpu as pltpu
from jax.sharding import PartitionSpec as P

MIX_TERMS = 16
SUM_TERMS = 4
MIB = 1024 * 1024


def wrapped(value, size):
    if size & (size - 1) == 0:
        return value & (size - 1)
    return lax.rem(value + size, size)


def mix_kernel(split, wave_ref, left_ref, right_ref, mixed_ref, held_ref, wave, left, sems):
    sec_dev = wave.shape[0]
    terms, rows, width = left.shape
    chunks = terms // MIX_TERMS

    def left_copy(c):
        part = pl.ds(c * MIX_TERMS, MIX_TERMS)
        return pltpu.make_async_copy(left_ref.at[part], left.at[part], sems.at[3 + c])

    wave_copy = pltpu.make_async_copy(wave_ref, wave, sems.at[0])
    wave_copy.start()
    for c in range(chunks):
        left_copy(c).start()
    if split:
        half = width // 2
        side = lax.axis_index("op")
        mine = pl.multiple_of(side * half, half)
        theirs = pl.multiple_of((1 - side) * half, half)
        right_copies = [
            pltpu.make_async_copy(
                right_ref.at[:, pl.ds(theirs, half)], held_ref.at[:, pl.ds(0, half)], sems.at[1]
            ),
            pltpu.make_async_copy(
                right_ref.at[:, pl.ds(mine, half)], held_ref.at[:, pl.ds(half, half)], sems.at[2]
            ),
        ]
    else:
        right_copies = [pltpu.make_async_copy(right_ref, held_ref, sems.at[1])]
    for copy in right_copies:
        copy.start()
    wave_copy.wait()

    @pl.loop(0, chunks)
    def _(c):
        left_copy(c).wait()
        part = pl.ds(c * MIX_TERMS, MIX_TERMS)
        rows_in = left[part].reshape(MIX_TERMS * rows, width)
        for s in range(sec_dev):
            product = jnp.dot(rows_in, wave[s], preferred_element_type=jnp.float32)
            mixed_ref[part, s] = product.astype(jnp.bfloat16).reshape(MIX_TERMS, rows, width)

    for copy in right_copies:
        copy.wait()


def mix(wavefunction, left_ops, right_ops, split):
    k_dev, rows, width = left_ops.shape
    sec_dev = wavefunction.shape[0]
    return pl.pallas_call(
        functools.partial(mix_kernel, split),
        out_shape=[
            pltpu.VMEM((k_dev, sec_dev, rows, width), jnp.bfloat16),
            pltpu.VMEM(right_ops.shape, jnp.bfloat16),
        ],
        in_specs=[pl.BlockSpec(memory_space=pltpu.HBM)] * 3,
        out_specs=[pl.BlockSpec(memory_space=pltpu.VMEM)] * 2,
        scratch_shapes=[
            pltpu.VMEM(wavefunction.shape, jnp.bfloat16),
            pltpu.VMEM(left_ops.shape, jnp.bfloat16),
            pltpu.SemaphoreType.DMA((3 + k_dev // MIX_TERMS,)),
        ],
        compiler_params=pltpu.CompilerParams(vmem_limit_bytes=24 * MIB),
        cost_estimate=pl.CostEstimate(
            flops=2 * k_dev * sec_dev * rows * width * width,
            bytes_accessed=2 * (left_ops.size + right_ops.size),
            transcendentals=0,
        ),
    )(*(pltpu.with_memory_space_constraint(x, pltpu.HBM) for x in (wavefunction, left_ops, right_ops)))


def sum_kernel(order, stage, shift_ref, coef_ref, mixed_ref, held_ref, *refs):
    terms, sec_dev, rows, width = mixed_ref.shape
    targets = coef_ref.shape[0]
    half = width // 2
    picked = refs[-1]
    first = lax.axis_index("sector") * sec_dev

    def reaches(k, group):
        start = (first ^ (group * sec_dev)) - first
        return wrapped(sec_dev - 1 - start - shift_ref[k], targets) < 2 * sec_dev - 1

    def pick(wanted):
        def body(k, count):
            picked[count] = k
            found = functools.reduce(jnp.logical_or, [reaches(k, group) for group in order[0]])
            return count + jnp.where(found == wanted, 1, 0)

        return body

    if stage is None:
        low, high = 0, terms // SUM_TERMS
    else:
        count = lax.fori_loop(0, terms, pick(True), 0)
        lax.fori_loop(0, terms, pick(False), count)
        steps = lax.div(jnp.maximum(count, terms // 2) + SUM_TERMS - 1, SUM_TERMS)
        low, high = (0, steps) if stage == 0 else (steps, terms // SUM_TERMS)

    if stage is None:
        sums = refs[:1]
    elif stage == 0:
        sums, outs = refs[:2], refs[2:-1]
    else:
        sums, outs = refs[2:4], refs[4:-1]
    if not stage:
        for total in sums:
            total[...] = jnp.zeros_like(total)

    @pl.loop(low, high)
    def _(step):
        for t in range(SUM_TERMS):
            k = step * SUM_TERMS + t
            if stage is not None:
                k = picked[k]
            product = lax.dot_general(
                mixed_ref[k].reshape(sec_dev * rows, width),
                held_ref[k],
                (((1,), (1,)), ((), ())),
                preferred_element_type=jnp.float32,
            )
            for s in range(sec_dev):
                slot = wrapped(first + s - shift_ref[k], targets)
                if stage is not None:
                    slot ^= first
                scaled = coef_ref[slot, k] * product[s * rows : (s + 1) * rows]
                if stage is None:
                    sums[0][slot] += scaled
                else:
                    sums[0][slot] += scaled[:, half:]
                    sums[1][slot] += scaled[:, :half]

    if stage is not None:
        for at, g in enumerate(order[stage]):
            part = slice(g * sec_dev, (g + 1) * sec_dev)
            outs[2 * at][...] = sums[0][part]
            outs[2 * at + 1][...] = sums[1][part].astype(jnp.bfloat16)


def summed(shift, coef, mixed, held, order, stage, sums=()):
    k_dev, sec_dev, rows, width = mixed.shape
    targets = coef.shape[0]
    columns = width if stage is None else width // 2
    whole = pltpu.VMEM((targets, rows, columns), jnp.float32)
    out_shape = [whole]
    if stage is not None:
        out_shape = [whole] * 2
        for _ in order[stage]:
            for dtype in (jnp.float32, jnp.bfloat16):
                out_shape.append(pltpu.VMEM((sec_dev, rows, columns), dtype))
    in_vmem = (mixed, held, *sums)
    return pl.pallas_call(
        functools.partial(sum_kernel, order, stage),
        out_shape=out_shape,
        in_specs=[pl.BlockSpec(memory_space=pltpu.SMEM)] * 2
        + [pl.BlockSpec(memory_space=pltpu.VMEM)] * len(in_vmem),
        out_specs=[pl.BlockSpec(memory_space=pltpu.VMEM)] * len(out_shape),
        input_output_aliases={4 + i: i for i in range(len(sums))},
        scratch_shapes=[pltpu.SMEM((k_dev + SUM_TERMS,), jnp.int32)],
        compiler_params=pltpu.CompilerParams(vmem_limit_bytes=24 * MIB),
        cost_estimate=pl.CostEstimate(
            flops=k_dev * sec_dev * rows * width * width,
            bytes_accessed=mixed.size + held.size,
            transcendentals=0,
        ),
    )(
        pltpu.with_memory_space_constraint(shift, pltpu.HBM),
        coef,
        *(pltpu.with_memory_space_constraint(x, pltpu.VMEM) for x in in_vmem),
    )


def swap(value, axis, mask):
    return lax.ppermute(value, axis, [(i, i ^ mask) for i in range(lax.axis_size(axis))])


def after(value, other):
    return lax.optimization_barrier((value, other))[0]


def per_device(wavefunction, left_ops, right_ops, site_coef, coupled, sector_shift):
    sec_dev = wavefunction.shape[0]
    devices = lax.axis_size("sector")
    live = jnp.where(coupled.T > 0, site_coef.T, 0.0)
    split = lax.axis_size("op") == 2 and devices == 4 and sec_dev & (sec_dev - 1) == 0
    mixed, held = mix(wavefunction, left_ops, right_ops, split)

    if split:
        coef = jnp.concatenate([live] + [swap(live, "sector", g) for g in (1, 2, 3)], axis=0)
        order = ((3,), (2, 1, 0))
        *sums, mine_3, theirs_3 = summed(sector_shift, coef, mixed, held, order, 0)
        crossed_3 = swap(theirs_3, "op", 1)
        _, _, mine_2, theirs_2, mine_1, theirs_1, mine_0, theirs_0 = summed(
            sector_shift, after(coef, theirs_3), mixed, held, order, 1, sums
        )
        both_3 = (mine_3 + after(crossed_3, mine_2).astype(jnp.float32)).astype(jnp.bfloat16)
        arrived_3 = swap(both_3, "sector", 3)
        crossed_2 = swap(after(theirs_2, both_3), "op", 1)
        crossed_1 = swap(after(theirs_1, both_3), "op", 1)
        both_2 = (mine_2 + after(crossed_2, both_3).astype(jnp.float32)).astype(jnp.bfloat16)
        arrived_2 = swap(both_2, "sector", 2)
        crossed_0 = swap(after(theirs_0, both_2), "op", 1)
        both_1 = (mine_1 + after(crossed_1, both_2).astype(jnp.float32)).astype(jnp.bfloat16)
        arrived_1 = swap(both_1, "sector", 1)
        sigma = mine_0 + after(crossed_0, both_1).astype(jnp.float32)
        for other in (arrived_3, arrived_2, arrived_1):
            sigma = lax.optimization_barrier(sigma) + other.astype(jnp.float32)
        return sigma

    coef = lax.all_gather(live, "sector", axis=0, tiled=True)
    (total,) = summed(sector_shift, coef, mixed, held, (), None)
    total = lax.psum_scatter(total, "op", scatter_dimension=2, tiled=True)
    return lax.psum_scatter(total, "sector", scatter_dimension=0, tiled=True)


def solution(mesh):
    placed = (
        P(("groups", "sector"), None, None),
        P(("groups", "op"), "rep", None),
        P(("groups", "op"), None, None),
        P(("groups", "op"), "sector"),
        P(("groups", "op"), "sector"),
        P(("groups", "op")),
    )
    return jax.shard_map(
        per_device,
        mesh=mesh,
        in_specs=placed,
        out_specs=P(("groups", "sector"), "rep", "op"),
        check_vma=False,
    )
```

```python
import functools

import jax
import jax.numpy as jnp
from jax import lax
from jax.experimental import pallas as pl
from jax.experimental.pallas import tpu as pltpu
from jax.sharding import PartitionSpec as P

MIX_TERMS = 16
SUM_TERMS = 4
MIB = 1024 * 1024


def wrapped(value, size):
    if size & (size - 1) == 0:
        return value & (size - 1)
    return lax.rem(value + size, size)


def mix_kernel(split, wave_ref, left_ref, right_ref, mixed_ref, held_ref, *refs):
    *zeros, wave, left, sems = refs
    sec_dev = wave.shape[0]
    terms, rows, width = left.shape
    chunks = terms // MIX_TERMS

    def left_copy(c):
        part = pl.ds(c * MIX_TERMS, MIX_TERMS)
        return pltpu.make_async_copy(left_ref.at[part], left.at[part], sems.at[3 + c])

    wave_copy = pltpu.make_async_copy(wave_ref, wave, sems.at[0])
    wave_copy.start()
    for c in range(chunks):
        left_copy(c).start()
    if split:
        half = width // 2
        side = lax.axis_index("op")
        mine = pl.multiple_of(side * half, half)
        theirs = pl.multiple_of((1 - side) * half, half)
        right_copies = [
            pltpu.make_async_copy(
                right_ref.at[:, pl.ds(theirs, half)], held_ref.at[:, pl.ds(0, half)], sems.at[1]
            ),
            pltpu.make_async_copy(
                right_ref.at[:, pl.ds(mine, half)], held_ref.at[:, pl.ds(half, half)], sems.at[2]
            ),
        ]
    else:
        right_copies = [pltpu.make_async_copy(right_ref, held_ref, sems.at[1])]
    for copy in right_copies:
        copy.start()
    for ref in zeros:
        ref[...] = jnp.zeros_like(ref)
    wave_copy.wait()

    @pl.loop(0, chunks)
    def _(c):
        left_copy(c).wait()
        part = pl.ds(c * MIX_TERMS, MIX_TERMS)
        rows_in = left[part].reshape(MIX_TERMS * rows, width)
        for s in range(sec_dev):
            product = jnp.dot(rows_in, wave[s], preferred_element_type=jnp.float32)
            mixed_ref[part, s] = product.astype(jnp.bfloat16).reshape(MIX_TERMS, rows, width)

    for copy in right_copies:
        copy.wait()


def mix(wavefunction, left_ops, right_ops, targets, split):
    k_dev, rows, width = left_ops.shape
    sec_dev = wavefunction.shape[0]
    zeros = [pltpu.VMEM((targets, rows, width // 2), jnp.float32)] * (2 if split else 0)
    return pl.pallas_call(
        functools.partial(mix_kernel, split),
        out_shape=[
            pltpu.VMEM((k_dev, sec_dev, rows, width), jnp.bfloat16),
            pltpu.VMEM(right_ops.shape, jnp.bfloat16),
        ]
        + zeros,
        in_specs=[pl.BlockSpec(memory_space=pltpu.HBM)] * 3,
        out_specs=[pl.BlockSpec(memory_space=pltpu.VMEM)] * (2 + len(zeros)),
        scratch_shapes=[
            pltpu.VMEM(wavefunction.shape, jnp.bfloat16),
            pltpu.VMEM(left_ops.shape, jnp.bfloat16),
            pltpu.SemaphoreType.DMA((3 + k_dev // MIX_TERMS,)),
        ],
        compiler_params=pltpu.CompilerParams(vmem_limit_bytes=24 * MIB),
        cost_estimate=pl.CostEstimate(
            flops=2 * k_dev * sec_dev * rows * width * width,
            bytes_accessed=2 * (left_ops.size + right_ops.size),
            transcendentals=0,
        ),
    )(*(pltpu.with_memory_space_constraint(x, pltpu.HBM) for x in (wavefunction, left_ops, right_ops)))


def reaches(shift, group, sec_dev, targets):
    return wrapped(-shift - group * sec_dev + sec_dev - 1, targets) < 2 * sec_dev - 1


def sum_kernel(order, stage, shift_ref, coef_ref, mixed_ref, held_ref, *refs):
    terms, sec_dev, rows, width = mixed_ref.shape
    targets = coef_ref.shape[0]
    half = width // 2
    picked = refs[-1]

    def pick(k, count):
        picked[count] = k
        if stage is None:
            return count + 1
        wanted = True
        for at, groups in enumerate(order[: stage + 1]):
            if at < stage:
                wanted &= ~reaches(shift_ref[k], groups[0], sec_dev, targets)
            elif at < len(order) - 1:
                wanted &= reaches(shift_ref[k], groups[0], sec_dev, targets)
        return count + jnp.where(wanted, 1, 0)

    count = lax.fori_loop(0, terms, pick, 0, unroll=8)
    for i in range(SUM_TERMS):
        picked[count + i] = 0

    if stage is None:
        sums = refs[:1]
        sums[0][...] = jnp.zeros_like(sums[0])
    else:
        sums, outs = refs[2:4], refs[4:-1]

    @pl.loop(0, lax.div(count + SUM_TERMS - 1, SUM_TERMS))
    def _(step):
        for t in range(SUM_TERMS):
            at = step * SUM_TERMS + t
            k = picked[at]
            product = lax.dot_general(
                mixed_ref[k].reshape(sec_dev * rows, width),
                held_ref[k],
                (((1,), (1,)), ((), ())),
                preferred_element_type=jnp.float32,
            )
            for s in range(sec_dev):
                target = wrapped(s - shift_ref[k], targets)
                weight = jnp.where(at < count, coef_ref[target, k], 0.0)
                scaled = weight * product[s * rows : (s + 1) * rows]
                if stage is None:
                    sums[0][target] += scaled
                else:
                    sums[0][target] += scaled[:, half:]
                    sums[1][target] += scaled[:, :half]

    if stage is not None:
        for at, g in enumerate(order[stage]):
            part = slice(g * sec_dev, (g + 1) * sec_dev)
            outs[2 * at][...] = sums[0][part]
            outs[2 * at + 1][...] = sums[1][part].astype(jnp.bfloat16)


def summed(shift, coef, mixed, held, order, stage, sums=()):
    k_dev, sec_dev, rows, width = mixed.shape
    targets = coef.shape[0]
    columns = width if stage is None else width // 2
    whole = pltpu.VMEM((targets, rows, columns), jnp.float32)
    out_shape = [whole]
    if stage is not None:
        out_shape = [whole] * 2
        for _ in order[stage]:
            for dtype in (jnp.float32, jnp.bfloat16):
                out_shape.append(pltpu.VMEM((sec_dev, rows, columns), dtype))
    in_vmem = (mixed, held, *sums)
    return pl.pallas_call(
        functools.partial(sum_kernel, order, stage),
        out_shape=out_shape,
        in_specs=[pl.BlockSpec(memory_space=pltpu.SMEM)] * 2
        + [pl.BlockSpec(memory_space=pltpu.VMEM)] * len(in_vmem),
        out_specs=[pl.BlockSpec(memory_space=pltpu.VMEM)] * len(out_shape),
        input_output_aliases={4 + i: i for i in range(len(sums))},
        scratch_shapes=[pltpu.SMEM((k_dev + SUM_TERMS,), jnp.int32)],
        compiler_params=pltpu.CompilerParams(vmem_limit_bytes=24 * MIB),
        cost_estimate=pl.CostEstimate(
            flops=k_dev * sec_dev * rows * width * width,
            bytes_accessed=mixed.size + held.size,
            transcendentals=0,
        ),
    )(
        pltpu.with_memory_space_constraint(shift, pltpu.HBM),
        coef,
        *(pltpu.with_memory_space_constraint(x, pltpu.VMEM) for x in in_vmem),
    )


def shift_by(value, axis, distance):
    size = lax.axis_size(axis)
    return lax.ppermute(value, axis, [(i, (i + distance) % size) for i in range(size)])


def after(value, other):
    return lax.optimization_barrier((value, other))[0]


def per_device(wavefunction, left_ops, right_ops, site_coef, coupled, sector_shift):
    sec_dev = wavefunction.shape[0]
    devices = lax.axis_size("sector")
    live = jnp.where(coupled.T > 0, site_coef.T, 0.0)
    split = lax.axis_size("op") == 2 and devices == 4
    mixed, held, *sums = mix(
        wavefunction, left_ops, right_ops, sec_dev * devices, split
    )

    if split:
        coefs = [live] + [shift_by(live, "sector", -g) for g in range(1, devices)]
        coef = jnp.concatenate(coefs, axis=0)
        order = ((2,), (1, 3, 0))
        *sums, mine_2, theirs_2 = summed(sector_shift, coef, mixed, held, order, 0, sums)
        crossed_2 = shift_by(theirs_2, "op", 1)
        _, _, mine_1, theirs_1, mine_3, theirs_3, mine_0, theirs_0 = summed(
            sector_shift, after(coef, theirs_2), mixed, held, order, 1, sums
        )
        both_2 = (mine_2 + after(crossed_2, mine_1).astype(jnp.float32)).astype(jnp.bfloat16)
        arrived_2 = shift_by(both_2, "sector", 2)
        crossed_1 = shift_by(after(theirs_1, both_2), "op", 1)
        crossed_3 = shift_by(after(theirs_3, both_2), "op", 1)
        both_1 = (mine_1 + after(crossed_1, both_2).astype(jnp.float32)).astype(jnp.bfloat16)
        arrived_1 = shift_by(both_1, "sector", 1)
        crossed_0 = shift_by(after(theirs_0, both_1), "op", 1)
        both_3 = (mine_3 + after(crossed_3, both_1).astype(jnp.float32)).astype(jnp.bfloat16)
        arrived_3 = shift_by(both_3, "sector", 3)
        sigma = mine_0 + after(crossed_0, both_3).astype(jnp.float32)
        for other in (arrived_2, arrived_1, arrived_3):
            sigma = lax.optimization_barrier(sigma) + other.astype(jnp.float32)
        return sigma

    first = lax.axis_index("sector") * sec_dev
    coef = jnp.roll(lax.all_gather(live, "sector", axis=0, tiled=True), -first, axis=0)
    (total,) = summed(sector_shift, coef, mixed, held, (), None)
    total = jnp.roll(total, first, axis=0)
    total = lax.psum_scatter(total, "op", scatter_dimension=2, tiled=True)
    return lax.psum_scatter(total, "sector", scatter_dimension=0, tiled=True)


def solution(mesh):
    placed = (
        P(("groups", "sector"), None, None),
        P(("groups", "op"), "rep", None),
        P(("groups", "op"), None, None),
        P(("groups", "op"), "sector"),
        P(("groups", "op"), "sector"),
        P(("groups", "op")),
    )
    return jax.shard_map(
        per_device,
        mesh=mesh,
        in_specs=placed,
        out_specs=P(("groups", "sector"), "rep", "op"),
        check_vma=False,
    )
```

```python
import functools

import jax
import jax.numpy as jnp
from jax import lax
from jax.experimental import pallas as pl
from jax.experimental.pallas import tpu as pltpu
from jax.sharding import PartitionSpec as P

MIX_TERMS = 16
SUM_TERMS = 4
MIB = 1024 * 1024


def wrapped(value, size):
    if size & (size - 1) == 0:
        return value & (size - 1)
    return lax.rem(value + size, size)


def mix_kernel(split, shift_ref, wave_ref, left_ref, right_ref, mixed_ref, held_ref, row_ref, *refs):
    *zeros, shifts, wave, left, sems = refs
    sec_dev = wave.shape[0]
    terms, rows, width = left.shape
    chunks = terms // MIX_TERMS

    def left_copy(c):
        part = pl.ds(c * MIX_TERMS, MIX_TERMS)
        return pltpu.make_async_copy(left_ref.at[part], left.at[part], sems.at[4 + c])

    wave_copy = pltpu.make_async_copy(wave_ref, wave, sems.at[0])
    wave_copy.start()
    shift_copy = pltpu.make_async_copy(shift_ref, shifts, sems.at[3])
    shift_copy.start()
    for c in range(chunks):
        left_copy(c).start()
    if split:
        half = width // 2
        side = lax.axis_index("op")
        mine = pl.multiple_of(side * half, half)
        theirs = pl.multiple_of((1 - side) * half, half)
        right_copies = [
            pltpu.make_async_copy(
                right_ref.at[:, pl.ds(theirs, half)], held_ref.at[:, pl.ds(0, half)], sems.at[1]
            ),
            pltpu.make_async_copy(
                right_ref.at[:, pl.ds(mine, half)], held_ref.at[:, pl.ds(half, half)], sems.at[2]
            ),
        ]
    else:
        right_copies = [pltpu.make_async_copy(right_ref, held_ref, sems.at[1])]
    for copy in right_copies:
        copy.start()
    for ref in zeros:
        ref[...] = jnp.zeros_like(ref)
    shift_copy.wait()
    row_ref[...] = shifts[...].astype(jnp.float32)
    wave_copy.wait()

    @pl.loop(0, chunks)
    def _(c):
        left_copy(c).wait()
        part = pl.ds(c * MIX_TERMS, MIX_TERMS)
        rows_in = left[part].reshape(MIX_TERMS * rows, width)
        for s in range(sec_dev):
            product = jnp.dot(rows_in, wave[s], preferred_element_type=jnp.float32)
            mixed_ref[part, s] = product.astype(jnp.bfloat16).reshape(MIX_TERMS, rows, width)

    for copy in right_copies:
        copy.wait()


def mix(shift, wavefunction, left_ops, right_ops, targets, split):
    k_dev, rows, width = left_ops.shape
    sec_dev = wavefunction.shape[0]
    zeros = [pltpu.VMEM((targets, rows, width // 2), jnp.float32)] * (2 if split else 0)
    return pl.pallas_call(
        functools.partial(mix_kernel, split),
        out_shape=[
            pltpu.VMEM((k_dev, sec_dev, rows, width), jnp.bfloat16),
            pltpu.VMEM(right_ops.shape, jnp.bfloat16),
            pltpu.VMEM(shift.shape, jnp.float32),
        ]
        + zeros,
        in_specs=[pl.BlockSpec(memory_space=pltpu.HBM)] * 4,
        out_specs=[pl.BlockSpec(memory_space=pltpu.VMEM)] * (3 + len(zeros)),
        scratch_shapes=[
            pltpu.VMEM(shift.shape, jnp.int32),
            pltpu.VMEM(wavefunction.shape, jnp.bfloat16),
            pltpu.VMEM(left_ops.shape, jnp.bfloat16),
            pltpu.SemaphoreType.DMA((4 + k_dev // MIX_TERMS,)),
        ],
        compiler_params=pltpu.CompilerParams(vmem_limit_bytes=24 * MIB),
        cost_estimate=pl.CostEstimate(
            flops=2 * k_dev * sec_dev * rows * width * width,
            bytes_accessed=2 * (left_ops.size + right_ops.size),
            transcendentals=0,
        ),
    )(
        *(
            pltpu.with_memory_space_constraint(x, pltpu.HBM)
            for x in (shift, wavefunction, left_ops, right_ops)
        )
    )


def reaches(shift, group, sec_dev, targets):
    return wrapped(-shift - group * sec_dev + sec_dev - 1, targets) < 2 * sec_dev - 1


def sum_kernel(order, stage, table_ref, mixed_ref, held_ref, *refs):
    terms, sec_dev, rows, width = mixed_ref.shape
    targets = table_ref.shape[0] - 1
    half = width // 2
    picked = refs[-1]

    def shift_of(k):
        return table_ref[targets, k].astype(jnp.int32)

    def pick(k, count):
        picked[count] = k
        if stage is None:
            return count + 1
        wanted, shift = True, shift_of(k)
        for at, groups in enumerate(order[: stage + 1]):
            if at < stage:
                wanted &= ~reaches(shift, groups[0], sec_dev, targets)
            elif at < len(order) - 1:
                wanted &= reaches(shift, groups[0], sec_dev, targets)
        return count + jnp.where(wanted, 1, 0)

    count = lax.fori_loop(0, terms, pick, 0, unroll=8)
    for i in range(SUM_TERMS):
        picked[count + i] = 0

    if stage is None:
        sums = refs[:1]
        sums[0][...] = jnp.zeros_like(sums[0])
    else:
        sums, outs = refs[2:4], refs[4:-1]

    @pl.loop(0, lax.div(count + SUM_TERMS - 1, SUM_TERMS))
    def _(step):
        for t in range(SUM_TERMS):
            at = step * SUM_TERMS + t
            k = picked[at]
            shift = shift_of(k)
            product = lax.dot_general(
                mixed_ref[k].reshape(sec_dev * rows, width),
                held_ref[k],
                (((1,), (1,)), ((), ())),
                preferred_element_type=jnp.float32,
            )
            for s in range(sec_dev):
                target = wrapped(s - shift, targets)
                weight = jnp.where(at < count, table_ref[target, k], 0.0)
                scaled = weight * product[s * rows : (s + 1) * rows]
                if stage is None:
                    sums[0][target] += scaled
                else:
                    sums[0][target] += scaled[:, half:]
                    sums[1][target] += scaled[:, :half]

    if stage is not None:
        for at, g in enumerate(order[stage]):
            part = slice(g * sec_dev, (g + 1) * sec_dev)
            outs[2 * at][...] = sums[0][part]
            outs[2 * at + 1][...] = sums[1][part].astype(jnp.bfloat16)


def summed(table, mixed, held, order, stage, sums=()):
    k_dev, sec_dev, rows, width = mixed.shape
    targets = table.shape[0] - 1
    columns = width if stage is None else width // 2
    whole = pltpu.VMEM((targets, rows, columns), jnp.float32)
    out_shape = [whole]
    if stage is not None:
        out_shape = [whole] * 2
        for _ in order[stage]:
            for dtype in (jnp.float32, jnp.bfloat16):
                out_shape.append(pltpu.VMEM((sec_dev, rows, columns), dtype))
    in_vmem = (mixed, held, *sums)
    return pl.pallas_call(
        functools.partial(sum_kernel, order, stage),
        out_shape=out_shape,
        in_specs=[pl.BlockSpec(memory_space=pltpu.SMEM)]
        + [pl.BlockSpec(memory_space=pltpu.VMEM)] * len(in_vmem),
        out_specs=[pl.BlockSpec(memory_space=pltpu.VMEM)] * len(out_shape),
        input_output_aliases={3 + i: i for i in range(len(sums))},
        scratch_shapes=[pltpu.SMEM((k_dev + SUM_TERMS,), jnp.int32)],
        compiler_params=pltpu.CompilerParams(vmem_limit_bytes=24 * MIB),
        cost_estimate=pl.CostEstimate(
            flops=k_dev * sec_dev * rows * width * width,
            bytes_accessed=mixed.size + held.size,
            transcendentals=0,
        ),
    )(table, *(pltpu.with_memory_space_constraint(x, pltpu.VMEM) for x in in_vmem))


def shift_by(value, axis, distance):
    size = lax.axis_size(axis)
    return lax.ppermute(value, axis, [(i, (i + distance) % size) for i in range(size)])


def after(value, other):
    return lax.optimization_barrier((value, other))[0]


def per_device(wavefunction, left_ops, right_ops, site_coef, coupled, sector_shift):
    sec_dev = wavefunction.shape[0]
    devices = lax.axis_size("sector")
    live = jnp.where(coupled.T > 0, site_coef.T, 0.0)
    split = lax.axis_size("op") == 2 and devices == 4
    mixed, held, row, *sums = mix(
        sector_shift[None], wavefunction, left_ops, right_ops, sec_dev * devices, split
    )

    if split:
        coefs = [live] + [shift_by(live, "sector", -g) for g in range(1, devices)]
        table = jnp.concatenate(coefs + [row], axis=0)
        order = ((2,), (1, 3, 0))
        *sums, mine_2, theirs_2 = summed(table, mixed, held, order, 0, sums)
        crossed_2 = shift_by(theirs_2, "op", 1)
        _, _, mine_1, theirs_1, mine_3, theirs_3, mine_0, theirs_0 = summed(
            after(table, theirs_2), mixed, held, order, 1, sums
        )
        both_2 = (mine_2 + after(crossed_2, mine_1).astype(jnp.float32)).astype(jnp.bfloat16)
        arrived_2 = shift_by(both_2, "sector", 2)
        crossed_1 = shift_by(after(theirs_1, both_2), "op", 1)
        crossed_3 = shift_by(after(theirs_3, both_2), "op", 1)
        both_1 = (mine_1 + after(crossed_1, both_2).astype(jnp.float32)).astype(jnp.bfloat16)
        arrived_1 = shift_by(both_1, "sector", 1)
        crossed_0 = shift_by(after(theirs_0, both_1), "op", 1)
        both_3 = (mine_3 + after(crossed_3, both_1).astype(jnp.float32)).astype(jnp.bfloat16)
        arrived_3 = shift_by(both_3, "sector", 3)
        sigma = mine_0 + after(crossed_0, both_3).astype(jnp.float32)
        for other in (arrived_2, arrived_1, arrived_3):
            sigma = lax.optimization_barrier(sigma) + other.astype(jnp.float32)
        return sigma

    first = lax.axis_index("sector") * sec_dev
    coef = jnp.roll(lax.all_gather(live, "sector", axis=0, tiled=True), -first, axis=0)
    (total,) = summed(jnp.concatenate([coef, row], axis=0), mixed, held, (), None)
    total = jnp.roll(total, first, axis=0)
    total = lax.psum_scatter(total, "op", scatter_dimension=2, tiled=True)
    return lax.psum_scatter(total, "sector", scatter_dimension=0, tiled=True)


def solution(mesh):
    placed = (
        P(("groups", "sector"), None, None),
        P(("groups", "op"), "rep", None),
        P(("groups", "op"), None, None),
        P(("groups", "op"), "sector"),
        P(("groups", "op"), "sector"),
        P(("groups", "op")),
    )
    return jax.shard_map(
        per_device,
        mesh=mesh,
        in_specs=placed,
        out_specs=P(("groups", "sector"), "rep", "op"),
        check_vma=False,
    )
```

```python
import functools

import jax
import jax.numpy as jnp
from jax import lax
from jax.experimental import pallas as pl
from jax.experimental.pallas import tpu as pltpu
from jax.sharding import PartitionSpec as P

MIX_TERMS = 16
SUM_TERMS = 4
MIB = 1024 * 1024


def wrapped(value, size):
    if size & (size - 1) == 0:
        return value & (size - 1)
    return lax.rem(value + size, size)


def mix_kernel(split, wave_ref, left_ref, right_ref, mixed_ref, held_ref, *refs):
    *zeros, wave, left, sems = refs
    sec_dev = wave.shape[0]
    terms, rows, width = left.shape
    chunks = terms // MIX_TERMS

    def left_copy(c):
        part = pl.ds(c * MIX_TERMS, MIX_TERMS)
        return pltpu.make_async_copy(left_ref.at[part], left.at[part], sems.at[3 + c])

    wave_copy = pltpu.make_async_copy(wave_ref, wave, sems.at[0])
    wave_copy.start()
    for c in range(chunks):
        left_copy(c).start()
    if split:
        half = width // 2
        side = lax.axis_index("op")
        mine = pl.multiple_of(side * half, half)
        theirs = pl.multiple_of((1 - side) * half, half)
        right_copies = [
            pltpu.make_async_copy(
                right_ref.at[:, pl.ds(theirs, half)], held_ref.at[:, pl.ds(0, half)], sems.at[1]
            ),
            pltpu.make_async_copy(
                right_ref.at[:, pl.ds(mine, half)], held_ref.at[:, pl.ds(half, half)], sems.at[2]
            ),
        ]
    else:
        right_copies = [pltpu.make_async_copy(right_ref, held_ref, sems.at[1])]
    for copy in right_copies:
        copy.start()
    for ref in zeros:
        ref[...] = jnp.zeros_like(ref)
    wave_copy.wait()

    @pl.loop(0, chunks)
    def _(c):
        left_copy(c).wait()
        part = pl.ds(c * MIX_TERMS, MIX_TERMS)
        rows_in = left[part].reshape(MIX_TERMS * rows, width)
        for s in range(sec_dev):
            product = jnp.dot(rows_in, wave[s], preferred_element_type=jnp.float32)
            mixed_ref[part, s] = product.astype(jnp.bfloat16).reshape(MIX_TERMS, rows, width)

    for copy in right_copies:
        copy.wait()


def mix(wavefunction, left_ops, right_ops, targets, split):
    k_dev, rows, width = left_ops.shape
    sec_dev = wavefunction.shape[0]
    zeros = [pltpu.VMEM((targets, rows, width // 2), jnp.float32)] * (2 if split else 0)
    return pl.pallas_call(
        functools.partial(mix_kernel, split),
        out_shape=[
            pltpu.VMEM((k_dev, sec_dev, rows, width), jnp.bfloat16),
            pltpu.VMEM(right_ops.shape, jnp.bfloat16),
        ]
        + zeros,
        in_specs=[pl.BlockSpec(memory_space=pltpu.HBM)] * 3,
        out_specs=[pl.BlockSpec(memory_space=pltpu.VMEM)] * (2 + len(zeros)),
        scratch_shapes=[
            pltpu.VMEM(wavefunction.shape, jnp.bfloat16),
            pltpu.VMEM(left_ops.shape, jnp.bfloat16),
            pltpu.SemaphoreType.DMA((3 + k_dev // MIX_TERMS,)),
        ],
        compiler_params=pltpu.CompilerParams(vmem_limit_bytes=24 * MIB),
        cost_estimate=pl.CostEstimate(
            flops=2 * k_dev * sec_dev * rows * width * width,
            bytes_accessed=2 * (left_ops.size + right_ops.size),
            transcendentals=0,
        ),
    )(*(pltpu.with_memory_space_constraint(x, pltpu.HBM) for x in (wavefunction, left_ops, right_ops)))


def reaches(shift, group, sec_dev, targets):
    return wrapped(-shift - group * sec_dev + sec_dev - 1, targets) < 2 * sec_dev - 1


def sum_kernel(order, stage, shift_ref, coef_ref, mixed_ref, held_ref, *refs):
    terms, sec_dev, rows, width = mixed_ref.shape
    targets = coef_ref.shape[0]
    half = width // 2
    picked = refs[-1]

    def pick(k, count):
        picked[count] = k
        if stage is None:
            return count + 1
        wanted = True
        for at, groups in enumerate(order[: stage + 1]):
            if at < stage:
                wanted &= ~reaches(shift_ref[k], groups[0], sec_dev, targets)
            elif at < len(order) - 1:
                wanted &= reaches(shift_ref[k], groups[0], sec_dev, targets)
        return count + jnp.where(wanted, 1, 0)

    count = lax.fori_loop(0, terms, pick, 0, unroll=8)
    for i in range(SUM_TERMS):
        picked[count + i] = 0

    if stage is None:
        sums = refs[:1]
        sums[0][...] = jnp.zeros_like(sums[0])
    else:
        sums, outs = refs[2:4], refs[4:-1]

    @pl.loop(0, lax.div(count + SUM_TERMS - 1, SUM_TERMS))
    def _(step):
        ks = [picked[step * SUM_TERMS + t] for t in range(SUM_TERMS)]
        shifts = [shift_ref[k] for k in ks]
        places = [[wrapped(s - shift, targets) for s in range(sec_dev)] for shift in shifts]
        weights = [
            [
                jnp.where(step * SUM_TERMS + t < count, coef_ref[target, ks[t]], 0.0)
                for target in places[t]
            ]
            for t in range(SUM_TERMS)
        ]
        for t, k in enumerate(ks):
            product = lax.dot_general(
                mixed_ref[k].reshape(sec_dev * rows, width),
                held_ref[k],
                (((1,), (1,)), ((), ())),
                preferred_element_type=jnp.float32,
            )
            for s, target in enumerate(places[t]):
                scaled = weights[t][s] * product[s * rows : (s + 1) * rows]
                if stage is None:
                    sums[0][target] += scaled
                else:
                    sums[0][target] += scaled[:, half:]
                    sums[1][target] += scaled[:, :half]

    if stage is not None:
        for at, g in enumerate(order[stage]):
            part = slice(g * sec_dev, (g + 1) * sec_dev)
            outs[2 * at][...] = sums[0][part]
            outs[2 * at + 1][...] = sums[1][part].astype(jnp.bfloat16)


def summed(shift, coef, mixed, held, order, stage, sums=()):
    k_dev, sec_dev, rows, width = mixed.shape
    targets = coef.shape[0]
    columns = width if stage is None else width // 2
    whole = pltpu.VMEM((targets, rows, columns), jnp.float32)
    out_shape = [whole]
    if stage is not None:
        out_shape = [whole] * 2
        for _ in order[stage]:
            for dtype in (jnp.float32, jnp.bfloat16):
                out_shape.append(pltpu.VMEM((sec_dev, rows, columns), dtype))
    in_vmem = (mixed, held, *sums)
    return pl.pallas_call(
        functools.partial(sum_kernel, order, stage),
        out_shape=out_shape,
        in_specs=[pl.BlockSpec(memory_space=pltpu.SMEM)] * 2
        + [pl.BlockSpec(memory_space=pltpu.VMEM)] * len(in_vmem),
        out_specs=[pl.BlockSpec(memory_space=pltpu.VMEM)] * len(out_shape),
        input_output_aliases={4 + i: i for i in range(len(sums))},
        scratch_shapes=[pltpu.SMEM((k_dev + SUM_TERMS,), jnp.int32)],
        compiler_params=pltpu.CompilerParams(vmem_limit_bytes=24 * MIB),
        cost_estimate=pl.CostEstimate(
            flops=k_dev * sec_dev * rows * width * width,
            bytes_accessed=mixed.size + held.size,
            transcendentals=0,
        ),
    )(
        pltpu.with_memory_space_constraint(shift, pltpu.HBM),
        coef,
        *(pltpu.with_memory_space_constraint(x, pltpu.VMEM) for x in in_vmem),
    )


def shift_by(value, axis, distance):
    size = lax.axis_size(axis)
    return lax.ppermute(value, axis, [(i, (i + distance) % size) for i in range(size)])


def after(value, other):
    return lax.optimization_barrier((value, other))[0]


def per_device(wavefunction, left_ops, right_ops, site_coef, coupled, sector_shift):
    sec_dev = wavefunction.shape[0]
    devices = lax.axis_size("sector")
    live = jnp.where(coupled.T > 0, site_coef.T, 0.0)
    split = lax.axis_size("op") == 2 and devices == 4
    mixed, held, *sums = mix(
        wavefunction, left_ops, right_ops, sec_dev * devices, split
    )

    if split:
        coefs = [live] + [shift_by(live, "sector", -g) for g in range(1, devices)]
        coef = jnp.concatenate(coefs, axis=0)
        order = ((2,), (1, 3, 0))
        *sums, mine_2, theirs_2 = summed(sector_shift, coef, mixed, held, order, 0, sums)
        crossed_2 = shift_by(theirs_2, "op", 1)
        _, _, mine_1, theirs_1, mine_3, theirs_3, mine_0, theirs_0 = summed(
            sector_shift, after(coef, theirs_2), mixed, held, order, 1, sums
        )
        both_2 = (mine_2 + after(crossed_2, mine_1).astype(jnp.float32)).astype(jnp.bfloat16)
        arrived_2 = shift_by(both_2, "sector", 2)
        crossed_1 = shift_by(after(theirs_1, both_2), "op", 1)
        crossed_3 = shift_by(after(theirs_3, both_2), "op", 1)
        both_1 = (mine_1 + after(crossed_1, both_2).astype(jnp.float32)).astype(jnp.bfloat16)
        arrived_1 = shift_by(both_1, "sector", 1)
        crossed_0 = shift_by(after(theirs_0, both_1), "op", 1)
        both_3 = (mine_3 + after(crossed_3, both_1).astype(jnp.float32)).astype(jnp.bfloat16)
        arrived_3 = shift_by(both_3, "sector", 3)
        sigma = mine_0 + after(crossed_0, both_3).astype(jnp.float32)
        for other in (arrived_2, arrived_1, arrived_3):
            sigma = lax.optimization_barrier(sigma) + other.astype(jnp.float32)
        return sigma

    first = lax.axis_index("sector") * sec_dev
    coef = jnp.roll(lax.all_gather(live, "sector", axis=0, tiled=True), -first, axis=0)
    (total,) = summed(sector_shift, coef, mixed, held, (), None)
    total = jnp.roll(total, first, axis=0)
    total = lax.psum_scatter(total, "op", scatter_dimension=2, tiled=True)
    return lax.psum_scatter(total, "sector", scatter_dimension=0, tiled=True)


def solution(mesh):
    placed = (
        P(("groups", "sector"), None, None),
        P(("groups", "op"), "rep", None),
        P(("groups", "op"), None, None),
        P(("groups", "op"), "sector"),
        P(("groups", "op"), "sector"),
        P(("groups", "op")),
    )
    return jax.shard_map(
        per_device,
        mesh=mesh,
        in_specs=placed,
        out_specs=P(("groups", "sector"), "rep", "op"),
        check_vma=False,
    )
```

```python
import functools

import jax
import jax.numpy as jnp
from jax import lax
from jax.experimental import pallas as pl
from jax.experimental.pallas import tpu as pltpu
from jax.sharding import PartitionSpec as P

MIX_TERMS = 16
SUM_TERMS = 2
MIB = 1024 * 1024


def wrapped(value, size):
    if size & (size - 1) == 0:
        return value & (size - 1)
    return lax.rem(value + size, size)


def mix_kernel(split, wave_ref, left_ref, right_ref, mixed_ref, held_ref, *refs):
    *zeros, wave, left, sems = refs
    sec_dev = wave.shape[0]
    terms, rows, width = left.shape
    chunks = terms // MIX_TERMS

    def left_copy(c):
        part = pl.ds(c * MIX_TERMS, MIX_TERMS)
        return pltpu.make_async_copy(left_ref.at[part], left.at[part], sems.at[3 + c])

    wave_copy = pltpu.make_async_copy(wave_ref, wave, sems.at[0])
    wave_copy.start()
    for c in range(chunks):
        left_copy(c).start()
    if split:
        half = width // 2
        side = lax.axis_index("op")
        mine = pl.multiple_of(side * half, half)
        theirs = pl.multiple_of((1 - side) * half, half)
        right_copies = [
            pltpu.make_async_copy(
                right_ref.at[:, pl.ds(theirs, half)], held_ref.at[:, pl.ds(0, half)], sems.at[1]
            ),
            pltpu.make_async_copy(
                right_ref.at[:, pl.ds(mine, half)], held_ref.at[:, pl.ds(half, half)], sems.at[2]
            ),
        ]
    else:
        right_copies = [pltpu.make_async_copy(right_ref, held_ref, sems.at[1])]
    for copy in right_copies:
        copy.start()
    for ref in zeros:
        ref[...] = jnp.zeros_like(ref)
    wave_copy.wait()

    @pl.loop(0, chunks)
    def _(c):
        left_copy(c).wait()
        part = pl.ds(c * MIX_TERMS, MIX_TERMS)
        rows_in = left[part].reshape(MIX_TERMS * rows, width)
        for s in range(sec_dev):
            product = jnp.dot(rows_in, wave[s], preferred_element_type=jnp.float32)
            mixed_ref[part, s] = product.astype(jnp.bfloat16).reshape(MIX_TERMS, rows, width)

    for copy in right_copies:
        copy.wait()


def mix(wavefunction, left_ops, right_ops, targets, split):
    k_dev, rows, width = left_ops.shape
    sec_dev = wavefunction.shape[0]
    zeros = [pltpu.VMEM((targets, rows, width // 2), jnp.float32)] * (2 if split else 0)
    return pl.pallas_call(
        functools.partial(mix_kernel, split),
        out_shape=[
            pltpu.VMEM((k_dev, sec_dev, rows, width), jnp.bfloat16),
            pltpu.VMEM(right_ops.shape, jnp.bfloat16),
        ]
        + zeros,
        in_specs=[pl.BlockSpec(memory_space=pltpu.HBM)] * 3,
        out_specs=[pl.BlockSpec(memory_space=pltpu.VMEM)] * (2 + len(zeros)),
        scratch_shapes=[
            pltpu.VMEM(wavefunction.shape, jnp.bfloat16),
            pltpu.VMEM(left_ops.shape, jnp.bfloat16),
            pltpu.SemaphoreType.DMA((3 + k_dev // MIX_TERMS,)),
        ],
        compiler_params=pltpu.CompilerParams(vmem_limit_bytes=24 * MIB),
        cost_estimate=pl.CostEstimate(
            flops=2 * k_dev * sec_dev * rows * width * width,
            bytes_accessed=2 * (left_ops.size + right_ops.size),
            transcendentals=0,
        ),
    )(*(pltpu.with_memory_space_constraint(x, pltpu.HBM) for x in (wavefunction, left_ops, right_ops)))


def reaches(shift, group, sec_dev, targets):
    return wrapped(-shift - group * sec_dev + sec_dev - 1, targets) < 2 * sec_dev - 1


def sum_kernel(order, stage, shift_ref, coef_ref, mixed_ref, held_ref, *refs):
    terms, sec_dev, rows, width = mixed_ref.shape
    targets = coef_ref.shape[0]
    half = width // 2
    picked = refs[-1]

    def pick(k, count):
        picked[count] = k
        if stage is None:
            return count + 1
        wanted = True
        for at, groups in enumerate(order[: stage + 1]):
            if at < stage:
                wanted &= ~reaches(shift_ref[k], groups[0], sec_dev, targets)
            elif at < len(order) - 1:
                wanted &= reaches(shift_ref[k], groups[0], sec_dev, targets)
        return count + jnp.where(wanted, 1, 0)

    count = lax.fori_loop(0, terms, pick, 0, unroll=8)
    for i in range(SUM_TERMS):
        picked[count + i] = 0

    if stage is None:
        sums = refs[:1]
        sums[0][...] = jnp.zeros_like(sums[0])
    else:
        sums, outs = refs[2:4], refs[4:-1]

    @pl.loop(0, lax.div(count + SUM_TERMS - 1, SUM_TERMS))
    def _(step):
        for t in range(SUM_TERMS):
            at = step * SUM_TERMS + t
            k = picked[at]
            product = lax.dot_general(
                mixed_ref[k].reshape(sec_dev * rows, width),
                held_ref[k],
                (((1,), (1,)), ((), ())),
                preferred_element_type=jnp.float32,
            )
            for s in range(sec_dev):
                target = wrapped(s - shift_ref[k], targets)
                weight = jnp.where(at < count, coef_ref[target, k], 0.0)
                scaled = weight * product[s * rows : (s + 1) * rows]
                if stage is None:
                    sums[0][target] += scaled
                else:
                    sums[0][target] += scaled[:, half:]
                    sums[1][target] += scaled[:, :half]

    if stage is not None:
        for at, g in enumerate(order[stage]):
            part = slice(g * sec_dev, (g + 1) * sec_dev)
            outs[2 * at][...] = sums[0][part]
            outs[2 * at + 1][...] = sums[1][part].astype(jnp.bfloat16)


def summed(shift, coef, mixed, held, order, stage, sums=()):
    k_dev, sec_dev, rows, width = mixed.shape
    targets = coef.shape[0]
    columns = width if stage is None else width // 2
    whole = pltpu.VMEM((targets, rows, columns), jnp.float32)
    out_shape = [whole]
    if stage is not None:
        out_shape = [whole] * 2
        for _ in order[stage]:
            for dtype in (jnp.float32, jnp.bfloat16):
                out_shape.append(pltpu.VMEM((sec_dev, rows, columns), dtype))
    in_vmem = (mixed, held, *sums)
    return pl.pallas_call(
        functools.partial(sum_kernel, order, stage),
        out_shape=out_shape,
        in_specs=[pl.BlockSpec(memory_space=pltpu.SMEM)] * 2
        + [pl.BlockSpec(memory_space=pltpu.VMEM)] * len(in_vmem),
        out_specs=[pl.BlockSpec(memory_space=pltpu.VMEM)] * len(out_shape),
        input_output_aliases={4 + i: i for i in range(len(sums))},
        scratch_shapes=[pltpu.SMEM((k_dev + SUM_TERMS,), jnp.int32)],
        compiler_params=pltpu.CompilerParams(vmem_limit_bytes=24 * MIB),
        cost_estimate=pl.CostEstimate(
            flops=k_dev * sec_dev * rows * width * width,
            bytes_accessed=mixed.size + held.size,
            transcendentals=0,
        ),
    )(
        pltpu.with_memory_space_constraint(shift, pltpu.HBM),
        coef,
        *(pltpu.with_memory_space_constraint(x, pltpu.VMEM) for x in in_vmem),
    )


def shift_by(value, axis, distance):
    size = lax.axis_size(axis)
    return lax.ppermute(value, axis, [(i, (i + distance) % size) for i in range(size)])


def after(value, other):
    return lax.optimization_barrier((value, other))[0]


def per_device(wavefunction, left_ops, right_ops, site_coef, coupled, sector_shift):
    sec_dev = wavefunction.shape[0]
    devices = lax.axis_size("sector")
    live = jnp.where(coupled.T > 0, site_coef.T, 0.0)
    split = lax.axis_size("op") == 2 and devices == 4
    mixed, held, *sums = mix(
        wavefunction, left_ops, right_ops, sec_dev * devices, split
    )

    if split:
        coefs = [live] + [shift_by(live, "sector", -g) for g in range(1, devices)]
        coef = jnp.concatenate(coefs, axis=0)
        order = ((2,), (1, 3, 0))
        *sums, mine_2, theirs_2 = summed(sector_shift, coef, mixed, held, order, 0, sums)
        crossed_2 = shift_by(theirs_2, "op", 1)
        _, _, mine_1, theirs_1, mine_3, theirs_3, mine_0, theirs_0 = summed(
            sector_shift, after(coef, theirs_2), mixed, held, order, 1, sums
        )
        both_2 = (mine_2 + after(crossed_2, mine_1).astype(jnp.float32)).astype(jnp.bfloat16)
        arrived_2 = shift_by(both_2, "sector", 2)
        crossed_1 = shift_by(after(theirs_1, both_2), "op", 1)
        crossed_3 = shift_by(after(theirs_3, both_2), "op", 1)
        both_1 = (mine_1 + after(crossed_1, both_2).astype(jnp.float32)).astype(jnp.bfloat16)
        arrived_1 = shift_by(both_1, "sector", 1)
        crossed_0 = shift_by(after(theirs_0, both_1), "op", 1)
        both_3 = (mine_3 + after(crossed_3, both_1).astype(jnp.float32)).astype(jnp.bfloat16)
        arrived_3 = shift_by(both_3, "sector", 3)
        sigma = mine_0 + after(crossed_0, both_3).astype(jnp.float32)
        for other in (arrived_2, arrived_1, arrived_3):
            sigma = lax.optimization_barrier(sigma) + other.astype(jnp.float32)
        return sigma

    first = lax.axis_index("sector") * sec_dev
    coef = jnp.roll(lax.all_gather(live, "sector", axis=0, tiled=True), -first, axis=0)
    (total,) = summed(sector_shift, coef, mixed, held, (), None)
    total = jnp.roll(total, first, axis=0)
    total = lax.psum_scatter(total, "op", scatter_dimension=2, tiled=True)
    return lax.psum_scatter(total, "sector", scatter_dimension=0, tiled=True)


def solution(mesh):
    placed = (
        P(("groups", "sector"), None, None),
        P(("groups", "op"), "rep", None),
        P(("groups", "op"), None, None),
        P(("groups", "op"), "sector"),
        P(("groups", "op"), "sector"),
        P(("groups", "op")),
    )
    return jax.shard_map(
        per_device,
        mesh=mesh,
        in_specs=placed,
        out_specs=P(("groups", "sector"), "rep", "op"),
        check_vma=False,
    )
```
